32 devices in a mesh: head: 4 (over y, x), dp: 8 (over z, core).
Axes of the slice: x: 2, y: 2, z: 4, core: 2. Of those that a mesh axis runs over, the one named last changes fastest.
Arguments:
- tokens: bfloat16 [8, 1024, 1024], P('dp', 'head'), may hold values from -6 to 6
- cotangent: bfloat16 [8, 1024, 1024], P('dp', 'head'), may hold values from -6 to 6
- segments: int32 [8, 1024], P('dp'), may hold values from 0 to 15, never falling along the last dimension, each value on 1 to 512 neighbouring positions
- value_expert_route: int32 [8, 1024, 4, 2], P('dp', None, 'head'), may hold values from 0 to 4, all different within a row
- output_expert_route: int32 [8, 1024, 4, 2], P('dp', None, 'head'), may hold values from 0 to 4, all different within a row
- feedforward_route: int32 [8, 1024, 16], P('dp', 'head'), may hold values from 0 to 31, all different within a row; in each aligned block of 256 rows (0 to 255, 256 to 511, ..., all dimensions but the last counted through in order) at most 160 rows name the same one
- attention_norm_gain: float32 [1024], replicated, may hold values from 0.5 to 1.5
- attention_norm_bias: float32 [1024], replicated, may hold values from -2 to 2
- feedforward_norm_gain: float32 [1024], replicated, may hold values from 0.5 to 1.5
- feedforward_norm_bias: float32 [1024], replicated, may hold values from -2 to 2
- query_projection: bfloat16 [1024, 512], P('dp', 'head'), may hold values from -0.1875 to 0.1875
- key_projection: bfloat16 [1024, 512], P('dp', 'head'), may hold values from -0.1875 to 0.1875
- value_selector: bfloat16 [1024, 20], P('dp', 'head'), may hold values from -0.125 to 0.125
- output_selector: bfloat16 [1024, 20], P('dp', 'head'), may hold values from -0.125 to 0.125
- value_experts: bfloat16 [4, 1024, 640], P('head', 'dp'), may hold values from -0.1875 to 0.1875
- output_experts: bfloat16 [4, 640, 1024], P('head', None, 'dp'), may hold values from -1 to 1
- feedforward_selector: bfloat16 [32, 1024], P(('head', 'dp')), may hold values from -0.09375 to 0.09375
- expert_up_weight: bfloat16 [32, 1024, 128], P(('head', 'dp')), may hold values from -0.1875 to 0.1875
- expert_down_weight: bfloat16 [32, 128, 1024], P(('head', 'dp')), may hold values from -0.5 to 0.5
Outputs:
- output: bfloat16 [8, 1024, 1024], P('dp', 'head')
- grad_tokens: bfloat16 [8, 1024, 1024], P('dp', 'head')
- grad_norms: float32 [4, 1024], P(None, ('head', 'dp'))
- grad_query: float32 [1024, 512], P('dp', 'head')
- grad_key: float32 [1024, 512], P('dp', 'head')
- value_selector_grads: float32 [1024, 20], P('dp', 'head')
- grad_osel: float32 [1024, 20], P('dp', 'head')
- grad_value: float32 [4, 1024, 640], P('head', 'dp')
- grad_out: float32 [4, 640, 1024], P('head', None, 'dp')
- grad_router: float32 [32, 1024], P(('head', 'dp'))
- grad_up: float32 [32, 1024, 128], P(('head', 'dp'))
- grad_down: float32 [32, 128, 1024], P(('head', 'dp'))
The draws below stay inside these ranges and needn't reach their ends.
Inputs may be any that keep to these rules, and one draw needn't show every extreme that they name: `segments`: segment numbers never fall along a pack; 16 documents of 1 to 512 tokens, one of exactly 512. `value_expert_route`: A token's 2 value experts of one head differ. `output_expert_route`: A token's 2 output experts of one head differ. `feedforward_route`: A token's 16 experts differ; in the rows of one device (aligned blocks of 256 rows) no expert is named more than 160 times, a bound that some block reaches.
All inputs are finite; a program needn't handle non-finite values.
Results may differ from the reference program's by a relative error of at most 0.02.
Values may be sent and summed in bfloat16 or wider, within the bound.
No kernel may reach another device: no remote copies, remote signals or barrier semaphores. Data moves between devices by JAX's collectives and lax.ppermute only.
A program may use at most 256 MiB of HBM per device.

```python
import math
import jax
import jax.numpy as jnp
import numpy as np
from jax import lax

MODEL_WIDTH = 1024
HEAD_COUNT = 4
HS = 128
VALUE_EXPERTS = 5
VTOP = 2
EXP_H = 128
TOPK = 16
SEQ = 1024
ROWS = 256
EXPERTS = 32
CAP = 160
DOCS = 16
LONGEST = 512
N_HEAD = 4
N_DP = 8


def shard_levels(key, extent, shards, least, high):
    def one(position, parts):
        heights = jax.random.uniform(jax.random.fold_in(jax.random.fold_in(key, 6), position), (parts,), jnp.float32, least / len(shards), high / len(shards))
        return jnp.repeat(jnp.exp(heights), extent[position] // parts).reshape((-1,) + (1,) * (len(extent) - position - 1))

    loudness = one(*shards[0])
    for cut in shards[1:]:
        loudness = loudness * one(*cut)
    return loudness


def different_ones(own_key, rows, number_of, top, lift):
    sequence = jax.random.permutation(jax.random.fold_in(own_key, 1), number_of)
    boost = sequence
    for power in range(3):
        boost = boost * boost // number_of
    boost = boost * lift // number_of
    lots = jax.random.randint(jax.random.fold_in(own_key, 2), (rows, number_of), 0, 4096) + boost
    fixed_rows = jax.random.permutation(jax.random.fold_in(own_key, 3), rows)[jnp.arange(number_of) % rows]
    lots = jnp.where(jnp.arange(rows)[:, None] == fixed_rows[None, :], 1 << 14, lots)
    priority = lots * number_of + jnp.arange(number_of)
    return lax.top_k(priority.astype(jnp.int32), top)[1].astype(jnp.int32)


def split_up(count, total, bound, lean):
    portions = [(1 << 20) // math.isqrt(standing ** lean) + 1 for standing in range(2, count + 1)]
    rest, given = total - bound - (count - 1), [1] * (count - 1)
    while rest > 0:
        movable = [i for i in range(count - 1) if given[i] < bound]
        whole, remaining = sum([portions[i] for i in movable]), rest
        for i in movable:
            addition = min(bound - given[i], max(1, remaining * portions[i] // whole), rest)
            given[i] = given[i] + addition
            rest = rest - addition
    return np.array([bound] + given)


def uneven(rng, amount, total, reach, slope):
    if amount == 2:
        one = jax.random.randint(rng, (), max(1, total - reach), min(reach, total - 1) + 1)
        return jnp.stack([one, total - one])
    lengths = jnp.asarray(split_up(amount, total, reach, slope), jnp.int32)
    pairs = (amount - 1) // 2
    donor, receiver = lengths[1:1 + 2 * pairs:2], lengths[2:2 + 2 * pairs:2]
    margin = jnp.minimum(donor - 1, reach - receiver)
    shifted = jax.random.randint(jax.random.fold_in(rng, 1), (pairs,), 0, 1 << 20) % (margin + 1)
    lengths = lengths.at[1:1 + 2 * pairs:2].set(donor - shifted).at[2:2 + 2 * pairs:2].set(receiver + shifted)
    return lengths[jax.random.permutation(jax.random.fold_in(rng, 2), amount)]


def deal_out(stream_key, own, number, rows, count, top, reach, skew):
    ranking = jax.random.permutation(stream_key, count)
    packed, usual = shares(count, rows * top, reach, skew, True), shares(count, rows * top, reach, skew, False)
    places = jnp.arange(count)

    def named(tallies, turn):
        used = int((tallies > 0).sum())
        fixed = max(1, used // 4)
        moved = fixed + (places - fixed + turn * (used - fixed)) % max(1, count - fixed)
        return jnp.zeros((count,), jnp.int32).at[ranking[jnp.where(places < fixed, places, moved)]].set(jnp.asarray(tallies, jnp.int32))

    tallies = jnp.where(number % 4 == 0, named(packed, number // 4), named(usual, number - number // 4 - 1))
    mixed = jax.random.permutation(jax.random.fold_in(own, 3), count)
    source_of, taker = mixed[0:count // 2 * 2:2], mixed[1:count // 2 * 2:2]
    margin = jnp.minimum(tallies[source_of] - 1, reach - tallies[taker]) // 2
    margin = jnp.where((source_of == ranking[0]) | (taker == ranking[0]) | (tallies[taker] == 0), 0, jnp.maximum(margin, 0))
    moved = jax.random.randint(jax.random.fold_in(own, 4), (count // 2,), 0, 1 << 20) % (margin + 1)
    tallies = tallies.at[source_of].add(-moved).at[taker].add(moved)
    members = jnp.searchsorted(jnp.cumsum(tallies), jnp.arange(rows * top), side="right").astype(jnp.int32)
    table = members.reshape(top, rows).T
    table = table[jax.random.permutation(jax.random.fold_in(own, 1), rows)]
    turn = jax.random.randint(jax.random.fold_in(own, 2), (rows, 1), 0, top)
    return jnp.take_along_axis(table, (jnp.arange(top)[None, :] + turn) % top, axis=1)


def shares(number_of, total, limit, lean, full):
    loads = [(1 << 20) // math.isqrt(rank ** lean) + 1 for rank in range(1, number_of + 1)]
    largest = limit if full else min(limit, max(-(-total // number_of), total * loads[0] // sum(loads)))
    least = 1 if total - largest >= number_of - 1 else 0
    holding, surplus = [largest] + [least] * (number_of - 1), total - largest - least * (number_of - 1)
    while surplus > 0:
        candidates = [i for i in range(1, number_of) if holding[i] < largest] or [i for i in range(1, number_of) if holding[i] < limit]
        pool, budget = sum([loads[i] for i in candidates]), surplus
        for i in candidates:
            more = min(limit - holding[i], max(1, budget * loads[i] // pool), surplus)
            holding[i] = holding[i] + more
            surplus = surplus - more
    return np.array(holding)


def gaussian(rng, extent, deviation, most, cuts=(), held_as=jnp.bfloat16):
    values = deviation * jax.random.normal(rng, extent, jnp.float32)
    if cuts:
        values = values * shard_levels(rng, extent, cuts, -0.22, 0.18)
    return jnp.clip(values, -most, most).astype(held_as)


def setup_inputs(seed: int = 0) -> dict:
    seeds = jax.random.split(jax.random.key(seed), 20)
    tokens = gaussian(seeds[0], (N_DP, SEQ, MODEL_WIDTH), 1.0, 6.0, ((0, 8), (1, 4)))
    cotangent = gaussian(seeds[1], (N_DP, SEQ, MODEL_WIDTH), 1.0, 6.0, ((0, 8), (1, 4)))
    segments = jax.vmap(lambda own: jnp.searchsorted(jnp.cumsum(uneven(own, DOCS, SEQ, LONGEST, 2)), jnp.arange(SEQ), side="right"))(jax.random.split(seeds[2], N_DP)).reshape((N_DP, SEQ)).astype(jnp.int32)
    value_expert_route = different_ones(seeds[3], N_DP * SEQ * HEAD_COUNT, VALUE_EXPERTS, VTOP, 0).reshape((N_DP, SEQ, HEAD_COUNT, VTOP))
    output_expert_route = different_ones(seeds[4], N_DP * SEQ * HEAD_COUNT, VALUE_EXPERTS, VTOP, 0).reshape((N_DP, SEQ, HEAD_COUNT, VTOP))
    feedforward_route_keys = jax.random.split(jax.random.fold_in(seeds[5], 1), N_DP * SEQ // ROWS)
    feedforward_route_turns = jax.random.permutation(jax.random.fold_in(seeds[5], 3), N_DP * SEQ // ROWS)
    feedforward_route = jax.vmap(lambda own, number: deal_out(jax.random.fold_in(seeds[5], 2), own, number, ROWS, EXPERTS, TOPK, CAP, 1))(feedforward_route_keys, feedforward_route_turns).reshape((N_DP, SEQ, TOPK))
    attention_norm_gain = jnp.clip(1.0 + 0.1 * jax.random.normal(seeds[6], (MODEL_WIDTH,), jnp.float32), 0.5, 1.5)
    attention_norm_bias = gaussian(seeds[7], (MODEL_WIDTH,), 0.3, 2.0, (), jnp.float32)
    feedforward_norm_gain = jnp.clip(1.0 + 0.1 * jax.random.normal(seeds[8], (MODEL_WIDTH,), jnp.float32), 0.5, 1.5)
    feedforward_norm_bias = gaussian(seeds[9], (MODEL_WIDTH,), 0.3, 2.0, (), jnp.float32)
    query_projection = gaussian(seeds[10], (MODEL_WIDTH, HEAD_COUNT * HS), MODEL_WIDTH ** -0.5, 0.1875, ((0, 8), (1, 4)))
    key_projection = gaussian(seeds[11], (MODEL_WIDTH, HEAD_COUNT * HS), MODEL_WIDTH ** -0.5, 0.1875, ((0, 8), (1, 4)))
    value_selector = gaussian(seeds[12], (MODEL_WIDTH, HEAD_COUNT * VALUE_EXPERTS), (2 * MODEL_WIDTH) ** -0.5, 0.125, ((0, 8), (1, 4)))
    output_selector = gaussian(seeds[13], (MODEL_WIDTH, HEAD_COUNT * VALUE_EXPERTS), (2 * MODEL_WIDTH) ** -0.5, 0.125, ((0, 8), (1, 4)))
    value_experts = gaussian(seeds[14], (HEAD_COUNT, MODEL_WIDTH, VALUE_EXPERTS * HS), MODEL_WIDTH ** -0.5, 0.1875, ((0, 4), (1, 8)))
    output_experts = gaussian(seeds[15], (HEAD_COUNT, VALUE_EXPERTS * HS, MODEL_WIDTH), (HS // 4) ** -0.5, 1.0, ((0, 4), (2, 8)))
    feedforward_selector = gaussian(seeds[16], (EXPERTS, MODEL_WIDTH), (4 * MODEL_WIDTH) ** -0.5, 0.09375, ((0, 32),))
    expert_up_weight = gaussian(seeds[17], (EXPERTS, MODEL_WIDTH, EXP_H), MODEL_WIDTH ** -0.5, 0.1875, ((0, 32),))
    expert_down_weight = gaussian(seeds[18], (EXPERTS, EXP_H, MODEL_WIDTH), EXP_H ** -0.5, 0.5, ((0, 32),))
    return {"tokens": tokens, "cotangent": cotangent, "segments": segments, "value_expert_route": value_expert_route, "output_expert_route": output_expert_route, "feedforward_route": feedforward_route, "attention_norm_gain": attention_norm_gain, "attention_norm_bias": attention_norm_bias, "feedforward_norm_gain": feedforward_norm_gain, "feedforward_norm_bias": feedforward_norm_bias, "query_projection": query_projection, "key_projection": key_projection, "value_selector": value_selector, "output_selector": output_selector, "value_experts": value_experts, "output_experts": output_experts, "feedforward_selector": feedforward_selector, "expert_up_weight": expert_up_weight, "expert_down_weight": expert_down_weight}


EPS = 1e-05
HIGH = lax.Precision.HIGHEST

@jax.custom_vjp
def low(v):
    return lax.optimization_barrier(v.astype(jnp.bfloat16)).astype(jnp.float32)

@jax.custom_vjp
def low_back(v):
    return v

def low_keep(v):
    return (low(v), None)

def low_pass(kept, grad):
    return (grad,)

def back_keep(v):
    return (v, None)

def back_low(kept, grad):
    return (low(grad),)
low.defvjp(low_keep, low_pass)
low_back.defvjp(back_keep, back_low)

def matrix_product(left, right):
    return jnp.dot(left, right, precision=HIGH)

def layer_norm(values, gain, bias):
    center = values - lax.optimization_barrier(jnp.mean(values, -1, keepdims=True))
    return center * lax.rsqrt(lax.optimization_barrier(jnp.mean(center * center, -1, keepdims=True)) + EPS) * gain + bias

def per_head_attention(normed_input, input_values, document_index, value_route_chosen, output_route_chosen, query_weight, key_weight, value_selector_weight, output_selector_weight, value_weight, output_weight):
    length = normed_input.shape[0]
    block_rows = min(512, length)
    query = low(low_back(matrix_product(normed_input, query_weight) * HS ** (-0.5)))
    keys = low(low_back(matrix_product(normed_input, key_weight)))
    value_mask = lax.optimization_barrier(jnp.sum(jax.nn.one_hot(value_route_chosen, VALUE_EXPERTS, dtype=jnp.float32), 1))
    omask = lax.optimization_barrier(jnp.sum(jax.nn.one_hot(output_route_chosen, VALUE_EXPERTS, dtype=jnp.float32), 1))
    value_gate_scores = jax.nn.sigmoid(matrix_product(normed_input, value_selector_weight)) * value_mask
    ogate = jax.nn.sigmoid(matrix_product(normed_input, output_selector_weight)) * omask
    experts_v = low_back(matrix_product(input_values, value_weight)).reshape(length, VALUE_EXPERTS, HS)
    value = low(lax.optimization_barrier(jnp.sum(value_gate_scores[:, :, None] * experts_v, 1)))
    positions = jnp.arange(length, dtype=jnp.int32)

    def block(start):
        rows = lax.dynamic_slice_in_dim(query, start, block_rows, 0)
        spots = start + jnp.arange(block_rows, dtype=jnp.int32)
        docs = lax.dynamic_slice_in_dim(document_index, start, block_rows, 0)
        visible = (docs[:, None] == document_index[None, :]) & (positions[None, :] <= spots[:, None])
        scores = jnp.where(visible, low_back(matrix_product(rows, keys.T)), -jnp.inf)
        return matrix_product(low(jax.nn.softmax(scores, axis=-1)), value)
    starts = jnp.arange(length // block_rows, dtype=jnp.int32) * block_rows
    attended = low_back(lax.map(jax.checkpoint(block), starts).reshape(length, HS))
    mixed = low((ogate[:, :, None] * attended[:, None, :]).reshape(length, VALUE_EXPERTS * HS))
    return matrix_product(mixed, output_weight)

def expert_mix(resid, froute, second_gain, second_bias, router_weight, up_weight, down_weight):
    resid_low = low(resid)
    flat = froute.reshape(-1)
    owners = jnp.arange(flat.shape[0], dtype=jnp.int32) // TOPK
    capacity = N_HEAD * CAP
    slots = jnp.arange(capacity, dtype=jnp.int32)

    def step(total, item):
        expert, router_e, up_e, down_e = item
        hits = (flat == expert).astype(jnp.int32)
        places = jnp.where(hits > 0, jnp.cumsum(hits, dtype=jnp.int32) - 1, capacity)
        table = jnp.zeros((capacity,), jnp.int32).at[places].set(owners, mode='drop')
        live = (slots < jnp.sum(hits, dtype=jnp.int32)).astype(jnp.float32)
        rows = low_back(resid_low[table])
        normed_input = low(layer_norm(rows, second_gain, second_bias))
        gate = jax.nn.sigmoid(matrix_product(normed_input, router_e))
        pre = low_back(matrix_product(rows, up_e))
        active = low(jax.nn.gelu(pre, approximate=False))
        unit = low_back(matrix_product(active, down_e))
        routed = low(low_back(gate[:, None] * unit))
        return (total.at[table].add(routed * live[:, None]), None)
    ids = jnp.arange(EXPERTS, dtype=jnp.int32)
    total, unused = lax.scan(jax.checkpoint(step), jnp.zeros_like(resid), (ids, router_weight, up_weight, down_weight))
    return total

def layer(packed_values, document_index, value_route_chosen, output_route_chosen, froute, weight_values):
    first_gain, first_bias, second_gain, second_bias, query_weight, key_weight, value_selector_weight, output_selector_weight, value_weight, output_weight, router_weight, up_weight, down_weight = weight_values
    normed_input = low(layer_norm(packed_values, first_gain, first_bias))
    branch_output = jnp.zeros_like(packed_values)
    for head_number in range(HEAD_COUNT):
        lower_bound = head_number * HS
        upper_bound = (head_number + 1) * HS
        first_position = head_number * VALUE_EXPERTS
        last_position = (head_number + 1) * VALUE_EXPERTS
        branch_output = branch_output + per_head_attention(normed_input, packed_values, document_index, value_route_chosen[:, head_number], output_route_chosen[:, head_number], query_weight[:, lower_bound:upper_bound], key_weight[:, lower_bound:upper_bound], value_selector_weight[:, first_position:last_position], output_selector_weight[:, first_position:last_position], value_weight[head_number], output_weight[head_number])
    resid = packed_values + low_back(branch_output)
    return resid + expert_mix(resid, froute, second_gain, second_bias, router_weight, up_weight, down_weight)

def reference(tokens, cotangent, segments, value_expert_route, output_expert_route, feedforward_route, attention_norm_gain, attention_norm_bias, feedforward_norm_gain, feedforward_norm_bias, query_projection, key_projection, value_selector, output_selector, value_experts, output_experts, feedforward_selector, expert_up_weight, expert_down_weight):
    weight_values = tuple((source_array.astype(jnp.float32) for source_array in (attention_norm_gain, attention_norm_bias, feedforward_norm_gain, feedforward_norm_bias, query_projection, key_projection, value_selector, output_selector, value_experts, output_experts, feedforward_selector, expert_up_weight, expert_down_weight)))

    def per_pack(sums, items):
        packed_values, grad, document_index, value_route_chosen, output_route_chosen, froute = items

        def apply(values, params):
            return layer(values, document_index, value_route_chosen, output_route_chosen, froute, params)
        result, pull = jax.vjp(apply, packed_values.astype(jnp.float32), weight_values)
        d_pack, d_weights = pull(grad.astype(jnp.float32))
        sums = jax.tree.map(lambda a, b: a + b, sums, d_weights)
        return (sums, (result.astype(jnp.bfloat16), d_pack.astype(jnp.bfloat16)))
    zeros = jax.tree.map(jnp.zeros_like, weight_values)
    sums, (outputs, grads) = lax.scan(per_pack, zeros, (tokens, cotangent, segments, value_expert_route, output_expert_route, feedforward_route))
    grad_norms = jnp.stack([sums[0], sums[1], sums[2], sums[3]])
    return (outputs, grads, grad_norms, sums[4], sums[5], sums[6], sums[7], sums[8], sums[9], sums[10], sums[11], sums[12])
```

```python
import jax
import jax.numpy as jnp
from jax import lax
from jax.sharding import PartitionSpec as P

EPS = 1e-05
F32 = jnp.float32
BF16 = jnp.bfloat16
CHUNK = 8


def dot(a, b, dims):
    return lax.dot_general(a, b, (dims, ((), ())), preferred_element_type=F32)


def mm(a, b):
    return dot(a, b, ((1,), (0,)))


def mm_nt(a, b):
    return dot(a, b, ((1,), (1,)))


def mm_tn(a, b):
    return dot(a, b, ((0,), (0,)))


def layer_unit(values):
    center = values - jnp.mean(values, -1, keepdims=True)
    spread = lax.rsqrt(jnp.mean(center * center, -1, keepdims=True) + EPS)
    return center * spread, spread


def norm_back(scaled, unit, spread):
    return spread * (
        scaled
        - jnp.mean(scaled, -1, keepdims=True)
        - unit * jnp.mean(scaled * unit, -1, keepdims=True)
    )


def to_head(value, flip):
    n = lax.axis_size("head")
    return lax.ppermute(value, "head", [(i, i ^ flip) for i in range(n)])


def spread_rows(value):
    half = value.shape[0] // 2
    near_x = to_head(value, 1)
    near_y = to_head(value, 2)
    far = jnp.concatenate([to_head(near_y[:half], 1), to_head(near_x[half:], 2)])
    return jnp.concatenate([value, near_x, near_y, far])


def collect_rows(partial):
    own = partial.shape[0] // 4
    low = partial.astype(BF16)
    total = partial[:own]
    for flip in (3, 1, 2):
        total = total + to_head(low[flip * own : (flip + 1) * own], flip).astype(F32)
    return total


def experts_pass(rows, grad, hits, router, up, down, unit, normed):
    count, width, hidden = up.shape
    up_all = up.transpose(1, 0, 2).reshape(width, count * hidden)
    down_all = down.reshape(count * hidden, width)
    gate = jax.nn.sigmoid(mm_nt(normed, router)) * hits
    wide = lambda g: jnp.broadcast_to(g[:, :, None], g.shape + (hidden,)).reshape(g.shape[0], -1)
    pre = mm(rows, up_all)
    bell = 0.5 * (1.0 + lax.erf(pre * 0.7071067811865476))
    active = (pre * bell).astype(BF16)
    slope = bell + pre * jnp.exp(-0.5 * pre * pre) * 0.3989422804014327
    gate_wide = wide(gate)
    gated = (gate_wide * active.astype(F32)).astype(BF16)
    out = mm(gated, down_all)
    back = mm_nt(grad, down_all)
    d_gate = jnp.sum((active.astype(F32) * back).reshape(-1, count, hidden), -1)
    d_logit = d_gate * gate * (1.0 - gate) * hits
    d_pre = (gate_wide * back * slope).astype(BF16)
    d_rows = mm_nt(d_pre, up_all)
    d_logit_low = d_logit.astype(BF16)
    d_n2 = mm(d_logit_low, router)
    grad_up = mm_tn(d_pre, rows).reshape(count, hidden, width)
    grad_down = mm_tn(gated, grad).reshape(count, hidden, width)
    grad_router = mm_tn(d_logit_low, normed)
    grads = jnp.concatenate([grad_up, grad_down], 1).astype(BF16)
    return out, d_rows, d_n2, grads, grad_router


def shards(
    tokens,
    cotangent,
    segments,
    value_expert_route,
    output_expert_route,
    feedforward_route,
    attention_norm_gain,
    attention_norm_bias,
    feedforward_norm_gain,
    feedforward_norm_bias,
    query_projection,
    key_projection,
    value_selector,
    output_selector,
    value_experts,
    output_experts,
    feedforward_selector,
    expert_up_weight,
    expert_down_weight,
):
    n_data = lax.axis_size("dp")
    head = lax.axis_index("head")
    own, width = tokens.shape[1:]
    length = segments.shape[1]
    size = query_projection.shape[1]
    kinds = value_selector.shape[1]
    hidden = expert_up_weight.shape[2]
    scale = size ** (-0.5)

    def arranged(value):
        return jnp.concatenate(
            [lax.dynamic_slice_in_dim(value, (head ^ k) * own, own, 0) for k in range(4)]
        )

    x_own = tokens[0]
    in_own = jnp.concatenate(
        [query_projection, key_projection, value_experts[0], value_selector, output_selector], 1
    )
    x = spread_rows(x_own)
    in_all = lax.all_gather(in_own, "dp", axis=0, tiled=True)
    out_all = (
        lax.all_gather(output_experts[0], "dp", axis=0, tiled=False)
        .transpose(1, 0, 2)
        .reshape(kinds * size, width)
    )
    ffn_own = jnp.concatenate([expert_up_weight[0].T, expert_down_weight[0]], 0)
    ffn_all = lax.all_gather(ffn_own, "dp", axis=0, tiled=False)
    router = lax.all_gather(feedforward_selector[0], "dp", axis=0, tiled=False)
    grad = spread_rows(cotangent[0])
    routes = spread_rows(feedforward_route[0])

    qk_w = in_all[:, : 2 * size]
    v_w = in_all[:, 2 * size : (2 + kinds) * size]
    sel_w = in_all[:, (2 + kinds) * size :]

    unit1, spread1 = layer_unit(x.astype(F32))
    normed = (unit1 * attention_norm_gain + attention_norm_bias).astype(BF16)
    qk = mm(normed, qk_w)
    query = (qk[:, :size] * scale).astype(BF16)
    key = qk[:, size:].astype(BF16)
    sig = jax.nn.sigmoid(mm(normed, sel_w))
    mask_v = arranged(
        jnp.sum(jax.nn.one_hot(value_expert_route[0, :, 0], kinds, dtype=F32), 1)
    )
    mask_o = arranged(
        jnp.sum(jax.nn.one_hot(output_expert_route[0, :, 0], kinds, dtype=F32), 1)
    )
    sig_v, sig_o = sig[:, :kinds], sig[:, kinds:]
    gate_v, gate_o = sig_v * mask_v, sig_o * mask_o
    experts_v = mm(x, v_w)
    part = lambda a, e: a[:, e * size : (e + 1) * size]
    value = sum(gate_v[:, e : e + 1] * part(experts_v, e) for e in range(kinds)).astype(BF16)

    spots = arranged(jnp.arange(length, dtype=jnp.int32))
    docs = arranged(segments[0])
    visible = (docs[:, None] == docs[None, :]) & (spots[None, :] <= spots[:, None])
    scores = jnp.where(visible, mm_nt(query, key), -jnp.inf)
    row_max = jnp.max(scores, -1, keepdims=True)
    weights = jnp.exp(scores - row_max)
    total = jnp.sum(weights, -1, keepdims=True)
    probs = (weights / total).astype(BF16)
    log_total = row_max + jnp.log(total)
    attended = mm(probs, value)
    mixed = jnp.concatenate(
        [(gate_o[:, e : e + 1] * attended).astype(BF16) for e in range(kinds)], 1
    )
    resid = x_own.astype(F32) + collect_rows(mm(mixed, out_all))
    rows = spread_rows(resid.astype(BF16))

    unit2, spread2 = layer_unit(rows.astype(F32))
    normed2 = (unit2 * feedforward_norm_gain + feedforward_norm_bias).astype(BF16)
    ids = head * n_data + jnp.arange(n_data, dtype=jnp.int32)
    hits = jnp.sum((routes[:, :, None] == ids[None, None, :]).astype(F32), 1)
    up = ffn_all[:, :width].reshape(n_data, hidden, width) if False else ffn_all[:, :hidden]
    down = ffn_all[:, hidden:]
    up = up.transpose(0, 2, 1)
    if n_data <= CHUNK:
        ffn, d_rows, d_n2, ffn_grads, grad_router = experts_pass(
            rows, grad, hits, router, up, down, unit2, normed2
        )
    else:
        cut = lambda a: a.reshape((n_data // CHUNK, CHUNK) + a.shape[1:])

        def step(carry, item):
            hit, rt, u, d = item
            a, b, c, g, r = experts_pass(rows, grad, hit.T, rt, u, d, unit2, normed2)
            return (carry[0] + a, carry[1] + b, carry[2] + c), (g, r)

        zero = jnp.zeros((length, width), F32)
        (ffn, d_rows, d_n2), (ffn_grads, grad_router) = lax.scan(
            step, (zero, zero, zero), (cut(hits.T), cut(router), cut(up), cut(down))
        )
        ffn_grads = ffn_grads.reshape((n_data,) + ffn_grads.shape[2:])
        grad_router = grad_router.reshape(n_data, width)
    d_rows = d_rows + norm_back(d_n2 * feedforward_norm_gain, unit2, spread2)
    norm2 = jnp.stack([jnp.sum(d_n2 * unit2, 0), jnp.sum(d_n2, 0)])

    d_resid = cotangent[0].astype(F32) + collect_rows(d_rows)
    d_pack = spread_rows(d_resid.astype(BF16))
    output = (resid + collect_rows(ffn)).astype(BF16)[None]
    ffn_grads = lax.psum_scatter(ffn_grads, "dp", scatter_dimension=0, tiled=True)[0].astype(F32)

    grad_out = mm_tn(mixed, d_pack)
    d_mixed = mm_nt(d_pack, out_all)
    d_gate_o = jnp.stack([jnp.sum(part(d_mixed, e) * attended, -1) for e in range(kinds)], 1)
    d_attended = sum(gate_o[:, e : e + 1] * part(d_mixed, e) for e in range(kinds)).astype(BF16)
    scores_b = jnp.where(visible, mm_nt(query, key), -jnp.inf)
    probs_b = jnp.exp(scores_b - log_total)
    d_probs = mm_nt(d_attended, value)
    centered = jnp.sum(probs_b * d_probs, -1, keepdims=True)
    d_scores = (probs_b * (d_probs - centered)).astype(BF16)
    d_query = mm(d_scores, key).astype(BF16)
    d_key = mm_tn(d_scores, query).astype(BF16)
    d_value = mm_tn(probs_b.astype(BF16), d_attended)
    d_gate_v = jnp.stack([jnp.sum(d_value * part(experts_v, e), -1) for e in range(kinds)], 1)
    d_experts = jnp.concatenate(
        [(gate_v[:, e : e + 1] * d_value).astype(BF16) for e in range(kinds)], 1
    )
    d_sel = jnp.concatenate(
        [d_gate_v * mask_v * sig_v * (1.0 - sig_v), d_gate_o * mask_o * sig_o * (1.0 - sig_o)], 1
    ).astype(BF16)
    d_in = jnp.concatenate([(d_query.astype(F32) * scale).astype(BF16), d_key, d_sel], 1)
    in_w = jnp.concatenate([qk_w, sel_w], 1)
    grad_in = mm_tn(normed, d_in)
    grad_value = mm_tn(x, d_experts)
    d_normed = mm_nt(d_in, in_w)
    d_input = norm_back(d_normed * attention_norm_gain, unit1, spread1) + mm_nt(d_experts, v_w)
    norm1 = jnp.stack([jnp.sum(d_normed * unit1, 0), jnp.sum(d_normed, 0)])
    grad_tokens = (d_resid + collect_rows(d_input)).astype(BF16)[None]

    weight_grads = jnp.concatenate([grad_in, grad_value], 1).astype(BF16)
    weight_grads = lax.psum_scatter(weight_grads, "dp", scatter_dimension=0, tiled=True)
    weight_grads = weight_grads.astype(F32)
    gq = weight_grads[:, :size]
    gk = weight_grads[:, size : 2 * size]
    gvs = weight_grads[:, 2 * size : 2 * size + kinds]
    gos = weight_grads[:, 2 * size + kinds : 2 * size + 2 * kinds]
    gv = weight_grads[:, 2 * size + 2 * kinds :][None]
    out_grads = lax.psum_scatter(
        grad_out.reshape(kinds * size, n_data, width // n_data).transpose(1, 0, 2).astype(BF16),
        "dp",
        scatter_dimension=0,
        tiled=True,
    )[0].astype(F32)[None]
    router_grads = lax.psum_scatter(grad_router, "dp", scatter_dimension=0, tiled=True)
    norms = jnp.concatenate([norm1, norm2])
    norms = lax.psum_scatter(norms, "head", scatter_dimension=1, tiled=True)
    norms = lax.psum_scatter(norms, "dp", scatter_dimension=1, tiled=True)
    return (
        output,
        grad_tokens,
        norms,
        gq,
        gk,
        gvs,
        gos,
        gv,
        out_grads,
        router_grads,
        ffn_grads[:hidden].T[None],
        ffn_grads[hidden:][None],
    )


def solution(mesh):
    placed = (
        P("dp", "head", None),
        P("dp", "head", None),
        P("dp", None),
        P("dp", None, "head", None),
        P("dp", None, "head", None),
        P("dp", "head", None),
        P(),
        P(),
        P(),
        P(),
        P("dp", "head"),
        P("dp", "head"),
        P("dp", "head"),
        P("dp", "head"),
        P("head", "dp", None),
        P("head", None, "dp"),
        P(("head", "dp"), None),
        P(("head", "dp"), None, None),
        P(("head", "dp"), None, None),
    )
    return jax.shard_map(
        shards,
        mesh=mesh,
        in_specs=placed,
        out_specs=(
            P("dp", "head", None),
            P("dp", "head", None),
            P(None, ("head", "dp")),
            P("dp", "head"),
            P("dp", "head"),
            P("dp", "head"),
            P("dp", "head"),
            P("head", "dp", None),
            P("head", None, "dp"),
            P(("head", "dp"), None),
            P(("head", "dp"), None, None),
            P(("head", "dp"), None, None),
        ),
        check_vma=False,
    )
```

```python
import functools

import jax
import jax.numpy as jnp
from jax import lax
from jax.experimental import pallas as pl
from jax.experimental.pallas import tpu as pltpu
from jax.sharding import PartitionSpec as P

EPS = 1e-05
F32 = jnp.float32
BF16 = jnp.bfloat16
CHUNK = 8
LANES = 128
WIDE = 256
PAD = 16
MEAN, SPREAD = 16, 17
VMEM_BYTES = 56 * 2**20
ROOT_HALF = 0.7071067811865476
INV_ROOT_2PI = 0.3989422804014327
ANY = pl.BlockSpec(memory_space=pl.ANY)
SMEM = pl.BlockSpec(memory_space=pltpu.SMEM)


def dot(a, b, dims):
    return lax.dot_general(a, b, (dims, ((), ())), preferred_element_type=F32)


def nn(a, b):
    return dot(a, b, ((1,), (0,)))


def nt(a, b):
    return dot(a, b, ((1,), (1,)))


def tn(a, b):
    return dot(a, b, ((0,), (0,)))


def shape(dims, kind):
    return jax.ShapeDtypeStruct(dims, kind)


def cost(micros):
    return pl.CostEstimate(flops=int(micros * 1e9), bytes_accessed=0, transcendentals=0)


class Rows:
    def __init__(self, arrays, most=1 << 20):
        self.arrays = list(arrays)
        most = most if isinstance(most, list) else [most] * len(self.arrays)
        self.counts = [min(a.shape[0], m) for a, m in zip(arrays, most)]
        self.dims = (sum(self.counts),) + tuple(arrays[0].shape[1:])


class Part:
    def __init__(self, array, first, count):
        self.arrays, self.first, self.count = [array], first, count
        self.dims = (array.shape[0], count) + tuple(array.shape[2:])


class In:
    def __init__(self, ref, copies, spans):
        self.ref, self.copies, self.spans, self.waited = ref, copies, spans, set()

    def ready(self, first=0, count=1 << 20):
        for i, (copy, (start, size)) in enumerate(zip(self.copies, self.spans)):
            if i not in self.waited and start < first + count and first < start + size:
                copy.wait()
                self.waited.add(i)
        return self.ref

    def rows(self, first, count):
        return self.ready(first, count)[pl.ds(first, count), :]

    def __getitem__(self, at):
        return self.ready()[at]


class Out:
    def __init__(self, ref, dest, sems):
        self.ref, self.dest, self.sems, self.copies = ref, dest, sems, []

    def __setitem__(self, at, value):
        self.ref[at] = value

    def __getitem__(self, at):
        return self.ref[at]

    def send(self, first=None, count=None):
        source, dest = self.ref, self.dest
        if first is not None:
            source, dest = source.at[pl.ds(first, count)], dest.at[pl.ds(first, count)]
        copy = pltpu.make_async_copy(source, dest, self.sems.at[len(self.copies)])
        copy.start()
        self.copies.append(copy)


def call(name, micros, body, outs, args, after=()):
    entries = [a if isinstance(a, (Rows, Part)) else Rows([a]) for a in args]
    arrays = [a for e in entries for a in e.arrays]
    single = not isinstance(outs, (list, tuple))
    out_list = [outs] if single else list(outs)

    def kernel(*refs):
        refs = list(refs)
        sources, refs = refs[: len(arrays)], refs[len(arrays) + len(after) :]
        dests, refs = refs[: len(out_list)], refs[len(out_list) :]
        bufs, refs = refs[: len(entries)], refs[len(entries) :]
        in_sems, refs = refs[: len(entries)], refs[len(entries) :]
        out_bufs, out_sems = refs[: len(out_list)], refs[len(out_list) :]
        ins = []
        for entry, buf, sems in zip(entries, bufs, in_sems):
            pairs, spans, at = [], [], 0
            for i, array in enumerate(entry.arrays):
                source, n = sources.pop(0), array.shape[0]
                if isinstance(entry, Rows) and entry.counts[i] < n:
                    n = entry.counts[i]
                    source = source.at[pl.ds(0, n)]
                spans.append((at, n))
                if isinstance(entry, Part):
                    pairs.append((source.at[:, pl.ds(entry.first, entry.count)], buf))
                elif len(entry.arrays) == 1:
                    pairs.append((source, buf))
                else:
                    pairs.append((source, buf.at[pl.ds(at, n)]))
                at += n
            copies = [
                pltpu.make_async_copy(source, dest, sems.at[i])
                for i, (source, dest) in enumerate(pairs)
            ]
            for copy in copies:
                copy.start()
            ins.append(In(buf, copies, spans))
        results = [Out(b, d, s) for b, d, s in zip(out_bufs, dests, out_sems)]
        body(*ins, *results)
        for entry in ins:
            entry.ready()
        for result in results:
            if not result.copies:
                result.send()
        for result in results:
            for copy in result.copies:
                copy.wait()

    return pl.pallas_call(
        kernel,
        name=name,
        out_shape=outs,
        in_specs=[ANY] * (len(arrays) + len(after)),
        out_specs=ANY if single else [ANY] * len(out_list),
        scratch_shapes=[pltpu.VMEM(e.dims, e.arrays[0].dtype) for e in entries]
        + [pltpu.SemaphoreType.DMA((len(e.arrays),)) for e in entries]
        + [pltpu.VMEM(o.shape, o.dtype) for o in out_list]
        + [pltpu.SemaphoreType.DMA((8,)) for o in out_list],
        compiler_params=pltpu.CompilerParams(vmem_limit_bytes=VMEM_BYTES),
        cost_estimate=cost(micros),
    )(*arrays, *after)


def pack_in_kernel(kinds, q, k, v, vsel, osel, o, out):
    size = q.ref.shape[1]
    out[:, 3 * LANES + kinds * size :] = o[...].T
    out[:, 2 * size : 3 * LANES] = jnp.zeros((q.ref.shape[0], LANES), BF16)
    out[:, :size] = q[...]
    out[:, size : 2 * size] = k[...]
    out[:, 2 * size : 2 * size + kinds] = vsel[...]
    out[:, 2 * size + kinds : 2 * size + 2 * kinds] = osel[...]
    out[:, 3 * LANES : 3 * LANES + kinds * size] = v[...]


def pack_experts_kernel(up, down, router, out):
    hidden = up.ref.shape[1]
    out[:hidden, :] = up[...].T
    out[hidden : 2 * hidden, :] = down[...]
    out[2 * hidden :, :] = jnp.broadcast_to(router[...], (PAD, router.ref.shape[1]))


def stack_kernel(pieces, out):
    out[...] = pieces[...]


def split_kernel(rows, top, bottom):
    half = top.ref.shape[0]
    top[...] = rows[:half, :]
    bottom[...] = rows[half:, :]


def residual_kernel(*refs):
    parts, (total, top, bottom) = refs[:-3], refs[-3:]
    half = top.ref.shape[0]
    for first, low in ((0, top), (half, bottom)):
        at = pl.ds(first, half)
        found = parts[0][at, :].astype(F32)
        for part in parts[1:]:
            found = found + part[at, :].astype(F32)
        low[...] = found.astype(BF16)
        low.send()
        total[at, :] = found
        total.send(first, half)


def finish_kernel(*refs):
    parts, out = refs[:-1], refs[-1]
    found = parts[0][...].astype(F32)
    for part in parts[1:]:
        found = found + part[...].astype(F32)
    out[...] = found.astype(BF16)


def layer_stats(values):
    mean = jnp.mean(values, -1, keepdims=True)
    center = values - mean
    return mean, lax.rsqrt(jnp.mean(center * center, -1, keepdims=True) + EPS)


def norm_back(scaled, unit, spread):
    return spread * (
        scaled
        - jnp.mean(scaled, -1, keepdims=True)
        - unit * jnp.mean(scaled * unit, -1, keepdims=True)
    )


def project_kernel(own, scale, kinds, size, x, gain, bias, info, w, q, k, v, ev, gate):
    for b in range(4):
        at = pl.ds(b * own, own)
        rows = x.rows(b * own, own)
        mean, spread = layer_stats(rows.astype(F32))
        normed = ((rows.astype(F32) - mean) * spread * gain[...] + bias[...]).astype(BF16)
        first = nn(normed, w[:, : 3 * LANES])
        q[at, :] = (first[:, :size] * scale).astype(BF16)
        k[at, :] = first[:, size : 2 * size].astype(BF16)
        lane = lax.broadcasted_iota(jnp.int32, (own, LANES), 1)
        chosen = lane < 0
        for c in range(2, 6):
            chosen = chosen | (lane == info[at, c : c + 1])
        found = jnp.where(chosen, jax.nn.sigmoid(first[:, 2 * size :]), 0.0)
        gate[at, :] = jnp.where(lane == MEAN, mean, jnp.where(lane == SPREAD, spread, found))
        experts = nn(rows, w[:, 3 * LANES :])
        ev[at, :] = experts.astype(BF16)
        ev.send(b * own, own)
        value = found[:, :1] * experts[:, :size]
        for e in range(1, kinds):
            value = value + found[:, e : e + 1] * experts[:, e * size : (e + 1) * size]
        v[at, :] = value.astype(BF16)


def visible(info, code):
    return (code >= info[:, 0:1]) & (code <= info[:, 1:2])


def attend_kernel(own, blocks, kinds, size, q, k, v, info, code, gate, w, *outs):
    att, lse, mixed = outs[len(blocks) :]
    base = min(blocks)
    for i, b in enumerate(blocks):
        at = pl.ds(b * own, own)
        to = pl.ds((b - base) * own, own)
        scores = jnp.where(visible(info[at, :], code[...]), nt(q[at, :], k[...]), -jnp.inf)
        top = jnp.max(scores, -1, keepdims=True)
        weights = jnp.exp(scores - top)
        total = jnp.sum(weights, -1, keepdims=True)
        probs = (weights / total).astype(BF16)
        found = nn(probs, v[...])
        att[to, :] = found
        lse[to, :] = jnp.broadcast_to(top + jnp.log(total), (own, LANES))
        opened = gate[at, :]
        for e in range(kinds):
            mixed[to, e * size : (e + 1) * size] = (
                opened[:, kinds + e : kinds + e + 1] * found
            ).astype(BF16)
        outs[i][...] = nt(mixed[to, :], w[...]).astype(BF16)
        outs[i].send()


def expert_kernel(n_blocks, count, hidden, rows_in, gain, bias, router, hits, up_in, grad_in, down_in, *outs):
    back_outs, outs = outs[:n_blocks], outs[n_blocks:]
    dpre_outs, outs = outs[:n_blocks], outs[n_blocks:]
    gated_outs, outs = outs[:n_blocks], outs[n_blocks:]
    norm, route = outs
    width = rows_in.ref.shape[1]
    own = rows_in.ref.shape[0] // n_blocks
    flat_up = lambda: up_in[...].reshape(count * hidden, width)
    flat_down = lambda: down_in[...].reshape(count * hidden, width)
    for i in range(n_blocks):
        at = pl.ds(i * own, own)
        rows = rows_in.rows(i * own, own)
        mean, spread = layer_stats(rows.astype(F32))
        unit = (rows.astype(F32) - mean) * spread
        normed = (unit * gain[...] + bias[...]).astype(BF16)
        gate = jax.nn.sigmoid(nt(normed, router[...])) * hits[at, :]
        pre = nt(rows, flat_up())
        back = nt(grad_in.rows(i * own, own), flat_down())
        d_gate = []
        for e in range(count):
            col = slice(e * hidden, (e + 1) * hidden)
            p, b, g = pre[:, col], back[:, col], gate[:, e : e + 1]
            bell = 0.5 * (1.0 + lax.erf(p * ROOT_HALF))
            active = p * bell
            slope = bell + p * jnp.exp(-0.5 * p * p) * INV_ROOT_2PI
            gated_outs[i][:, col] = (g * active).astype(BF16)
            dpre_outs[i][:, col] = (g * b * slope).astype(BF16)
            d_gate.append(jnp.sum(active * b, -1, keepdims=True))
        gated_outs[i].send()
        dpre_outs[i].send()
        d_logit = (jnp.concatenate(d_gate, 1) * gate * (1.0 - gate)).astype(BF16)
        d_n2 = nn(d_logit, router[...])
        back_outs[i][...] = (
            nn(dpre_outs[i][...], flat_up()) + norm_back(d_n2 * gain[...], unit, spread)
        ).astype(BF16)
        back_outs[i].send()
        sums = jnp.concatenate(
            [jnp.sum(d_n2 * unit, 0, keepdims=True), jnp.sum(d_n2, 0, keepdims=True)], 0
        )
        routes = tn(d_logit, normed)
        norm[...] = sums if i == 0 else norm[...] + sums
        route[...] = routes if i == 0 else route[...] + routes


def expert_out_kernel(count, hidden, gated, down, *outs):
    own, width = outs[0].ref.shape
    for i, out in enumerate(outs):
        rows = gated.rows(i * own, own)
        out[...] = nn(rows, down[...].reshape(count * hidden, width)).astype(BF16)
        out.send()


def expert_grad_kernel(count, hidden, gated, grad, dpre, rows, *refs):
    routes, out = refs[:-1], refs[-1]
    for first in range(0, count * hidden, WIDE):
        col = slice(first, first + WIDE)
        down = tn(gated[:, col], grad[...]).astype(BF16)
        up = tn(dpre[:, col], rows[...]).astype(BF16)
        for e in range(first // hidden, (first + WIDE) // hidden):
            at = slice(e * hidden - first, (e + 1) * hidden - first)
            out[e, :hidden, :] = up[at]
            out[e, hidden : 2 * hidden, :] = down[at]
            route = sum(r[e : e + 1, :] for r in routes)
            out[e, 2 * hidden :, :] = jnp.broadcast_to(route, (PAD, route.shape[1])).astype(BF16)
        out.send(first // hidden, WIDE // hidden)


def attend_back_rows(own, blocks, base, kinds, size, d_rows, w, q, k, v, info, code, gate, att, lse, store):
    dk = dv = None
    lane = lax.broadcasted_iota(jnp.int32, (own, LANES), 1)
    for i, b in enumerate(blocks):
        at = pl.ds(b * own, own)
        to = pl.ds((b - base) * own, own)
        found = att[to, :]
        opened = gate[at, :]
        queries = q[at, :]
        scores = jnp.where(visible(info[at, :], code[...]), nt(queries, k[...]), -jnp.inf)
        probs = jnp.exp(scores - lse[to, 0:1])
        d_mixed = nn(d_rows.rows(i * own, own), w[...])
        d_att = jnp.zeros((own, size), F32)
        d_sel = jnp.zeros((own, LANES), F32)
        for e in range(kinds):
            part = d_mixed[:, e * size : (e + 1) * size]
            d_att = d_att + opened[:, kinds + e : kinds + e + 1] * part
            d_sel = jnp.where(
                lane == kinds + e, jnp.sum(part * found, -1, keepdims=True), d_sel
            )
        d_att = d_att.astype(BF16)
        d_probs = nt(d_att, v[...])
        centered = jnp.sum(probs * d_probs, -1, keepdims=True)
        d_scores = (probs * (d_probs - centered)).astype(BF16)
        store(i, nn(d_scores, k[...]).astype(BF16), d_sel * opened * (1.0 - opened))
        more_k, more_v = tn(d_scores, queries), tn(probs.astype(BF16), d_att)
        dk = more_k if dk is None else dk + more_k
        dv = more_v if dv is None else dv + more_v
    return dk, dv


def attend_back_kernel(own, blocks, kinds, size, q, k, info, code, lse, w, d_rows, v, gate, att, dq, dsel, dk, dv):
    def store(i, query, selector):
        at = pl.ds((blocks[i] - min(blocks)) * own, own)
        dq[at, :] = query
        dsel[at, :] = selector

    dk[...], dv[...] = attend_back_rows(
        own, blocks, min(blocks), kinds, size, d_rows, w, q, k, v, info, code, gate, att, lse, store
    )


def attend_last_kernel(own, kinds, size, q, k, info, code, lse, w, d_rows, v, gate, att, dq, dsel, dk, dv, ev, din, dexp):
    last = 3 * own
    sel = [None]

    def store(i, query, selector):
        din[last:, :size] = query
        sel[0] = selector

    more_k, more_v = attend_back_rows(
        own, (3,), 3, kinds, size, d_rows, w, q, k, v, info, code, gate, att, lse, store
    )
    lane = lax.broadcasted_iota(jnp.int32, (own, LANES), 1)
    din[:last, :size] = dq[...]
    for b in range(4):
        at = pl.ds(b * own, own)
        cut = slice(b * own, (b + 1) * own)
        opened = gate[at, :]
        factor = opened * (1.0 - opened)
        value = dv[at, :] + more_v[cut]
        din[at, size : 2 * size] = (dk[at, :] + more_k[cut]).astype(BF16)
        d_sel = dsel[at, :] if b < 3 else sel[0]
        for e in range(kinds):
            col = slice(e * size, (e + 1) * size)
            moved = jnp.sum(ev[at, col].astype(F32) * value, -1, keepdims=True)
            d_sel = jnp.where(lane == e, moved * factor, d_sel)
            dexp[at, col] = (opened[:, e : e + 1] * value).astype(BF16)
        din[at, 2 * size :] = d_sel.astype(BF16)


def weight_kernel(din, dexp, x, gate, gain, bias, d_rows, mixed, out):
    width = x.ref.shape[1]
    mean, spread = gate[:, MEAN : MEAN + 1], gate[:, SPREAD : SPREAD + 1]
    first_end = din.ref.shape[1]
    second_end = first_end + dexp.ref.shape[1]
    for first in range(0, width, WIDE):
        col = slice(first, first + WIDE)
        rows = x[:, col]
        normed = ((rows.astype(F32) - mean) * spread * gain[:, col] + bias[:, col]).astype(BF16)
        at = slice(first, first + WIDE)
        out[at, :first_end] = tn(normed, din[...]).astype(BF16)
        out[at, first_end:second_end] = tn(rows, dexp[...]).astype(BF16)
        out[at, second_end:] = tn(d_rows[:, col], mixed[...]).astype(BF16)
        out.send(first, WIDE)


def input_grad_kernel(own, blocks, scale, size, x, din, gate, gain, w, dexp, *outs):
    norm = outs[-1]
    for i, b in enumerate(blocks):
        at = pl.ds(b * own, own)
        rows = x.rows(b * own, own).astype(F32)
        spread = gate[at, SPREAD : SPREAD + 1]
        unit = (rows - gate[at, MEAN : MEAN + 1]) * spread
        d_normed = nt(din[at, :size], w[:, :size]) * scale + nt(
            din[at, size:], w[:, size : 3 * LANES]
        )
        outs[i][...] = (
            norm_back(d_normed * gain[...], unit, spread) + nt(dexp[at, :], w[:, 3 * LANES :])
        ).astype(BF16)
        outs[i].send()
        sums = jnp.concatenate(
            [jnp.sum(d_normed * unit, 0, keepdims=True), jnp.sum(d_normed, 0, keepdims=True)], 0
        )
        norm[...] = sums if i == 0 else norm[...] + sums


def to_head(value, flip):
    n = lax.axis_size("head")
    return lax.ppermute(value, "head", [(i, i ^ flip) for i in range(n)])


def to_core(value):
    n = lax.axis_size("dp")
    return lax.ppermute(value, "dp", [(i, i ^ 1) for i in range(n)])


def to_later(value, step):
    n = lax.axis_size("dp")
    return lax.ppermute(value, "dp", [(i, (i + step) % n) for i in range(n)])


def spread_rows(top, bottom):
    y_top, x_bottom = to_head(top, 2), to_head(bottom, 1)
    y_bottom, x_top = to_head(bottom, 2), to_head(top, 1)
    far_top, far_bottom = to_head(y_top, 1), to_head(x_bottom, 2)
    return [[top, bottom], [x_top, x_bottom], [y_top, y_bottom], [far_top, far_bottom]]


def flat(blocks):
    return [piece for block in blocks for piece in block]


def expert_blocks(name, rows, grads, hits, weights, router, gain, bias, after=()):
    count, hidden = weights.shape[0], (weights.shape[1] - PAD) // 2
    n, own, width = len(hits), hits[0].shape[0], weights.shape[2]
    block = shape((own, width), BF16)
    wide = shape((own, count * hidden), BF16)
    got = call(
        name,
        3 * n + 2,
        functools.partial(expert_kernel, n, count, hidden),
        [block] * n + [wide] * (2 * n) + [shape((2, width), F32), shape((count, width), F32)],
        [
            Rows(flat(rows)),
            gain,
            bias,
            router,
            Rows(hits),
            Part(weights, 0, hidden),
            Rows(flat(grads), most=own // 2 if len(flat(grads)) > n else own),
            Part(weights, hidden, hidden),
        ],
        after,
    )
    return [list(got[i * n : (i + 1) * n]) for i in range(3)] + [got[-2], got[-1]]


def expert_chunk(rows, grads, hits, weights, router, gain, bias, moves=()):
    count, hidden = weights.shape[0], (weights.shape[1] - PAD) // 2
    width, own = weights.shape[2], hits[0].shape[0]
    shared = (weights, router, gain, bias)
    first = expert_blocks("experts_own", rows[:1], grads[:1], hits[:1], *shared)
    near = expert_blocks("experts_near", rows[1:3], grads[1:3], hits[1:3], *shared, first[0])
    far = expert_blocks("experts_far", rows[3:], grads[3:], hits[3:], *shared, near[0])
    back, dpre, gated = (first[i] + near[i] + far[i] for i in range(3))
    norm = first[3] + near[3] + far[3]
    moved = [to_head(back[flip], flip) for flip in moves]
    slabs = call(
        "experts_weights",
        8,
        functools.partial(expert_grad_kernel, count, hidden),
        shape((count, 2 * hidden + PAD, width), BF16),
        [
            Rows(gated),
            Rows(flat(grads), most=[own] * 3 + [own // 2] * 2),
            Rows(dpre),
            Rows(flat(rows)),
            first[4],
            near[4],
            far[4],
        ],
    )
    return back, moved, gated, norm, slabs


def expert_out(gated, weights, after):
    count, hidden = weights.shape[0], (weights.shape[1] - PAD) // 2
    return call(
        "experts_out",
        4,
        functools.partial(expert_out_kernel, count, hidden),
        [shape((gated[0].shape[0], weights.shape[2]), BF16)] * len(gated),
        [Rows(gated), Part(weights, hidden, hidden)],
        after,
    )


def shards(
    tokens,
    cotangent,
    segments,
    value_expert_route,
    output_expert_route,
    feedforward_route,
    attention_norm_gain,
    attention_norm_bias,
    feedforward_norm_gain,
    feedforward_norm_bias,
    query_projection,
    key_projection,
    value_selector,
    output_selector,
    value_experts,
    output_experts,
    feedforward_selector,
    expert_up_weight,
    expert_down_weight,
):
    n_data = lax.axis_size("dp")
    head, data = lax.axis_index("head"), lax.axis_index("dp")
    own, width = tokens.shape[1:]
    half = own // 2
    length = segments.shape[1]
    size = query_projection.shape[1]
    kinds = value_selector.shape[1]
    hidden = expert_up_weight.shape[2]
    scale = size ** (-0.5)
    mixed_width = kinds * size
    direct = n_data == width // LANES
    core = data % 2

    def arranged(value):
        return jnp.concatenate(
            [lax.dynamic_slice_in_dim(value, (head ^ k) * own, own, 0) for k in range(4)]
        )

    x_own, grad_own = tokens[0], cotangent[0]
    last = 3 * LANES + mixed_width
    all_own = call(
        "pack_weights",
        1,
        functools.partial(pack_in_kernel, kinds),
        shape((query_projection.shape[0], last + mixed_width), BF16),
        [
            query_projection,
            key_projection,
            value_experts[0],
            value_selector,
            output_selector,
            output_experts[0],
        ],
    )
    all_in = lax.all_gather(all_own, "dp", axis=0, tiled=True)
    in_all, out_all = Part(all_in, 0, last), Part(all_in, last, mixed_width)
    x = spread_rows(
        *call("split_rows", 1, split_kernel, [shape((half, width), BF16)] * 2, [x_own])
    )
    experts = 4 * n_data
    hot = jnp.sum(jax.nn.one_hot(feedforward_route[0], experts, dtype=BF16), 1)
    hot_rows = own * experts // width
    hot = hot.reshape(hot_rows, width)
    hot = jnp.concatenate([hot, jnp.zeros((-hot_rows % PAD, width), BF16)])
    grad_sent = call(
        "pack_grad",
        1,
        stack_kernel,
        shape((own + hot.shape[0], width), BF16),
        [Rows([grad_own, hot])],
        flat(x[1:3]),
    )
    near_x, near_y = to_head(grad_sent, 1), to_head(grad_sent, 2)
    far_top, far_bottom = to_head(near_y[:half], 1), to_head(near_x[half:], 2)
    grad = [[grad_own], [near_x], [near_y], [far_top, far_bottom]]

    def hits_of(rows):
        found = rows[:hot_rows].reshape(own, experts)
        return lax.dynamic_slice_in_dim(found, head * n_data, n_data, 1).astype(F32)

    hits = [hits_of(v) for v in (hot, near_x[own:], near_y[own:], far_bottom[half:])]
    ffn_own = call(
        "pack_experts",
        2,
        pack_experts_kernel,
        shape((2 * hidden + PAD, width), BF16),
        [expert_up_weight[0], expert_down_weight[0], feedforward_selector],
        flat(x[1:3]),
    )
    ffn_all = lax.all_gather(ffn_own, "dp", axis=0, tiled=False)
    router = ffn_all[:, 2 * hidden]

    spots = jnp.arange(length, dtype=jnp.int32)
    first_code = segments[0] * length
    info = arranged(
        jnp.concatenate(
            [
                first_code[:, None],
                (first_code + spots)[:, None],
                value_expert_route[0, :, 0],
                output_expert_route[0, :, 0] + kinds,
                jnp.zeros((length, 2), jnp.int32),
            ],
            1,
        )
    )
    code = arranged(first_code + spots)[None]
    gain1, bias1 = attention_norm_gain[None], attention_norm_bias[None]
    gain2, bias2 = feedforward_norm_gain[None], feedforward_norm_bias[None]
    query, key, value, experts_v, gate = call(
        "project",
        7,
        functools.partial(project_kernel, own, scale, kinds, size),
        [shape((length, size), BF16)] * 3
        + [shape((length, mixed_width), BF16), shape((length, LANES), F32)],
        [Rows(flat(x)), gain1, bias1, info, in_all],
        flat(grad[1:3]),
    )

    def attend(name, which, after=()):
        n = len(which)
        return call(
            name,
            2 * n + 1,
            functools.partial(attend_kernel, own, which, kinds, size),
            [shape((own, width), BF16)] * n
            + [
                shape((n * own, size), F32),
                shape((n * own, LANES), F32),
                shape((n * own, mixed_width), BF16),
            ],
            [query, key, value, info, code, gate, out_all],
            after,
        )

    part_far, att_far, lse_far, mixed_far = attend("attend_far", (3,))
    part_x, part_y, part_own, att_near, lse_near, mixed_near = attend(
        "attend_near", (1, 2, 0), (part_far, *grad[3])
    )

    def residual(name, parts, after=()):
        return call(
            name,
            2,
            residual_kernel,
            [shape((own, width), F32)] + [shape((half, width), BF16)] * 2,
            parts,
            after,
        )

    parts = [to_head(part, flip) for part, flip in ((part_far, 3), (part_x, 1), (part_y, 2))]
    resid, top, bottom = residual("residual", [x_own, part_own, *parts])
    rows = spread_rows(top, bottom)

    if n_data <= CHUNK:
        back, moved, gated, norm2, slabs = expert_chunk(
            rows, grad, hits, ffn_all, router, gain2, bias2, (1, 2, 3)
        )
    else:
        cut = lambda a: a.reshape((n_data // CHUNK, CHUNK) + a.shape[1:])
        hit_cuts = [
            h.reshape(own, n_data // CHUNK, CHUNK).transpose(1, 0, 2) for h in hits
        ]

        def step(carry, item):
            hit, rt, w = item
            got_back, _, got_gated, got_norm, slab = expert_chunk(
                rows, grad, hit, w, rt, gain2, bias2
            )
            got_out = expert_out(got_gated, w, ())
            add = lambda old, new: [o + v.astype(F32) for o, v in zip(old, new)]
            new = (add(carry[0], got_out), add(carry[1], got_back), carry[2] + got_norm)
            return new, slab

        zero = [jnp.zeros((own, width), F32)] * 4
        (out, back, norm2), slabs = lax.scan(
            step,
            (zero, zero, jnp.zeros((2, width), F32)),
            (hit_cuts, cut(router), cut(ffn_all)),
        )
        out, back = [v.astype(BF16) for v in out], [v.astype(BF16) for v in back]
        moved = [to_head(back[flip], flip) for flip in (1, 2, 3)]
        slabs = slabs.reshape((n_data,) + slabs.shape[2:])

    ffn_grads = lax.psum_scatter(slabs, "dp", scatter_dimension=0, tiled=True)
    d_resid, top, bottom = residual("residual_back", [grad_own, back[0], *moved], [slabs])
    d_pack = spread_rows(top, bottom)
    if n_data <= CHUNK:
        out = expert_out(gated, ffn_all, flat(d_pack[1:3]))

    dq, dsel, dk, dv = call(
        "attend_back",
        6,
        functools.partial(attend_back_kernel, own, (0, 1, 2), kinds, size),
        [
            shape((3 * own, size), BF16),
            shape((3 * own, LANES), F32),
            shape((length, size), F32),
            shape((length, size), F32),
        ],
        [query, key, info, code, lse_near, out_all, Rows(flat(d_pack[:3])), value, gate, att_near],
        out,
    )
    out_moved = [to_head(out[flip], flip) for flip in (3, 1, 2)]
    d_in, d_exp = call(
        "attend_last",
        5,
        functools.partial(attend_last_kernel, own, kinds, size),
        [shape((length, 3 * LANES), BF16), shape((length, mixed_width), BF16)],
        [
            query,
            key,
            info,
            code,
            lse_far,
            out_all,
            Rows(d_pack[3]),
            value,
            gate,
            att_far,
            dq,
            dsel,
            dk,
            dv,
            experts_v,
        ],
    )
    weight_part = call(
        "weights",
        6,
        weight_kernel,
        shape((width, 3 * LANES + 2 * mixed_width), BF16),
        [
            d_in,
            d_exp,
            Rows(flat(x)),
            gate,
            gain1,
            bias1,
            Rows(flat(d_pack)),
            Rows([mixed_near, mixed_far]),
        ],
        (ffn_grads, *out_moved[1:]),
    )
    d_far, d_x, d_y, d_own, norm1 = call(
        "input_back",
        6,
        functools.partial(input_grad_kernel, own, (3, 1, 2, 0), scale, size),
        [shape((own, width), BF16)] * 4 + [shape((2, width), F32)],
        [Rows(flat(x)), d_in, gate, gain1, in_all, d_exp],
        (weight_part,),
    )
    moved = [to_head(part, flip) for part, flip in ((d_far, 3), (d_x, 1), (d_y, 2))]
    block = shape((own, width), BF16)
    output = call("output", 2, finish_kernel, block, [resid, out[0], *out_moved])
    grad_tokens = call("token_grads", 2, finish_kernel, block, [d_resid, d_own, *moved])

    grads = lax.psum_scatter(weight_part, "dp", scatter_dimension=0, tiled=True).astype(F32)
    norms = jnp.concatenate([norm1, norm2])
    if direct:
        wide = width // 4
        take = lambda v, i, n: lax.dynamic_slice_in_dim(v, i * n, n, 1)
        shares = take(norms, head, wide)
        for flip in (1, 2, 3):
            shares = shares + to_head(take(norms, head ^ flip, wide), flip)
        cut = wide // n_data
        pairs = shares.reshape(4, n_data // 2, 2, cut)
        pick = lambda c: lax.dynamic_index_in_dim(pairs, c, 2, keepdims=False)
        pairs = (pick(core) + to_core(pick(1 - core))).reshape(4, -1)
        norms = take(pairs, data // 2, cut)
        for k in range(1, n_data // 2):
            norms = norms + to_later(take(pairs, (data // 2 + k) % (n_data // 2), cut), 2 * k)
    else:
        norms = lax.psum_scatter(norms, ("head", "dp"), scatter_dimension=1, tiled=True)

    ffn_grads = ffn_grads[0].astype(F32)
    two, three = 2 * size, 3 * LANES
    return (
        output[None],
        grad_tokens[None],
        norms,
        grads[:, :size] * scale,
        grads[:, size:two],
        grads[:, two : two + kinds],
        grads[:, two + kinds : two + 2 * kinds],
        grads[:, three:last][None],
        grads[:, last:].T[None],
        ffn_grads[2 * hidden : 2 * hidden + 1],
        ffn_grads[:hidden].T[None],
        ffn_grads[hidden : 2 * hidden][None],
    )


def solution(mesh):
    placed = (
        P("dp", "head", None),
        P("dp", "head", None),
        P("dp", None),
        P("dp", None, "head", None),
        P("dp", None, "head", None),
        P("dp", "head", None),
        P(),
        P(),
        P(),
        P(),
        P("dp", "head"),
        P("dp", "head"),
        P("dp", "head"),
        P("dp", "head"),
        P("head", "dp", None),
        P("head", None, "dp"),
        P(("head", "dp"), None),
        P(("head", "dp"), None, None),
        P(("head", "dp"), None, None),
    )
    return jax.shard_map(
        shards,
        mesh=mesh,
        in_specs=placed,
        out_specs=(
            P("dp", "head", None),
            P("dp", "head", None),
            P(None, ("head", "dp")),
            P("dp", "head"),
            P("dp", "head"),
            P("dp", "head"),
            P("dp", "head"),
            P("head", "dp", None),
            P("head", None, "dp"),
            P(("head", "dp"), None),
            P(("head", "dp"), None, None),
            P(("head", "dp"), None, None),
        ),
        check_vma=False,
    )
```

```python
import functools

import jax
import jax.numpy as jnp
from jax import lax
from jax.experimental import pallas as pl
from jax.experimental.pallas import tpu as pltpu
from jax.sharding import PartitionSpec as P

EPS = 1e-05
F32 = jnp.float32
BF16 = jnp.bfloat16
CHUNK = 8
LANES = 128
WIDE = 256
PAD = 16
MEAN, SPREAD = 16, 17
VMEM_BYTES = 56 * 2**20
ROOT_HALF = 0.7071067811865476
INV_ROOT_2PI = 0.3989422804014327
ANY = pl.BlockSpec(memory_space=pl.ANY)
SMEM = pl.BlockSpec(memory_space=pltpu.SMEM)


def dot(a, b, dims):
    return lax.dot_general(a, b, (dims, ((), ())), preferred_element_type=F32)


def nn(a, b):
    return dot(a, b, ((1,), (0,)))


def nt(a, b):
    return dot(a, b, ((1,), (1,)))


def tn(a, b):
    return dot(a, b, ((0,), (0,)))


def shape(dims, kind):
    return jax.ShapeDtypeStruct(dims, kind)


def cost(micros):
    return pl.CostEstimate(flops=int(micros * 1e9), bytes_accessed=0, transcendentals=0)


class Rows:
    def __init__(self, arrays, most=1 << 20):
        self.arrays = list(arrays)
        most = most if isinstance(most, list) else [most] * len(self.arrays)
        self.counts = [min(a.shape[0], m) for a, m in zip(arrays, most)]
        self.dims = (sum(self.counts),) + tuple(arrays[0].shape[1:])


class Part:
    def __init__(self, array, first, count):
        self.arrays, self.first, self.count = [array], first, count
        self.dims = (array.shape[0], count) + tuple(array.shape[2:])


class In:
    def __init__(self, ref, copies, spans):
        self.ref, self.copies, self.spans, self.waited = ref, copies, spans, set()

    def ready(self, first=0, count=1 << 20):
        for i, (copy, (start, size)) in enumerate(zip(self.copies, self.spans)):
            if i not in self.waited and start < first + count and first < start + size:
                copy.wait()
                self.waited.add(i)
        return self.ref

    def rows(self, first, count):
        return self.ready(first, count)[pl.ds(first, count), :]

    def __getitem__(self, at):
        return self.ready()[at]


class Split:
    def __init__(self, n, dims, kind):
        self.n, self.block, self.kind = n, dims, kind
        self.shape, self.dtype = (n * dims[0], dims[1]), kind


class Out:
    def __init__(self, ref, dest, sems):
        self.ref, self.dest, self.sems, self.copies = ref, dest, sems, []

    def block(self, i, count):
        at = pl.ds(i * count if isinstance(i, int) else pl.multiple_of(i * count, count), count)
        return pltpu.make_async_copy(self.ref.at[at], self.dest.at[at], self.sems.at[i])

    def blocks_sent(self, n, count):
        self.copies += [self.block(i, count) for i in range(n)]

    def __setitem__(self, at, value):
        self.ref[at] = value

    def __getitem__(self, at):
        return self.ref[at]

    def send(self, first=None, count=None):
        if isinstance(self.dest, list):
            n = self.dest[0].shape[0]
            for i, dest in enumerate(self.dest):
                source = self.ref.at[pl.ds(i * n, n)]
                self.copies.append(pltpu.make_async_copy(source, dest, self.sems.at[i]))
                self.copies[-1].start()
            return
        source, dest = self.ref, self.dest
        if first is not None:
            source, dest = source.at[pl.ds(first, count)], dest.at[pl.ds(first, count)]
        copy = pltpu.make_async_copy(source, dest, self.sems.at[len(self.copies)])
        copy.start()
        self.copies.append(copy)


def call(name, micros, body, outs, args, after=()):
    entries = [a if isinstance(a, (Rows, Part)) else Rows([a]) for a in args]
    arrays = [a for e in entries for a in e.arrays]
    single = not isinstance(outs, (list, tuple))
    out_list = [outs] if single else list(outs)

    def kernel(*refs):
        refs = list(refs)
        sources, refs = refs[: len(arrays)], refs[len(arrays) + len(after) :]
        dests = []
        for out in out_list:
            if isinstance(out, Split):
                dests.append(refs[: out.n])
                refs = refs[out.n :]
            else:
                dests.append(refs.pop(0))
        bufs, refs = refs[: len(entries)], refs[len(entries) :]
        in_sems, refs = refs[: len(entries)], refs[len(entries) :]
        out_bufs, out_sems = refs[: len(out_list)], refs[len(out_list) :]
        ins = []
        for entry, buf, sems in zip(entries, bufs, in_sems):
            pairs, spans, at = [], [], 0
            for i, array in enumerate(entry.arrays):
                source, n = sources.pop(0), array.shape[0]
                if isinstance(entry, Rows) and entry.counts[i] < n:
                    n = entry.counts[i]
                    source = source.at[pl.ds(0, n)]
                spans.append((at, n))
                if isinstance(entry, Part):
                    pairs.append((source.at[:, pl.ds(entry.first, entry.count)], buf))
                elif len(entry.arrays) == 1:
                    pairs.append((source, buf))
                else:
                    pairs.append((source, buf.at[pl.ds(at, n)]))
                at += n
            copies = [
                pltpu.make_async_copy(source, dest, sems.at[i])
                for i, (source, dest) in enumerate(pairs)
            ]
            for copy in copies:
                copy.start()
            ins.append(In(buf, copies, spans))
        results = [Out(b, d, s) for b, d, s in zip(out_bufs, dests, out_sems)]
        body(*ins, *results)
        for entry in ins:
            entry.ready()
        for result in results:
            if not result.copies:
                result.send()
        for result in results:
            for copy in result.copies:
                copy.wait()

    shapes = []
    for out in out_list:
        shapes += [shape(out.block, out.kind)] * out.n if isinstance(out, Split) else [out]
    return pl.pallas_call(
        kernel,
        name=name,
        out_shape=shapes[0] if single else shapes,
        in_specs=[ANY] * (len(arrays) + len(after)),
        out_specs=ANY if single else [ANY] * len(shapes),
        scratch_shapes=[pltpu.VMEM(e.dims, e.arrays[0].dtype) for e in entries]
        + [pltpu.SemaphoreType.DMA((len(e.arrays),)) for e in entries]
        + [pltpu.VMEM(o.shape, o.dtype) for o in out_list]
        + [pltpu.SemaphoreType.DMA((8,)) for o in out_list],
        compiler_params=pltpu.CompilerParams(vmem_limit_bytes=VMEM_BYTES),
        cost_estimate=cost(micros),
    )(*arrays, *after)


def repeat(n, body):
    if n == 1:
        body(0)
    else:
        lax.fori_loop(0, n, lambda i, carry: (body(i), carry)[1], 0)


def block_at(i, count):
    return pl.ds(i * count if isinstance(i, int) else pl.multiple_of(i * count, count), count)


def pack_in_kernel(kinds, q, k, v, vsel, osel, o, out):
    size = q.ref.shape[1]
    out[:, 3 * LANES + kinds * size :] = o[...].T
    out[:, 2 * size : 3 * LANES] = jnp.zeros((q.ref.shape[0], LANES), BF16)
    out[:, :size] = q[...]
    out[:, size : 2 * size] = k[...]
    out[:, 2 * size : 2 * size + kinds] = vsel[...]
    out[:, 2 * size + kinds : 2 * size + 2 * kinds] = osel[...]
    out[:, 3 * LANES : 3 * LANES + kinds * size] = v[...]


def pack_experts_kernel(up, down, router, out):
    hidden = up.ref.shape[1]
    out[:hidden, :] = up[...].T
    out[hidden : 2 * hidden, :] = down[...]
    out[2 * hidden :, :] = jnp.broadcast_to(router[...], (PAD, router.ref.shape[1]))


def stack_kernel(pieces, out):
    out[...] = pieces[...]


def split_copy_kernel(a, b, top, bottom):
    top[...] = a[...]
    bottom[...] = b[...]


def split_kernel(rows, top, bottom):
    half = top.ref.shape[0]
    top[...] = rows[:half, :]
    bottom[...] = rows[half:, :]


def residual_kernel(*refs):
    parts, (total, top, bottom) = refs[:-3], refs[-3:]
    half = top.ref.shape[0]
    for first, low in ((0, top), (half, bottom)):
        at = pl.ds(first, half)
        found = parts[0][at, :].astype(F32)
        for part in parts[1:]:
            found = found + part[at, :].astype(F32)
        low[...] = found.astype(BF16)
        low.send()
        total[at, :] = found
        total.send(first, half)


def finish_kernel(*refs):
    parts, out = refs[:-1], refs[-1]
    found = parts[0][...].astype(F32)
    for part in parts[1:]:
        found = found + part[...].astype(F32)
    out[...] = found.astype(BF16)


def finish_experts_kernel(found, up, down, router):
    hidden = up.ref.shape[1]
    up[...] = found[:hidden, :].astype(F32).T
    down[...] = found[hidden : 2 * hidden, :].astype(F32)
    router[...] = found[2 * hidden : 2 * hidden + 1, :].astype(F32)


def finish_weights_kernel(scale, kinds, found, q, k, vsel, osel, v, o):
    size = q.ref.shape[1]
    at = 3 * LANES
    q[...] = found[:, :size].astype(F32) * scale
    k[...] = found[:, size : 2 * size].astype(F32)
    both = found[:, 2 * size : at].astype(F32)
    vsel[...] = both[:, :kinds]
    osel[...] = both[:, kinds : 2 * kinds]
    v[...] = found[:, at : at + kinds * size].astype(F32)
    o[...] = found[:, at + kinds * size :].astype(F32).T


def layer_stats(values):
    mean = jnp.mean(values, -1, keepdims=True)
    center = values - mean
    return mean, lax.rsqrt(jnp.mean(center * center, -1, keepdims=True) + EPS)


def norm_back(scaled, unit, spread):
    return spread * (
        scaled
        - jnp.mean(scaled, -1, keepdims=True)
        - unit * jnp.mean(scaled * unit, -1, keepdims=True)
    )


def project_kernel(own, scale, kinds, size, x, gain, bias, info, w, q, k, v, ev, gate):
    for value in (x, gain, bias, info, w):
        value.ready()

    def block(b):
        at = block_at(b, own)
        rows = x.ref[at, :]
        mean, spread = layer_stats(rows.astype(F32))
        normed = ((rows.astype(F32) - mean) * spread * gain.ref[...] + bias.ref[...]).astype(BF16)
        first = nn(normed, w.ref[:, : 3 * LANES])
        q[at, :] = (first[:, :size] * scale).astype(BF16)
        k[at, :] = first[:, size : 2 * size].astype(BF16)
        lane = lax.broadcasted_iota(jnp.int32, (own, LANES), 1)
        chosen = lane < 0
        for c in range(2, 6):
            chosen = chosen | (lane == info.ref[at, c : c + 1])
        found = jnp.where(chosen, jax.nn.sigmoid(first[:, 2 * size :]), 0.0)
        gate[at, :] = jnp.where(lane == MEAN, mean, jnp.where(lane == SPREAD, spread, found))
        experts = nn(rows, w.ref[:, 3 * LANES :])
        ev[at, :] = experts.astype(BF16)
        ev.block(b, own).start()
        value = found[:, :1] * experts[:, :size]
        for e in range(1, kinds):
            value = value + found[:, e : e + 1] * experts[:, e * size : (e + 1) * size]
        v[at, :] = value.astype(BF16)

    repeat(4, block)
    ev.blocks_sent(4, own)


def visible(info, code):
    return (code >= info[:, 0:1]) & (code <= info[:, 1:2])


def attend_kernel(own, kinds, size, q, k, v, info, code, gate, w, parts, att, lse, mixed):
    for value in (q, k, v, info, code, gate, w):
        value.ready()

    def block(b):
        at = block_at(b, own)
        scores = jnp.where(
            visible(info.ref[at, :], code.ref[...]), nt(q.ref[at, :], k.ref[...]), -jnp.inf
        )
        top = jnp.max(scores, -1, keepdims=True)
        weights = jnp.exp(scores - top)
        total = jnp.sum(weights, -1, keepdims=True)
        probs = (weights / total).astype(BF16)
        found = nn(probs, v.ref[...])
        att[at, :] = found
        lse[at, :] = jnp.broadcast_to(top + jnp.log(total), (own, LANES))
        opened = gate.ref[at, :]
        for e in range(kinds):
            mixed[at, e * size : (e + 1) * size] = (
                opened[:, kinds + e : kinds + e + 1] * found
            ).astype(BF16)
        parts[at, :] = nt(mixed[at, :], w.ref[...]).astype(BF16)

    repeat(4, block)
    parts.send()


def expert_kernel(n_blocks, count, hidden, rows_in, gain, bias, router, hits, up_in, grad_in, down_in, backs, dpre, gated, norm, route):
    width = rows_in.ref.shape[1]
    own = rows_in.ref.shape[0] // n_blocks
    for value in (rows_in, gain, bias, router, hits, up_in):
        value.ready()
    norm[...] = jnp.zeros(norm.ref.shape, F32)
    route[...] = jnp.zeros(route.ref.shape, F32)
    if n_blocks > 1:
        grad_in.ready()
        down_in.ready()

    def block(i):
        at = block_at(i, own)
        rows = rows_in.ref[at, :]
        mean, spread = layer_stats(rows.astype(F32))
        unit = (rows.astype(F32) - mean) * spread
        normed = (unit * gain.ref[...] + bias.ref[...]).astype(BF16)
        gate = jax.nn.sigmoid(nt(normed, router.ref[...])) * hits.ref[at, :]
        pre = nt(rows, up_in.ref[...].reshape(count * hidden, width))
        if n_blocks == 1:
            grad_in.ready()
            down_in.ready()
        back = nt(grad_in.ref[at, :], down_in.ref[...].reshape(count * hidden, width))
        d_gate = []
        for e in range(count):
            col = slice(e * hidden, (e + 1) * hidden)
            p, b, g = pre[:, col], back[:, col], gate[:, e : e + 1]
            bell = 0.5 * (1.0 + lax.erf(p * ROOT_HALF))
            active = p * bell
            slope = bell + p * jnp.exp(-0.5 * p * p) * INV_ROOT_2PI
            gated[at, col] = (g * active).astype(BF16)
            dpre[at, col] = (g * b * slope).astype(BF16)
            d_gate.append(jnp.sum(active * b, -1, keepdims=True))
        gated.block(i, own).start()
        dpre.block(i, own).start()
        d_logit = (jnp.concatenate(d_gate, 1) * gate * (1.0 - gate)).astype(BF16)
        d_n2 = nn(d_logit, router.ref[...])
        backs[at, :] = (
            nn(dpre[at, :], up_in.ref[...].reshape(count * hidden, width))
            + norm_back(d_n2 * gain.ref[...], unit, spread)
        ).astype(BF16)
        norm[...] += jnp.concatenate(
            [jnp.sum(d_n2 * unit, 0, keepdims=True), jnp.sum(d_n2, 0, keepdims=True)], 0
        )
        route[...] += tn(d_logit, normed)

    repeat(n_blocks, block)
    gated.blocks_sent(n_blocks, own)
    dpre.blocks_sent(n_blocks, own)
    backs.send()


def expert_out_kernel(count, hidden, gated, down, outs):
    own, width = gated.ref.shape[0] // 4, outs.ref.shape[1]
    gated.ready()
    down.ready()

    def block(i):
        at = block_at(i, own)
        rows = gated.ref[at, :]
        outs[at, :] = nn(rows, down.ref[...].reshape(count * hidden, width)).astype(BF16)

    repeat(4, block)
    outs.send()


def expert_grad_kernel(count, hidden, gated, grad, dpre, rows, *refs):
    routes, out = refs[:-1], refs[-1]
    pair = WIDE // hidden
    for value in (gated, grad, dpre, rows, *routes):
        value.ready()
    for e in range(count):
        route = sum(r.ref[e : e + 1, :] for r in routes)
        out[e, 2 * hidden :, :] = jnp.broadcast_to(route, (PAD, route.shape[1])).astype(BF16)

    def block(c):
        col = block_at(c, WIDE)
        down = tn(gated.ref[:, col], grad.ref[...]).astype(BF16)
        up = tn(dpre.ref[:, col], rows.ref[...]).astype(BF16)
        for j in range(pair):
            out[c * pair + j, :hidden, :] = up[j * hidden : (j + 1) * hidden]
            out[c * pair + j, hidden : 2 * hidden, :] = down[j * hidden : (j + 1) * hidden]
        out.block(c, pair).start()

    repeat(count // pair, block)
    out.blocks_sent(count // pair, pair)


def attend_back_rows(own, b, d_rows, kinds, size, w, q, k, v, info, code, gate, att, lse):
    at = block_at(b, own)
    lane = lax.broadcasted_iota(jnp.int32, (own, LANES), 1)
    found, opened, queries = att.ref[at, :], gate.ref[at, :], q.ref[at, :]
    scores = jnp.where(visible(info.ref[at, :], code.ref[...]), nt(queries, k.ref[...]), -jnp.inf)
    probs = jnp.exp(scores - lse.ref[at, 0:1])
    d_mixed = nn(d_rows, w.ref[...])
    d_att = jnp.zeros((own, size), F32)
    d_sel = jnp.zeros((own, LANES), F32)
    for e in range(kinds):
        part = d_mixed[:, e * size : (e + 1) * size]
        d_att = d_att + opened[:, kinds + e : kinds + e + 1] * part
        d_sel = jnp.where(lane == kinds + e, jnp.sum(part * found, -1, keepdims=True), d_sel)
    d_att = d_att.astype(BF16)
    d_probs = nt(d_att, v.ref[...])
    centered = jnp.sum(probs * d_probs, -1, keepdims=True)
    d_scores = (probs * (d_probs - centered)).astype(BF16)
    return (
        nn(d_scores, k.ref[...]).astype(BF16),
        d_sel * opened * (1.0 - opened),
        tn(d_scores, queries),
        tn(probs.astype(BF16), d_att),
    )


def attend_back_kernel(own, n, kinds, size, q, k, info, code, lse, w, d_rows, v, gate, att, dq, dsel, dk, dv):
    for value in (q, k, info, code, lse, w, d_rows, v, gate, att):
        value.ready()
    dk[...] = jnp.zeros(dk.ref.shape, F32)
    dv[...] = jnp.zeros(dv.ref.shape, F32)

    def block(b):
        at = block_at(b, own)
        query, selector, key, value = attend_back_rows(
            own, b, d_rows.ref[at, :], kinds, size, w, q, k, v, info, code, gate, att, lse
        )
        dq[at, :] = query
        dsel[at, :] = selector
        dk[...] += key
        dv[...] += value

    repeat(n, block)


def attend_last_kernel(own, kinds, size, q, k, info, code, lse, w, d_rows, v, gate, att, dq, dsel, dk, dv, ev, din, dexp):
    last = 3 * own
    for value in (q, k, info, code, lse, w, d_rows, v, gate, att):
        value.ready()
    query, selector, more_k, more_v = attend_back_rows(
        own, 3, d_rows.ref[...], kinds, size, w, q, k, v, info, code, gate, att, lse
    )
    for value in (dq, dsel, dk, dv, ev):
        value.ready()
    din[last:, :size] = query
    din[:last, :size] = dq.ref[...]
    dk.ref[...] += more_k
    dv.ref[...] += more_v
    dsel.ref[last:, :] = selector
    lane = lax.broadcasted_iota(jnp.int32, (own, LANES), 1)

    def block(b):
        at = block_at(b, own)
        opened, value = gate.ref[at, :], dv.ref[at, :]
        factor = opened * (1.0 - opened)
        din[at, size : 2 * size] = dk.ref[at, :].astype(BF16)
        d_sel = dsel.ref[at, :]
        for e in range(kinds):
            col = slice(e * size, (e + 1) * size)
            moved = jnp.sum(ev.ref[at, col].astype(F32) * value, -1, keepdims=True)
            d_sel = jnp.where(lane == e, moved * factor, d_sel)
            dexp[at, col] = (opened[:, e : e + 1] * value).astype(BF16)
        din[at, 2 * size :] = d_sel.astype(BF16)

    repeat(4, block)


def weight_kernel(din, dexp, x, gate, gain, bias, d_rows, mixed, out):
    width = x.ref.shape[1]
    for value in (din, dexp, x, gate, gain, bias, d_rows, mixed):
        value.ready()
    mean, spread = gate.ref[:, MEAN : MEAN + 1], gate.ref[:, SPREAD : SPREAD + 1]
    first_end = din.ref.shape[1]
    second_end = first_end + dexp.ref.shape[1]

    for first in range(0, width, WIDE):
        at = slice(first, first + WIDE)
        rows = x.ref[:, at]
        normed = (rows.astype(F32) - mean) * spread * gain.ref[:, at] + bias.ref[:, at]
        out[at, :first_end] = tn(normed.astype(BF16), din.ref[...]).astype(BF16)
        out[at, first_end:second_end] = tn(rows, dexp.ref[...]).astype(BF16)
        out[at, second_end:] = tn(d_rows.ref[:, at], mixed.ref[...]).astype(BF16)
        out.send(first, WIDE)


def input_grad_kernel(own, scale, size, x, din, gate, gain, w, dexp, outs, norm):
    for value in (x, din, gate, gain, w, dexp):
        value.ready()
    norm[...] = jnp.zeros(norm.ref.shape, F32)

    def block(b):
        at = block_at(b, own)
        spread = gate.ref[at, SPREAD : SPREAD + 1]
        unit = (x.ref[at, :].astype(F32) - gate.ref[at, MEAN : MEAN + 1]) * spread
        d_normed = nt(din.ref[at, :size], w.ref[:, :size]) * scale + nt(
            din.ref[at, size:], w.ref[:, size : 3 * LANES]
        )
        outs[at, :] = (
            norm_back(d_normed * gain.ref[...], unit, spread)
            + nt(dexp.ref[at, :], w.ref[:, 3 * LANES :])
        ).astype(BF16)
        norm[...] += jnp.concatenate(
            [jnp.sum(d_normed * unit, 0, keepdims=True), jnp.sum(d_normed, 0, keepdims=True)], 0
        )

    repeat(4, block)
    outs.send()


def to_head(value, flip):
    n = lax.axis_size("head")
    return lax.ppermute(value, "head", [(i, i ^ flip) for i in range(n)])


def near_rows(top, bottom):
    y_top, x_bottom = to_head(top, 2), to_head(bottom, 1)
    y_bottom, x_top = to_head(bottom, 2), to_head(top, 1)
    return [[x_top, x_bottom], [y_top, y_bottom]]


def far_rows(near):
    return [to_head(near[1][0], 1), to_head(near[0][1], 2)]


def spread_rows(top, bottom):
    near = near_rows(top, bottom)
    return [[top, bottom], *near, far_rows(near)]


def far_rows_after(near, after):
    half = shape(near[0][0].shape, BF16)
    passed = call(
        "relay", 1, split_copy_kernel, [half, half], [near[1][0], near[0][1]], after
    )
    return [to_head(passed[0], 1), to_head(passed[1], 2)]


def flat(blocks):
    return [piece for block in blocks for piece in block]


def expert_blocks(name, rows, grads, hits, weights, router, gain, bias, after=()):
    count, hidden = weights.shape[0], (weights.shape[1] - PAD) // 2
    n, own, width = len(hits), hits[0].shape[0], weights.shape[2]
    wide = shape((n * own, count * hidden), BF16)
    got = call(
        name,
        3 * n + 2,
        functools.partial(expert_kernel, n, count, hidden),
        [
            Split(n, (own, width), BF16),
            wide,
            wide,
            shape((2, width), F32),
            shape((count, width), F32),
        ],
        [
            Rows(flat(rows)),
            gain,
            bias,
            router,
            Rows(hits),
            Part(weights, 0, hidden),
            Rows(flat(grads), most=[own // min(2, len(g)) for g in grads for _ in g]),
            Part(weights, hidden, hidden),
        ],
        after,
    )
    return [list(got[:n]), [got[n]], [got[n + 1]], got[-2], got[-1]]


def expert_chunk(rows, spread, grads, hits, weights, router, gain, bias, moves=()):
    count, hidden = weights.shape[0], (weights.shape[1] - PAD) // 2
    width, own = weights.shape[2], hits[0].shape[0]
    shared = (weights, router, gain, bias)
    first = expert_blocks("experts_own", rows[:1], grads[:1], hits[:1], *shared)
    rows = [rows[0], *spread(first[0])]
    near = expert_blocks(
        "experts_near", rows[1:3], grads[1:3], hits[1:3], *shared, (first[0][0], *rows[3])
    )
    far = expert_blocks("experts_far", rows[3:], grads[3:], hits[3:], *shared, near[0])
    back, dpre, gated = (first[i] + near[i] + far[i] for i in range(3))
    norm = first[3] + near[3] + far[3]
    moved = [to_head(back[flip], flip) for flip in moves]
    slabs = call(
        "experts_weights",
        8,
        functools.partial(expert_grad_kernel, count, hidden),
        shape((count, 2 * hidden + PAD, width), BF16),
        [
            Rows(gated),
            Rows(flat(grads), most=[own] * 3 + [own // 2] * 2),
            Rows(dpre),
            Rows(flat(rows)),
            first[4],
            near[4],
            far[4],
        ],
        moved[:2],
    )
    return back, moved, gated, norm, slabs


def expert_out(gated, weights, after):
    count, hidden = weights.shape[0], (weights.shape[1] - PAD) // 2
    return call(
        "experts_out",
        12,
        functools.partial(expert_out_kernel, count, hidden),
        [Split(4, (sum(g.shape[0] for g in gated) // 4, weights.shape[2]), BF16)],
        [Rows(gated), Part(weights, hidden, hidden)],
        after,
    )


def shards(
    tokens,
    cotangent,
    segments,
    value_expert_route,
    output_expert_route,
    feedforward_route,
    attention_norm_gain,
    attention_norm_bias,
    feedforward_norm_gain,
    feedforward_norm_bias,
    query_projection,
    key_projection,
    value_selector,
    output_selector,
    value_experts,
    output_experts,
    feedforward_selector,
    expert_up_weight,
    expert_down_weight,
):
    n_data = lax.axis_size("dp")
    head = lax.axis_index("head")
    own, width = tokens.shape[1:]
    half = own // 2
    length = segments.shape[1]
    size = query_projection.shape[1]
    kinds = value_selector.shape[1]
    hidden = expert_up_weight.shape[2]
    scale = size ** (-0.5)
    mixed_width = kinds * size

    def arranged(value):
        return jnp.concatenate(
            [lax.dynamic_slice_in_dim(value, (head ^ k) * own, own, 0) for k in range(4)]
        )

    x_own, grad_own = tokens[0], cotangent[0]
    last = 3 * LANES + mixed_width
    all_own = call(
        "pack_weights",
        1,
        functools.partial(pack_in_kernel, kinds),
        shape((query_projection.shape[0], last + mixed_width), BF16),
        [
            query_projection,
            key_projection,
            value_experts[0],
            value_selector,
            output_selector,
            output_experts[0],
        ],
    )
    all_in = lax.all_gather(all_own, "dp", axis=0, tiled=True)
    in_all, out_all = Part(all_in, 0, last), Part(all_in, last, mixed_width)
    x = spread_rows(
        *call("split_rows", 1, split_kernel, [shape((half, width), BF16)] * 2, [x_own])
    )
    experts = 4 * n_data
    hot = jnp.sum(jax.nn.one_hot(feedforward_route[0], experts, dtype=BF16), 1)
    hot_rows = own * experts // width
    hot = hot.reshape(hot_rows, width)
    hot = jnp.concatenate([hot, jnp.zeros((-hot_rows % PAD, width), BF16)])
    grad_sent = call(
        "pack_grad",
        1,
        stack_kernel,
        shape((own + hot.shape[0], width), BF16),
        [Rows([grad_own, hot])],
    )
    near_x, near_y = to_head(grad_sent, 1), to_head(grad_sent, 2)
    far_top, far_bottom = to_head(near_y[:half], 1), to_head(near_x[half:], 2)
    grad = [[grad_own], [near_x], [near_y], [far_top, far_bottom]]

    def hits_of(rows):
        found = rows[:hot_rows].reshape(own, experts)
        return lax.dynamic_slice_in_dim(found, head * n_data, n_data, 1).astype(F32)

    hits = [hits_of(v) for v in (hot, near_x[own:], near_y[own:], far_bottom[half:])]
    ffn_own = call(
        "pack_experts",
        2,
        pack_experts_kernel,
        shape((2 * hidden + PAD, width), BF16),
        [expert_up_weight[0], expert_down_weight[0], feedforward_selector],
        flat(x[1:3]),
    )
    ffn_all = lax.all_gather(ffn_own, "dp", axis=0, tiled=False)
    router = ffn_all[:, 2 * hidden]

    spots = jnp.arange(length, dtype=jnp.int32)
    first_code = segments[0] * length
    info = arranged(
        jnp.concatenate(
            [
                first_code[:, None],
                (first_code + spots)[:, None],
                value_expert_route[0, :, 0],
                output_expert_route[0, :, 0] + kinds,
                jnp.zeros((length, 2), jnp.int32),
            ],
            1,
        )
    )
    code = arranged(first_code + spots)[None]
    gain1, bias1 = attention_norm_gain[None], attention_norm_bias[None]
    gain2, bias2 = feedforward_norm_gain[None], feedforward_norm_bias[None]
    query, key, value, experts_v, gate = call(
        "project",
        7,
        functools.partial(project_kernel, own, scale, kinds, size),
        [shape((length, size), BF16)] * 3
        + [shape((length, mixed_width), BF16), shape((length, LANES), F32)],
        [Rows(flat(x)), gain1, bias1, info, in_all],
    )

    part_own, part_x, part_y, part_far, att, lse, mixed = call(
        "attend",
        8,
        functools.partial(attend_kernel, own, kinds, size),
        [
            Split(4, (own, width), BF16),
            shape((length, size), F32),
            shape((length, LANES), F32),
            shape((length, mixed_width), BF16),
        ],
        [query, key, value, info, code, gate, out_all],
        flat(grad[1:]),
    )

    def residual(name, parts, after=()):
        return call(
            name,
            2,
            residual_kernel,
            [shape((own, width), F32)] + [shape((half, width), BF16)] * 2,
            parts,
            after,
        )

    parts = [to_head(part, flip) for part, flip in ((part_far, 3), (part_x, 1), (part_y, 2))]
    resid, top, bottom = residual("residual", [x_own, part_own, *parts])
    near = near_rows(top, bottom)

    if n_data <= CHUNK:
        back, moved, gated, norm2, slabs = expert_chunk(
            [[top, bottom]],
            lambda after: [*near, far_rows_after(near, after)],
            grad,
            hits,
            ffn_all,
            router,
            gain2,
            bias2,
            (1, 2, 3),
        )
    else:
        cut = lambda a: a.reshape((n_data // CHUNK, CHUNK) + a.shape[1:])
        others = [*near, far_rows(near)]
        hit_cuts = [
            h.reshape(own, n_data // CHUNK, CHUNK).transpose(1, 0, 2) for h in hits
        ]

        def step(carry, item):
            hit, rt, w = item
            got_back, _, got_gated, got_norm, slab = expert_chunk(
                [[top, bottom]], lambda _: others, grad, hit, w, rt, gain2, bias2
            )
            got_out = expert_out(got_gated, w, ())
            add = lambda old, new: [o + v.astype(F32) for o, v in zip(old, new)]
            new = (add(carry[0], got_out), add(carry[1], got_back), carry[2] + got_norm)
            return new, slab

        zero = [jnp.zeros((own, width), F32)] * 4
        (out, back, norm2), slabs = lax.scan(
            step,
            (zero, zero, jnp.zeros((2, width), F32)),
            (hit_cuts, cut(router), cut(ffn_all)),
        )
        out, back = [v.astype(BF16) for v in out], [v.astype(BF16) for v in back]
        moved = [to_head(back[flip], flip) for flip in (1, 2, 3)]
        slabs = slabs.reshape((n_data,) + slabs.shape[2:])

    ffn_grads = lax.psum_scatter(slabs, "dp", scatter_dimension=0, tiled=True)
    if n_data <= CHUNK:
        out = expert_out(gated, ffn_all, ())
    d_resid, top, bottom = residual("residual_back", [grad_own, back[0], *moved], [slabs, *out])
    d_pack = spread_rows(top, bottom)

    dq, dsel, dk, dv = call(
        "attend_back",
        6,
        functools.partial(attend_back_kernel, own, 3, kinds, size),
        [
            shape((3 * own, size), BF16),
            shape((length, LANES), F32),
            shape((length, size), F32),
            shape((length, size), F32),
        ],
        [query, key, info, code, lse, out_all, Rows(flat(d_pack[:3])), value, gate, att],
        out,
    )
    out_moved = [to_head(out[flip], flip) for flip in (3, 1, 2)]
    d_in, d_exp = call(
        "attend_last",
        5,
        functools.partial(attend_last_kernel, own, kinds, size),
        [shape((length, 3 * LANES), BF16), shape((length, mixed_width), BF16)],
        [
            query,
            key,
            info,
            code,
            lse,
            out_all,
            Rows(d_pack[3]),
            value,
            gate,
            att,
            dq,
            dsel,
            dk,
            dv,
            experts_v,
        ],
    )
    weight_part = call(
        "weights",
        6,
        weight_kernel,
        shape((width, 3 * LANES + 2 * mixed_width), BF16),
        [
            d_in,
            d_exp,
            Rows(flat(x)),
            gate,
            gain1,
            bias1,
            Rows(flat(d_pack)),
            mixed,
        ],
        (ffn_grads, *out_moved[1:]),
    )
    d_own, d_x, d_y, d_far, norm1 = call(
        "input_back",
        6,
        functools.partial(input_grad_kernel, own, scale, size),
        [Split(4, (own, width), BF16), shape((2, width), F32)],
        [Rows(flat(x)), d_in, gate, gain1, in_all, d_exp],
        (weight_part,),
    )
    moved = [to_head(part, flip) for part, flip in ((d_far, 3), (d_x, 1), (d_y, 2))]
    block = shape((own, width), BF16)
    up_grad, down_grad, router_grad = call(
        "finish_experts",
        2,
        finish_experts_kernel,
        [shape((width, hidden), F32), shape((hidden, width), F32), shape((1, width), F32)],
        [ffn_grads[0]],
    )
    output = call(
        "output",
        2,
        finish_kernel,
        block,
        [resid, out[0], *out_moved],
        moved[1:],
    )
    grad_tokens = call(
        "token_grads", 2, finish_kernel, block, [d_resid, d_own, *moved]
    )

    part = width // n_data
    grads = lax.psum_scatter(weight_part, "dp", scatter_dimension=0, tiled=True)
    query_grad, key_grad, value_sel, output_sel, value_grad, output_grad = call(
        "finish_weights",
        2,
        functools.partial(finish_weights_kernel, scale, kinds),
        [
            shape((part, size), F32),
            shape((part, size), F32),
            shape((part, kinds), F32),
            shape((part, kinds), F32),
            shape((part, mixed_width), F32),
            shape((mixed_width, part), F32),
        ],
        [grads],
    )
    norms = jnp.concatenate([norm1, norm2]).reshape(4, 4 * n_data, -1).transpose(1, 0, 2)
    norms = lax.all_to_all(norms, ("head", "dp"), split_axis=0, concat_axis=0, tiled=True)
    norms = jnp.sum(norms, 0)
    return (
        output[None],
        grad_tokens[None],
        norms,
        query_grad,
        key_grad,
        value_sel,
        output_sel,
        value_grad[None],
        output_grad[None],
        router_grad,
        up_grad[None],
        down_grad[None],
    )


def solution(mesh):
    placed = (
        P("dp", "head", None),
        P("dp", "head", None),
        P("dp", None),
        P("dp", None, "head", None),
        P("dp", None, "head", None),
        P("dp", "head", None),
        P(),
        P(),
        P(),
        P(),
        P("dp", "head"),
        P("dp", "head"),
        P("dp", "head"),
        P("dp", "head"),
        P("head", "dp", None),
        P("head", None, "dp"),
        P(("head", "dp"), None),
        P(("head", "dp"), None, None),
        P(("head", "dp"), None, None),
    )
    return jax.shard_map(
        shards,
        mesh=mesh,
        in_specs=placed,
        out_specs=(
            P("dp", "head", None),
            P("dp", "head", None),
            P(None, ("head", "dp")),
            P("dp", "head"),
            P("dp", "head"),
            P("dp", "head"),
            P("dp", "head"),
            P("head", "dp", None),
            P("head", None, "dp"),
            P(("head", "dp"), None),
            P(("head", "dp"), None, None),
            P(("head", "dp"), None, None),
        ),
        check_vma=False,
    )
```

```python
import functools

import jax
import jax.numpy as jnp
from jax import lax
from jax.experimental import pallas as pl
from jax.experimental.pallas import tpu as pltpu
from jax.sharding import PartitionSpec as P

EPS = 1e-05
F32 = jnp.float32
BF16 = jnp.bfloat16
CHUNK = 8
LANES = 128
WIDE = 256
PAD = 16
MEAN, SPREAD = 16, 17
VMEM_BYTES = 56 * 2**20
ROOT_HALF = 0.7071067811865476
INV_ROOT_2PI = 0.3989422804014327
ANY = pl.BlockSpec(memory_space=pl.ANY)
SMEM = pl.BlockSpec(memory_space=pltpu.SMEM)


def dot(a, b, dims):
    return lax.dot_general(a, b, (dims, ((), ())), preferred_element_type=F32)


def nn(a, b):
    return dot(a, b, ((1,), (0,)))


def nt(a, b):
    return dot(a, b, ((1,), (1,)))


def tn(a, b):
    return dot(a, b, ((0,), (0,)))


def shape(dims, kind):
    return jax.ShapeDtypeStruct(dims, kind)


def cost(micros):
    return pl.CostEstimate(flops=int(micros * 1e9), bytes_accessed=0, transcendentals=0)


class Rows:
    def __init__(self, arrays, most=1 << 20):
        self.arrays = list(arrays)
        most = most if isinstance(most, list) else [most] * len(self.arrays)
        self.counts = [min(a.shape[0], m) for a, m in zip(arrays, most)]
        self.dims = (sum(self.counts),) + tuple(arrays[0].shape[1:])


class Part:
    def __init__(self, array, first, count):
        self.arrays, self.first, self.count = [array], first, count
        self.dims = (array.shape[0], count) + tuple(array.shape[2:])


class In:
    def __init__(self, ref, copies, spans):
        self.ref, self.copies, self.spans, self.waited = ref, copies, spans, set()

    def ready(self, first=0, count=1 << 20):
        for i, (copy, (start, size)) in enumerate(zip(self.copies, self.spans)):
            if i not in self.waited and start < first + count and first < start + size:
                copy.wait()
                self.waited.add(i)
        return self.ref

    def rows(self, first, count):
        return self.ready(first, count)[pl.ds(first, count), :]

    def __getitem__(self, at):
        return self.ready()[at]


class Split:
    def __init__(self, n, dims, kind):
        self.n, self.block, self.kind = n, dims, kind
        self.shape, self.dtype = (n * dims[0], dims[1]), kind


class Out:
    def __init__(self, ref, dest, sems):
        self.ref, self.dest, self.sems, self.copies = ref, dest, sems, []

    def block(self, i, count):
        at = pl.ds(i * count if isinstance(i, int) else pl.multiple_of(i * count, count), count)
        return pltpu.make_async_copy(self.ref.at[at], self.dest.at[at], self.sems.at[i])

    def blocks_sent(self, n, count):
        self.copies += [self.block(i, count) for i in range(n)]

    def __setitem__(self, at, value):
        self.ref[at] = value

    def __getitem__(self, at):
        return self.ref[at]

    def send(self, first=None, count=None):
        if isinstance(self.dest, list):
            n = self.dest[0].shape[0]
            for i, dest in enumerate(self.dest):
                source = self.ref.at[pl.ds(i * n, n)]
                self.copies.append(pltpu.make_async_copy(source, dest, self.sems.at[i]))
                self.copies[-1].start()
            return
        source, dest = self.ref, self.dest
        if first is not None:
            source, dest = source.at[pl.ds(first, count)], dest.at[pl.ds(first, count)]
        copy = pltpu.make_async_copy(source, dest, self.sems.at[len(self.copies)])
        copy.start()
        self.copies.append(copy)


def call(name, micros, body, outs, args, after=()):
    entries = [a if isinstance(a, (Rows, Part)) else Rows([a]) for a in args]
    arrays = [a for e in entries for a in e.arrays]
    single = not isinstance(outs, (list, tuple))
    out_list = [outs] if single else list(outs)

    def kernel(*refs):
        refs = list(refs)
        sources, refs = refs[: len(arrays)], refs[len(arrays) + len(after) :]
        dests = []
        for out in out_list:
            if isinstance(out, Split):
                dests.append(refs[: out.n])
                refs = refs[out.n :]
            else:
                dests.append(refs.pop(0))
        bufs, refs = refs[: len(entries)], refs[len(entries) :]
        in_sems, refs = refs[: len(entries)], refs[len(entries) :]
        out_bufs, out_sems = refs[: len(out_list)], refs[len(out_list) :]
        ins = []
        for entry, buf, sems in zip(entries, bufs, in_sems):
            pairs, spans, at = [], [], 0
            for i, array in enumerate(entry.arrays):
                source, n = sources.pop(0), array.shape[0]
                if isinstance(entry, Rows) and entry.counts[i] < n:
                    n = entry.counts[i]
                    source = source.at[pl.ds(0, n)]
                spans.append((at, n))
                if isinstance(entry, Part):
                    pairs.append((source.at[:, pl.ds(entry.first, entry.count)], buf))
                elif len(entry.arrays) == 1:
                    pairs.append((source, buf))
                else:
                    pairs.append((source, buf.at[pl.ds(at, n)]))
                at += n
            copies = [
                pltpu.make_async_copy(source, dest, sems.at[i])
                for i, (source, dest) in enumerate(pairs)
            ]
            for copy in copies:
                copy.start()
            ins.append(In(buf, copies, spans))
        results = [Out(b, d, s) for b, d, s in zip(out_bufs, dests, out_sems)]
        body(*ins, *results)
        for entry in ins:
            entry.ready()
        for result in results:
            if not result.copies:
                result.send()
        for result in results:
            for copy in result.copies:
                copy.wait()

    shapes = []
    for out in out_list:
        shapes += [shape(out.block, out.kind)] * out.n if isinstance(out, Split) else [out]
    return pl.pallas_call(
        kernel,
        name=name,
        out_shape=shapes[0] if single else shapes,
        in_specs=[ANY] * (len(arrays) + len(after)),
        out_specs=ANY if single else [ANY] * len(shapes),
        scratch_shapes=[pltpu.VMEM(e.dims, e.arrays[0].dtype) for e in entries]
        + [pltpu.SemaphoreType.DMA((len(e.arrays),)) for e in entries]
        + [pltpu.VMEM(o.shape, o.dtype) for o in out_list]
        + [pltpu.SemaphoreType.DMA((8,)) for o in out_list],
        compiler_params=pltpu.CompilerParams(vmem_limit_bytes=VMEM_BYTES),
        cost_estimate=cost(micros),
    )(*arrays, *after)


def repeat(n, body):
    if n == 1:
        body(0)
    else:
        lax.fori_loop(0, n, lambda i, carry: (body(i), carry)[1], 0)


def block_at(i, count):
    return pl.ds(i * count if isinstance(i, int) else pl.multiple_of(i * count, count), count)


def pack_in_kernel(kinds, q, k, v, vsel, osel, o, out):
    size = q.ref.shape[1]
    out[:, 3 * LANES + kinds * size :] = o[...].T
    out[:, 2 * size : 3 * LANES] = jnp.zeros((q.ref.shape[0], LANES), BF16)
    out[:, :size] = q[...]
    out[:, size : 2 * size] = k[...]
    out[:, 2 * size : 2 * size + kinds] = vsel[...].T
    out[:, 2 * size + kinds : 2 * size + 2 * kinds] = osel[...].T
    out[:, 3 * LANES : 3 * LANES + kinds * size] = v[...]


def pack_experts_kernel(up, down, router, out):
    hidden = up.ref.shape[1]
    out[:hidden, :] = up[...].T
    out[hidden : 2 * hidden, :] = down[...]
    out[2 * hidden :, :] = jnp.broadcast_to(router[...], (PAD, router.ref.shape[1]))


def stack_kernel(pieces, out):
    out[...] = pieces[...]


def residual_kernel(*refs):
    parts, (total, top, bottom) = refs[:-3], refs[-3:]
    half = top.ref.shape[0]
    for first, low in ((0, top), (half, bottom)):
        at = pl.ds(first, half)
        found = parts[0][at, :].astype(F32)
        for part in parts[1:]:
            found = found + part[at, :].astype(F32)
        low[...] = found.astype(BF16)
        low.send()
        total[at, :] = found
        total.send(first, half)


def finish_kernel(*refs):
    parts, out = refs[:-1], refs[-1]
    found = parts[0][...].astype(F32)
    for part in parts[1:]:
        found = found + part[...].astype(F32)
    out[...] = found.astype(BF16)


def finish_experts_kernel(found, up, down, router):
    hidden = up.ref.shape[1]
    up[...] = found[:hidden, :].astype(F32).T
    down[...] = found[hidden : 2 * hidden, :].astype(F32)
    router[...] = found[2 * hidden : 2 * hidden + 1, :].astype(F32)


def finish_weights_kernel(scale, kinds, found, q, k, vsel, osel, v, o):
    size = q.ref.shape[1]
    at = 3 * LANES
    q[...] = found[:, :size].astype(F32) * scale
    k[...] = found[:, size : 2 * size].astype(F32)
    both = found[:, 2 * size : at].astype(F32).T
    vsel[...] = both[:kinds, :]
    osel[...] = both[kinds : 2 * kinds, :]
    v[...] = found[:, at : at + kinds * size].astype(F32)
    o[...] = found[:, at + kinds * size :].astype(F32).T


def layer_stats(values):
    mean = jnp.mean(values, -1, keepdims=True)
    center = values - mean
    return mean, lax.rsqrt(jnp.mean(center * center, -1, keepdims=True) + EPS)


def norm_back(scaled, unit, spread):
    return spread * (
        scaled
        - jnp.mean(scaled, -1, keepdims=True)
        - unit * jnp.mean(scaled * unit, -1, keepdims=True)
    )


def project_block(own, scale, kinds, size, x, gain, bias, info, w, q, k, v, ev, gate):

    def block(b):
        at = block_at(b, own)
        rows = x.ref[at, :]
        mean, spread = layer_stats(rows.astype(F32))
        normed = ((rows.astype(F32) - mean) * spread * gain.ref[...] + bias.ref[...]).astype(BF16)
        first = nn(normed, w.ref[:, : 3 * LANES])
        q[at, :] = (first[:, :size] * scale).astype(BF16)
        k[at, :] = first[:, size : 2 * size].astype(BF16)
        lane = lax.broadcasted_iota(jnp.int32, (own, LANES), 1)
        chosen = lane < 0
        for c in range(2, 6):
            chosen = chosen | (lane == info.ref[at, c : c + 1])
        found = jnp.where(chosen, jax.nn.sigmoid(first[:, 2 * size :]), 0.0)
        gate[at, :] = jnp.where(lane == MEAN, mean, jnp.where(lane == SPREAD, spread, found))
        experts = nn(rows, w.ref[:, 3 * LANES :])
        ev[at, :] = experts.astype(BF16)
        ev.block(b, own).start()
        value = found[:, :1] * experts[:, :size]
        for e in range(1, kinds):
            value = value + found[:, e : e + 1] * experts[:, e * size : (e + 1) * size]
        v[at, :] = value.astype(BF16)

    return block


def visible(info, code):
    return (code >= info[:, 0:1]) & (code <= info[:, 1:2])


def forward_kernel(
    own, scale, kinds, size, x, gain, bias, info, w_in, code, w, parts, q, k, v, ev, gate, att, lse, mixed
):
    for value in (x, gain, bias, info, w_in):
        value.ready()
    repeat(4, project_block(own, scale, kinds, size, x, gain, bias, info, w_in, q, k, v, ev, gate))
    ev.blocks_sent(4, own)
    for value in (code, w):
        value.ready()
    for value in (q, k, v, gate):
        value.send()

    def block(b):
        at = block_at(b, own)
        scores = jnp.where(
            visible(info.ref[at, :], code.ref[...]), nt(q.ref[at, :], k.ref[...]), -jnp.inf
        )
        top = jnp.max(scores, -1, keepdims=True)
        weights = jnp.exp(scores - top)
        total = jnp.sum(weights, -1, keepdims=True)
        probs = (weights / total).astype(BF16)
        found = nn(probs, v.ref[...])
        att[at, :] = found
        lse[at, :] = jnp.broadcast_to(top + jnp.log(total), (own, LANES))
        opened = gate.ref[at, :]
        for e in range(kinds):
            mixed[at, e * size : (e + 1) * size] = (
                opened[:, kinds + e : kinds + e + 1] * found
            ).astype(BF16)
        parts[at, :] = nt(mixed[at, :], w.ref[...]).astype(BF16)

    repeat(4, block)
    parts.send()


def expert_kernel(n_blocks, count, hidden, rows_in, gain, bias, router, hits, up_in, grad_in, down_in, backs, dpre, gated, norm, route):
    width = rows_in.ref.shape[1]
    own = rows_in.ref.shape[0] // n_blocks
    for value in (rows_in, gain, bias, router, hits, up_in):
        value.ready()
    norm[...] = jnp.zeros(norm.ref.shape, F32)
    route[...] = jnp.zeros(route.ref.shape, F32)
    if n_blocks > 1:
        grad_in.ready()
        down_in.ready()

    def block(i):
        at = block_at(i, own)
        rows = rows_in.ref[at, :]
        mean, spread = layer_stats(rows.astype(F32))
        unit = (rows.astype(F32) - mean) * spread
        normed = (unit * gain.ref[...] + bias.ref[...]).astype(BF16)
        gate = jax.nn.sigmoid(nt(normed, router.ref[...])) * hits.ref[at, :]
        pre = nt(rows, up_in.ref[...].reshape(count * hidden, width))
        if n_blocks == 1:
            grad_in.ready()
            down_in.ready()
        back = nt(grad_in.ref[at, :], down_in.ref[...].reshape(count * hidden, width))
        d_gate = []
        for e in range(count):
            col = slice(e * hidden, (e + 1) * hidden)
            p, b, g = pre[:, col], back[:, col], gate[:, e : e + 1]
            bell = 0.5 * (1.0 + lax.erf(p * ROOT_HALF))
            active = p * bell
            slope = bell + p * jnp.exp(-0.5 * p * p) * INV_ROOT_2PI
            gated[at, col] = (g * active).astype(BF16)
            dpre[at, col] = (g * b * slope).astype(BF16)
            d_gate.append(jnp.sum(active * b, -1, keepdims=True))
        gated.block(i, own).start()
        dpre.block(i, own).start()
        d_logit = (jnp.concatenate(d_gate, 1) * gate * (1.0 - gate)).astype(BF16)
        d_n2 = nn(d_logit, router.ref[...])
        backs[at, :] = (
            nn(dpre[at, :], up_in.ref[...].reshape(count * hidden, width))
            + norm_back(d_n2 * gain.ref[...], unit, spread)
        ).astype(BF16)
        norm[...] += jnp.concatenate(
            [jnp.sum(d_n2 * unit, 0, keepdims=True), jnp.sum(d_n2, 0, keepdims=True)], 0
        )
        route[...] += tn(d_logit, normed)

    repeat(n_blocks, block)
    gated.blocks_sent(n_blocks, own)
    dpre.blocks_sent(n_blocks, own)
    backs.send()


def expert_out_kernel(count, hidden, gated, down, outs):
    own, width = gated.ref.shape[0] // 4, outs.ref.shape[1]
    gated.ready()
    down.ready()

    def block(i):
        at = block_at(i, own)
        rows = gated.ref[at, :]
        outs[at, :] = nn(rows, down.ref[...].reshape(count * hidden, width)).astype(BF16)

    repeat(4, block)
    outs.send()


def expert_grad_kernel(count, hidden, gated, grad, dpre, rows, *refs):
    routes, out = refs[:-1], refs[-1]
    pair = WIDE // hidden
    for value in (gated, grad):
        value.ready()

    def lower(c):
        down = tn(gated.ref[:, block_at(c, WIDE)], grad.ref[...]).astype(BF16)
        for j in range(pair):
            out[c * pair + j, hidden : 2 * hidden, :] = down[j * hidden : (j + 1) * hidden]

    repeat(count // pair, lower)
    for value in (dpre, rows, *routes):
        value.ready()
    for e in range(count):
        route = sum(r.ref[e : e + 1, :] for r in routes)
        out[e, 2 * hidden :, :] = jnp.broadcast_to(route, (PAD, route.shape[1])).astype(BF16)

    def upper(c):
        up = tn(dpre.ref[:, block_at(c, WIDE)], rows.ref[...]).astype(BF16)
        for j in range(pair):
            out[c * pair + j, :hidden, :] = up[j * hidden : (j + 1) * hidden]
        out.block(c, pair).start()

    repeat(count // pair, upper)
    out.blocks_sent(count // pair, pair)


def attend_back_rows(own, b, d_rows, kinds, size, w, q, k, v, info, code, gate, att, lse):
    at = block_at(b, own)
    lane = lax.broadcasted_iota(jnp.int32, (own, LANES), 1)
    found, opened, queries = att.ref[at, :], gate.ref[at, :], q.ref[at, :]
    scores = jnp.where(visible(info.ref[at, :], code.ref[...]), nt(queries, k.ref[...]), -jnp.inf)
    probs = jnp.exp(scores - lse.ref[at, 0:1])
    d_mixed = nn(d_rows, w.ref[...])
    d_att = jnp.zeros((own, size), F32)
    d_sel = jnp.zeros((own, LANES), F32)
    for e in range(kinds):
        part = d_mixed[:, e * size : (e + 1) * size]
        d_att = d_att + opened[:, kinds + e : kinds + e + 1] * part
        d_sel = jnp.where(lane == kinds + e, jnp.sum(part * found, -1, keepdims=True), d_sel)
    d_att = d_att.astype(BF16)
    d_probs = nt(d_att, v.ref[...])
    centered = jnp.sum(probs * d_probs, -1, keepdims=True)
    d_scores = (probs * (d_probs - centered)).astype(BF16)
    return (
        nn(d_scores, k.ref[...]).astype(BF16),
        d_sel * opened * (1.0 - opened),
        tn(d_scores, queries),
        tn(probs.astype(BF16), d_att),
    )


def attend_back_kernel(own, n, kinds, size, q, k, info, code, lse, w, d_rows, v, gate, att, dq, dsel, dk, dv):
    for value in (q, k, info, code, lse, w, d_rows, v, gate, att):
        value.ready()
    dk[...] = jnp.zeros(dk.ref.shape, F32)
    dv[...] = jnp.zeros(dv.ref.shape, F32)

    def block(b):
        at = block_at(b, own)
        query, selector, key, value = attend_back_rows(
            own, b, d_rows.ref[at, :], kinds, size, w, q, k, v, info, code, gate, att, lse
        )
        dq[at, :] = query
        dsel[at, :] = selector
        dk[...] += key
        dv[...] += value

    repeat(n, block)


def attend_last_kernel(own, kinds, size, q, k, info, code, lse, w, d_rows, v, gate, att, dq, dsel, dk, dv, ev, din, dexp):
    last = 3 * own
    for value in (q, k, info, code, lse, w, d_rows, v, gate, att):
        value.ready()
    query, selector, more_k, more_v = attend_back_rows(
        own, 3, d_rows.ref[...], kinds, size, w, q, k, v, info, code, gate, att, lse
    )
    for value in (dq, dsel, dk, dv, ev):
        value.ready()
    din[last:, :size] = query
    din[:last, :size] = dq.ref[...]
    dk.ref[...] += more_k
    dv.ref[...] += more_v
    dsel.ref[last:, :] = selector
    lane = lax.broadcasted_iota(jnp.int32, (own, LANES), 1)

    def block(b):
        at = block_at(b, own)
        opened, value = gate.ref[at, :], dv.ref[at, :]
        factor = opened * (1.0 - opened)
        din[at, size : 2 * size] = dk.ref[at, :].astype(BF16)
        d_sel = dsel.ref[at, :]
        for e in range(kinds):
            col = slice(e * size, (e + 1) * size)
            moved = jnp.sum(ev.ref[at, col].astype(F32) * value, -1, keepdims=True)
            d_sel = jnp.where(lane == e, moved * factor, d_sel)
            dexp[at, col] = (opened[:, e : e + 1] * value).astype(BF16)
        din[at, 2 * size :] = d_sel.astype(BF16)

    repeat(4, block)


def weight_kernel(d_rows, mixed, x, gate, gain, bias, din, dexp, out):
    width = x.ref.shape[1]
    first_end = din.ref.shape[1]
    second_end = first_end + dexp.ref.shape[1]
    cuts = [slice(first, first + WIDE) for first in range(0, width, WIDE)]
    for at in cuts:
        out[at, second_end:] = tn(d_rows[:, at], mixed[...]).astype(BF16)
    mean, spread = gate[:, MEAN : MEAN + 1], gate[:, SPREAD : SPREAD + 1]
    for at in cuts:
        rows = x[:, at]
        normed = (rows.astype(F32) - mean) * spread * gain[:, at] + bias[:, at]
        out[at, :first_end] = tn(normed.astype(BF16), din[...]).astype(BF16)
        out[at, first_end:second_end] = tn(rows, dexp[...]).astype(BF16)
        out.send(at.start, WIDE)


def input_grad_kernel(own, scale, size, x, din, gate, gain, w, dexp, outs, norm):
    for value in (x, din, gate, gain, w, dexp):
        value.ready()
    norm[...] = jnp.zeros(norm.ref.shape, F32)

    def block(b):
        at = block_at(b, own)
        spread = gate.ref[at, SPREAD : SPREAD + 1]
        unit = (x.ref[at, :].astype(F32) - gate.ref[at, MEAN : MEAN + 1]) * spread
        d_normed = nt(din.ref[at, :size], w.ref[:, :size]) * scale + nt(
            din.ref[at, size:], w.ref[:, size : 3 * LANES]
        )
        outs[at, :] = (
            norm_back(d_normed * gain.ref[...], unit, spread)
            + nt(dexp.ref[at, :], w.ref[:, 3 * LANES :])
        ).astype(BF16)
        norm[...] += jnp.concatenate(
            [jnp.sum(d_normed * unit, 0, keepdims=True), jnp.sum(d_normed, 0, keepdims=True)], 0
        )

    repeat(4, block)
    outs.send()


def to_head(value, flip):
    n = lax.axis_size("head")
    return lax.ppermute(value, "head", [(i, i ^ flip) for i in range(n)])


def spread_rows(top, bottom):
    y_top, x_bottom = to_head(top, 2), to_head(bottom, 1)
    y_bottom, x_top = to_head(bottom, 2), to_head(top, 1)
    far_top, far_bottom = to_head(y_top, 1), to_head(x_bottom, 2)
    return [[top, bottom], [x_top, x_bottom], [y_top, y_bottom], [far_top, far_bottom]]


def flat(blocks):
    return [piece for block in blocks for piece in block]


def expert_blocks(name, rows, grads, hits, weights, router, gain, bias, after=()):
    count, hidden = weights.shape[0], (weights.shape[1] - PAD) // 2
    n, own, width = len(hits), hits[0].shape[0], weights.shape[2]
    wide = shape((n * own, count * hidden), BF16)
    got = call(
        name,
        3 * n + 2,
        functools.partial(expert_kernel, n, count, hidden),
        [
            Split(n, (own, width), BF16),
            wide,
            wide,
            shape((2, width), F32),
            shape((count, width), F32),
        ],
        [
            Rows(flat(rows)),
            gain,
            bias,
            router,
            Rows(hits),
            Part(weights, 0, hidden),
            Rows(flat(grads), most=[own // min(2, len(g)) for g in grads for _ in g]),
            Part(weights, hidden, hidden),
        ],
        after,
    )
    return [list(got[:n]), [got[n]], [got[n + 1]], got[-2], got[-1]]


def expert_chunk(rows, grads, hits, weights, router, gain, bias, moves=()):
    count, hidden = weights.shape[0], (weights.shape[1] - PAD) // 2
    width, own = weights.shape[2], hits[0].shape[0]
    shared = (weights, router, gain, bias)
    first = expert_blocks("experts_own", rows[:1], grads[:1], hits[:1], *shared)
    near = expert_blocks("experts_near", rows[1:3], grads[1:3], hits[1:3], *shared, first[0])
    far = expert_blocks("experts_far", rows[3:], grads[3:], hits[3:], *shared, near[0])
    back, dpre, gated = (first[i] + near[i] + far[i] for i in range(3))
    norm = first[3] + near[3] + far[3]
    moved = [to_head(back[flip], flip) for flip in moves]
    slabs = call(
        "experts_weights",
        8,
        functools.partial(expert_grad_kernel, count, hidden),
        shape((count, 2 * hidden + PAD, width), BF16),
        [
            Rows(gated),
            Rows(flat(grads), most=[own] * 3 + [own // 2] * 2),
            Rows(dpre),
            Rows(flat(rows)),
            first[4],
            near[4],
            far[4],
        ],
        moved[:2],
    )
    return back, moved, gated, norm, slabs


def expert_out(gated, weights, after):
    count, hidden = weights.shape[0], (weights.shape[1] - PAD) // 2
    return call(
        "experts_out",
        12,
        functools.partial(expert_out_kernel, count, hidden),
        [Split(4, (sum(g.shape[0] for g in gated) // 4, weights.shape[2]), BF16)],
        [Rows(gated), Part(weights, hidden, hidden)],
        after,
    )


def shards(
    tokens,
    cotangent,
    segments,
    value_expert_route,
    output_expert_route,
    feedforward_route,
    attention_norm_gain,
    attention_norm_bias,
    feedforward_norm_gain,
    feedforward_norm_bias,
    query_projection,
    key_projection,
    value_selector,
    output_selector,
    value_experts,
    output_experts,
    feedforward_selector,
    expert_up_weight,
    expert_down_weight,
):
    n_data = lax.axis_size("dp")
    head = lax.axis_index("head")
    own, width = tokens.shape[1:]
    half = own // 2
    length = segments.shape[1]
    size = query_projection.shape[1]
    kinds = value_selector.shape[1]
    hidden = expert_up_weight.shape[2]
    scale = size ** (-0.5)
    mixed_width = kinds * size

    def arranged(value):
        return jnp.concatenate(
            [lax.dynamic_slice_in_dim(value, (head ^ k) * own, own, 0) for k in range(4)]
        )

    x_own, grad_own = tokens[0], cotangent[0]
    last = 3 * LANES + mixed_width
    all_own = call(
        "pack_weights",
        1,
        functools.partial(pack_in_kernel, kinds),
        shape((query_projection.shape[0], last + mixed_width), BF16),
        [
            query_projection,
            key_projection,
            value_experts[0],
            value_selector.T,
            output_selector.T,
            output_experts[0],
        ],
    )
    all_in = lax.all_gather(all_own, "dp", axis=0, tiled=True)
    in_all, out_all = Part(all_in, 0, last), Part(all_in, last, mixed_width)
    experts = 4 * n_data
    hot = jnp.sum(jax.nn.one_hot(feedforward_route[0], experts, dtype=BF16), 1)
    hot_rows = own * experts // width
    hot = hot.reshape(hot_rows, width)
    hot = jnp.concatenate([hot, jnp.zeros((-hot_rows % PAD, width), BF16)])
    grad_sent = call(
        "pack_grad",
        2,
        stack_kernel,
        shape((own + hot.shape[0], width), BF16),
        [Rows([grad_own, hot])],
    )

    def spread_whole(value):
        near_x, near_y = to_head(value, 1), to_head(value, 2)
        far = [to_head(near_y[:half], 1), to_head(near_x[half:], 2)]
        return [near_x], [near_y], far

    x = [[x_own], *spread_whole(x_own)]
    grad = [[grad_own], *spread_whole(grad_sent)]
    (near_x,), (near_y,), (_, far_bottom) = grad[1:]

    def hits_of(rows):
        found = rows[:hot_rows].reshape(own, experts)
        return lax.dynamic_slice_in_dim(found, head * n_data, n_data, 1).astype(F32)

    hits = [hits_of(v) for v in (hot, near_x[own:], near_y[own:], far_bottom[half:])]
    ffn_own = call(
        "pack_experts",
        2,
        pack_experts_kernel,
        shape((2 * hidden + PAD, width), BF16),
        [expert_up_weight[0], expert_down_weight[0], feedforward_selector],
        [all_own, grad_sent],
    )
    ffn_all = lax.all_gather(ffn_own, "dp", axis=0, tiled=False)
    router = ffn_all[:, 2 * hidden]

    spots = jnp.arange(length, dtype=jnp.int32)
    first_code = segments[0] * length
    info = arranged(
        jnp.concatenate(
            [
                first_code[:, None],
                (first_code + spots)[:, None],
                value_expert_route[0, :, 0],
                output_expert_route[0, :, 0] + kinds,
                jnp.zeros((length, 2), jnp.int32),
            ],
            1,
        )
    )
    code = arranged(first_code + spots)[None]
    gain1, bias1 = attention_norm_gain[None], attention_norm_bias[None]
    gain2, bias2 = feedforward_norm_gain[None], feedforward_norm_bias[None]
    (
        part_own,
        part_x,
        part_y,
        part_far,
        query,
        key,
        value,
        experts_v,
        gate,
        att,
        lse,
        mixed,
    ) = call(
        "forward",
        14,
        functools.partial(forward_kernel, own, scale, kinds, size),
        [Split(4, (own, width), BF16)]
        + [shape((length, size), BF16)] * 3
        + [
            shape((length, mixed_width), BF16),
            shape((length, LANES), F32),
            shape((length, size), F32),
            shape((length, LANES), F32),
            shape((length, mixed_width), BF16),
        ],
        [Rows(flat(x)), gain1, bias1, info, in_all, code, out_all],
        flat(grad[1:]),
    )

    def residual(name, parts, after=()):
        return call(
            name,
            2,
            residual_kernel,
            [shape((own, width), F32)] + [shape((half, width), BF16)] * 2,
            parts,
            after,
        )

    parts = [to_head(part, flip) for part, flip in ((part_far, 3), (part_x, 1), (part_y, 2))]
    resid, top, bottom = residual("residual", [x_own, part_own, *parts])
    rows = spread_rows(top, bottom)

    if n_data <= CHUNK:
        back, moved, gated, norm2, slabs = expert_chunk(
            rows,
            grad,
            hits,
            ffn_all,
            router,
            gain2,
            bias2,
            (1, 2, 3),
        )
    else:
        cut = lambda a: a.reshape((n_data // CHUNK, CHUNK) + a.shape[1:])
        hit_cuts = [
            h.reshape(own, n_data // CHUNK, CHUNK).transpose(1, 0, 2) for h in hits
        ]

        def step(carry, item):
            hit, rt, w = item
            got_back, _, got_gated, got_norm, slab = expert_chunk(
                rows, grad, hit, w, rt, gain2, bias2
            )
            got_out = expert_out(got_gated, w, ())
            add = lambda old, new: [o + v.astype(F32) for o, v in zip(old, new)]
            new = (add(carry[0], got_out), add(carry[1], got_back), carry[2] + got_norm)
            return new, slab

        zero = [jnp.zeros((own, width), F32)] * 4
        (out, back, norm2), slabs = lax.scan(
            step,
            (zero, zero, jnp.zeros((2, width), F32)),
            (hit_cuts, cut(router), cut(ffn_all)),
        )
        out, back = [v.astype(BF16) for v in out], [v.astype(BF16) for v in back]
        moved = [to_head(back[flip], flip) for flip in (1, 2, 3)]
        slabs = slabs.reshape((n_data,) + slabs.shape[2:])

    ffn_grads = lax.psum_scatter(slabs, "dp", scatter_dimension=0, tiled=True)
    if n_data <= CHUNK:
        out = expert_out(gated, ffn_all, ())
    d_resid, top, bottom = residual("residual_back", [grad_own, back[0], *moved], [slabs, *out])
    d_pack = spread_rows(top, bottom)

    dq, dsel, dk, dv = call(
        "attend_back",
        6,
        functools.partial(attend_back_kernel, own, 3, kinds, size),
        [
            shape((3 * own, size), BF16),
            shape((length, LANES), F32),
            shape((length, size), F32),
            shape((length, size), F32),
        ],
        [query, key, info, code, lse, out_all, Rows(flat(d_pack[:3])), value, gate, att],
        out,
    )
    out_moved = [to_head(out[flip], flip) for flip in (3, 1, 2)]
    d_in, d_exp = call(
        "attend_last",
        5,
        functools.partial(attend_last_kernel, own, kinds, size),
        [shape((length, 3 * LANES), BF16), shape((length, mixed_width), BF16)],
        [
            query,
            key,
            info,
            code,
            lse,
            out_all,
            Rows(d_pack[3]),
            value,
            gate,
            att,
            dq,
            dsel,
            dk,
            dv,
            experts_v,
        ],
    )
    weight_part = call(
        "weights",
        6,
        weight_kernel,
        shape((width, 3 * LANES + 2 * mixed_width), BF16),
        [
            Rows(flat(d_pack)),
            mixed,
            Rows(flat(x)),
            gate,
            gain1,
            bias1,
            d_in,
            d_exp,
        ],
        (ffn_grads, *out_moved[1:]),
    )
    d_own, d_x, d_y, d_far, norm1 = call(
        "input_back",
        6,
        functools.partial(input_grad_kernel, own, scale, size),
        [Split(4, (own, width), BF16), shape((2, width), F32)],
        [Rows(flat(x)), d_in, gate, gain1, in_all, d_exp],
        (weight_part,),
    )
    moved = [to_head(part, flip) for part, flip in ((d_far, 3), (d_x, 1), (d_y, 2))]
    block = shape((own, width), BF16)
    up_grad, down_grad, router_grad = call(
        "finish_experts",
        2,
        finish_experts_kernel,
        [shape((width, hidden), F32), shape((hidden, width), F32), shape((1, width), F32)],
        [ffn_grads[0]],
    )
    output = call(
        "output",
        2,
        finish_kernel,
        block,
        [resid, out[0], *out_moved],
        moved[1:],
    )
    grad_tokens = call(
        "token_grads", 2, finish_kernel, block, [d_resid, d_own, *moved]
    )

    part = width // n_data
    grads = lax.psum_scatter(weight_part, "dp", scatter_dimension=0, tiled=True)
    query_grad, key_grad, value_sel, output_sel, value_grad, output_grad = call(
        "finish_weights",
        2,
        functools.partial(finish_weights_kernel, scale, kinds),
        [
            shape((part, size), F32),
            shape((part, size), F32),
            shape((kinds, part), F32),
            shape((kinds, part), F32),
            shape((part, mixed_width), F32),
            shape((mixed_width, part), F32),
        ],
        [grads],
    )
    norms = jnp.concatenate([norm1, norm2]).reshape(4, 4 * n_data, -1).transpose(1, 0, 2)
    norms = lax.all_to_all(norms, ("head", "dp"), split_axis=0, concat_axis=0, tiled=True)
    norms = jnp.sum(norms, 0)
    return (
        output[None],
        grad_tokens[None],
        norms,
        query_grad,
        key_grad,
        value_sel.T,
        output_sel.T,
        value_grad[None],
        output_grad[None],
        router_grad,
        up_grad[None],
        down_grad[None],
    )


def solution(mesh):
    placed = (
        P("dp", "head", None),
        P("dp", "head", None),
        P("dp", None),
        P("dp", None, "head", None),
        P("dp", None, "head", None),
        P("dp", "head", None),
        P(),
        P(),
        P(),
        P(),
        P("dp", "head"),
        P("dp", "head"),
        P("dp", "head"),
        P("dp", "head"),
        P("head", "dp", None),
        P("head", None, "dp"),
        P(("head", "dp"), None),
        P(("head", "dp"), None, None),
        P(("head", "dp"), None, None),
    )
    return jax.shard_map(
        shards,
        mesh=mesh,
        in_specs=placed,
        out_specs=(
            P("dp", "head", None),
            P("dp", "head", None),
            P(None, ("head", "dp")),
            P("dp", "head"),
            P("dp", "head"),
            P("dp", "head"),
            P("dp", "head"),
            P("head", "dp", None),
            P("head", None, "dp"),
            P(("head", "dp"), None),
            P(("head", "dp"), None, None),
            P(("head", "dp"), None, None),
        ),
        check_vma=False,
    )
```

```python
import functools

import jax
import jax.numpy as jnp
from jax import lax
from jax.experimental import pallas as pl
from jax.experimental.pallas import tpu as pltpu
from jax.sharding import PartitionSpec as P

EPS = 1e-05
F32 = jnp.float32
BF16 = jnp.bfloat16
CHUNK = 8
LANES = 128
WIDE = 256
PAD = 16
MEAN, SPREAD = 16, 17
VMEM_BYTES = 56 * 2**20
ROOT_HALF = 0.7071067811865476
INV_ROOT_2PI = 0.3989422804014327
ANY = pl.BlockSpec(memory_space=pl.ANY)
SMEM = pl.BlockSpec(memory_space=pltpu.SMEM)


def dot(a, b, dims):
    return lax.dot_general(a, b, (dims, ((), ())), preferred_element_type=F32)


def nn(a, b):
    return dot(a, b, ((1,), (0,)))


def nt(a, b):
    return dot(a, b, ((1,), (1,)))


def tn(a, b):
    return dot(a, b, ((0,), (0,)))


def shape(dims, kind):
    return jax.ShapeDtypeStruct(dims, kind)


def cost(micros):
    return pl.CostEstimate(flops=int(micros * 1e9), bytes_accessed=0, transcendentals=0)


class Rows:
    def __init__(self, arrays, most=1 << 20):
        self.arrays = list(arrays)
        most = most if isinstance(most, list) else [most] * len(self.arrays)
        self.counts = [min(a.shape[0], m) for a, m in zip(arrays, most)]
        self.dims = (sum(self.counts),) + tuple(arrays[0].shape[1:])


class Part:
    def __init__(self, array, first, count):
        self.arrays, self.first, self.count = [array], first, count
        self.dims = (array.shape[0], count) + tuple(array.shape[2:])


class In:
    def __init__(self, ref, copies, spans):
        self.ref, self.copies, self.spans, self.waited = ref, copies, spans, set()

    def ready(self, first=0, count=1 << 20):
        for i, (copy, (start, size)) in enumerate(zip(self.copies, self.spans)):
            if i not in self.waited and start < first + count and first < start + size:
                copy.wait()
                self.waited.add(i)
        return self.ref

    def rows(self, first, count):
        return self.ready(first, count)[pl.ds(first, count), :]

    def __getitem__(self, at):
        return self.ready()[at]


class Split:
    def __init__(self, n, dims, kind):
        self.n, self.block, self.kind = n, dims, kind
        self.shape, self.dtype = (n * dims[0], dims[1]), kind


class Out:
    def __init__(self, ref, dest, sems):
        self.ref, self.dest, self.sems, self.copies = ref, dest, sems, []

    def block(self, i, count):
        at = pl.ds(i * count if isinstance(i, int) else pl.multiple_of(i * count, count), count)
        return pltpu.make_async_copy(self.ref.at[at], self.dest.at[at], self.sems.at[i])

    def blocks_sent(self, n, count):
        self.copies += [self.block(i, count) for i in range(n)]

    def __setitem__(self, at, value):
        self.ref[at] = value

    def __getitem__(self, at):
        return self.ref[at]

    def send(self, first=None, count=None):
        if isinstance(self.dest, list):
            n = self.dest[0].shape[0]
            for i, dest in enumerate(self.dest):
                source = self.ref.at[pl.ds(i * n, n)]
                self.copies.append(pltpu.make_async_copy(source, dest, self.sems.at[i]))
                self.copies[-1].start()
            return
        source, dest = self.ref, self.dest
        if first is not None:
            source, dest = source.at[pl.ds(first, count)], dest.at[pl.ds(first, count)]
        copy = pltpu.make_async_copy(source, dest, self.sems.at[len(self.copies)])
        copy.start()
        self.copies.append(copy)


def call(name, micros, body, outs, args, after=()):
    entries = [a if isinstance(a, (Rows, Part)) else Rows([a]) for a in args]
    arrays = [a for e in entries for a in e.arrays]
    single = not isinstance(outs, (list, tuple))
    out_list = [outs] if single else list(outs)

    def kernel(*refs):
        refs = list(refs)
        sources, refs = refs[: len(arrays)], refs[len(arrays) + len(after) :]
        dests = []
        for out in out_list:
            if isinstance(out, Split):
                dests.append(refs[: out.n])
                refs = refs[out.n :]
            else:
                dests.append(refs.pop(0))
        bufs, refs = refs[: len(entries)], refs[len(entries) :]
        in_sems, refs = refs[: len(entries)], refs[len(entries) :]
        out_bufs, out_sems = refs[: len(out_list)], refs[len(out_list) :]
        ins = []
        for entry, buf, sems in zip(entries, bufs, in_sems):
            pairs, spans, at = [], [], 0
            for i, array in enumerate(entry.arrays):
                source, n = sources.pop(0), array.shape[0]
                if isinstance(entry, Rows) and entry.counts[i] < n:
                    n = entry.counts[i]
                    source = source.at[pl.ds(0, n)]
                spans.append((at, n))
                if isinstance(entry, Part):
                    pairs.append((source.at[:, pl.ds(entry.first, entry.count)], buf))
                elif len(entry.arrays) == 1:
                    pairs.append((source, buf))
                else:
                    pairs.append((source, buf.at[pl.ds(at, n)]))
                at += n
            copies = [
                pltpu.make_async_copy(source, dest, sems.at[i])
                for i, (source, dest) in enumerate(pairs)
            ]
            for copy in copies:
                copy.start()
            ins.append(In(buf, copies, spans))
        results = [Out(b, d, s) for b, d, s in zip(out_bufs, dests, out_sems)]
        body(*ins, *results)
        for entry in ins:
            entry.ready()
        for result in results:
            if not result.copies:
                result.send()
        for result in results:
            for copy in result.copies:
                copy.wait()

    shapes = []
    for out in out_list:
        shapes += [shape(out.block, out.kind)] * out.n if isinstance(out, Split) else [out]
    return pl.pallas_call(
        kernel,
        name=name,
        out_shape=shapes[0] if single else shapes,
        in_specs=[ANY] * (len(arrays) + len(after)),
        out_specs=ANY if single else [ANY] * len(shapes),
        scratch_shapes=[pltpu.VMEM(e.dims, e.arrays[0].dtype) for e in entries]
        + [pltpu.SemaphoreType.DMA((len(e.arrays),)) for e in entries]
        + [pltpu.VMEM(o.shape, o.dtype) for o in out_list]
        + [pltpu.SemaphoreType.DMA((8,)) for o in out_list],
        compiler_params=pltpu.CompilerParams(vmem_limit_bytes=VMEM_BYTES),
        cost_estimate=cost(micros),
    )(*arrays, *after)


def repeat(n, body):
    if n == 1:
        body(0)
    else:
        lax.fori_loop(0, n, lambda i, carry: (body(i), carry)[1], 0)


def block_at(i, count):
    return pl.ds(i * count if isinstance(i, int) else pl.multiple_of(i * count, count), count)


def pack_in_kernel(kinds, q, k, v, vsel, osel, o, out):
    size = q.ref.shape[1]
    out[:, 3 * LANES + kinds * size :] = o[...].T
    out[:, 2 * size : 3 * LANES] = jnp.zeros((q.ref.shape[0], LANES), BF16)
    out[:, :size] = q[...]
    out[:, size : 2 * size] = k[...]
    out[:, 2 * size : 2 * size + kinds] = vsel[...].T
    out[:, 2 * size + kinds : 2 * size + 2 * kinds] = osel[...].T
    out[:, 3 * LANES : 3 * LANES + kinds * size] = v[...]


def pack_experts_kernel(up, down, router, out):
    hidden = up.ref.shape[1]
    out[:hidden, :] = up[...].T
    out[hidden : 2 * hidden, :] = down[...]
    out[2 * hidden :, :] = jnp.broadcast_to(router[...], (PAD, router.ref.shape[1]))


def stack_kernel(pieces, out):
    out[...] = pieces[...]


def residual_kernel(*refs):
    parts, (total, top, bottom) = refs[:-3], refs[-3:]
    half = top.ref.shape[0]
    for first, low in ((0, top), (half, bottom)):
        at = pl.ds(first, half)
        found = parts[0][at, :].astype(F32)
        for part in parts[1:]:
            found = found + part[at, :].astype(F32)
        low[...] = found.astype(BF16)
        low.send()
        total[at, :] = found
        total.send(first, half)


def finish_kernel(*refs):
    parts, out = refs[:-1], refs[-1]
    found = parts[0][...].astype(F32)
    for part in parts[1:]:
        found = found + part[...].astype(F32)
    out[...] = found.astype(BF16)


def finish_experts_kernel(found, up, down, router):
    hidden = up.ref.shape[1]
    up[...] = found[:hidden, :].astype(F32).T
    down[...] = found[hidden : 2 * hidden, :].astype(F32)
    router[...] = found[2 * hidden : 2 * hidden + 1, :].astype(F32)


def finish_weights_kernel(scale, kinds, found, q, k, vsel, osel, v, o):
    size = q.ref.shape[1]
    at = 3 * LANES
    q[...] = found[:, :size].astype(F32) * scale
    k[...] = found[:, size : 2 * size].astype(F32)
    both = found[:, 2 * size : at].astype(F32).T
    vsel[...] = both[:kinds, :]
    osel[...] = both[kinds : 2 * kinds, :]
    v[...] = found[:, at : at + kinds * size].astype(F32)
    o[...] = found[:, at + kinds * size :].astype(F32).T


def layer_stats(values):
    mean = jnp.mean(values, -1, keepdims=True)
    center = values - mean
    return mean, lax.rsqrt(jnp.mean(center * center, -1, keepdims=True) + EPS)


def norm_back(scaled, unit, spread):
    return spread * (
        scaled
        - jnp.mean(scaled, -1, keepdims=True)
        - unit * jnp.mean(scaled * unit, -1, keepdims=True)
    )


def project_block(own, scale, kinds, size, x, gain, bias, info, w, q, k, v, ev, gate):

    def block(b):
        at = block_at(b, own)
        rows = x.ref[at, :]
        mean, spread = layer_stats(rows.astype(F32))
        normed = ((rows.astype(F32) - mean) * spread * gain.ref[...] + bias.ref[...]).astype(BF16)
        first = nn(normed, w.ref[:, : 3 * LANES])
        q[at, :] = (first[:, :size] * scale).astype(BF16)
        k[at, :] = first[:, size : 2 * size].astype(BF16)
        lane = lax.broadcasted_iota(jnp.int32, (own, LANES), 1)
        chosen = lane < 0
        for c in range(2, 6):
            chosen = chosen | (lane == info.ref[at, c : c + 1])
        found = jnp.where(chosen, jax.nn.sigmoid(first[:, 2 * size :]), 0.0)
        gate[at, :] = jnp.where(lane == MEAN, mean, jnp.where(lane == SPREAD, spread, found))
        experts = nn(rows, w.ref[:, 3 * LANES :])
        ev[at, :] = experts.astype(BF16)
        ev.block(b, own).start()
        value = found[:, :1] * experts[:, :size]
        for e in range(1, kinds):
            value = value + found[:, e : e + 1] * experts[:, e * size : (e + 1) * size]
        v[at, :] = value.astype(BF16)

    return block


def visible(info, code):
    return (code >= info[:, 0:1]) & (code <= info[:, 1:2])


def forward_kernel(
    own, scale, kinds, size, x, gain, bias, info, w_in, code, w, parts, q, k, v, ev, gate, att, lse, mixed
):
    for value in (x, gain, bias, info, w_in):
        value.ready()
    repeat(4, project_block(own, scale, kinds, size, x, gain, bias, info, w_in, q, k, v, ev, gate))
    ev.blocks_sent(4, own)
    for value in (code, w):
        value.ready()
    for value in (q, k, v, gate):
        value.send()

    def block(b):
        at = block_at(b, own)
        scores = jnp.where(
            visible(info.ref[at, :], code.ref[...]), nt(q.ref[at, :], k.ref[...]), -jnp.inf
        )
        top = jnp.max(scores, -1, keepdims=True)
        weights = jnp.exp(scores - top)
        total = jnp.sum(weights, -1, keepdims=True)
        probs = (weights / total).astype(BF16)
        found = nn(probs, v.ref[...])
        att[at, :] = found
        lse[at, :] = jnp.broadcast_to(top + jnp.log(total), (own, LANES))
        opened = gate.ref[at, :]
        for e in range(kinds):
            mixed[at, e * size : (e + 1) * size] = (
                opened[:, kinds + e : kinds + e + 1] * found
            ).astype(BF16)
        parts[at, :] = nt(mixed[at, :], w.ref[...]).astype(BF16)

    repeat(4, block)
    parts.send()


def expert_kernel(n_blocks, count, hidden, rows_in, gain, bias, router, hits, up_in, grad_in, down_in, backs, dpre, gated, norm, route):
    width = rows_in.ref.shape[1]
    own = rows_in.ref.shape[0] // n_blocks
    for value in (rows_in, gain, bias, router, hits, up_in):
        value.ready()
    norm[...] = jnp.zeros(norm.ref.shape, F32)
    route[...] = jnp.zeros(route.ref.shape, F32)
    if n_blocks > 1:
        grad_in.ready()
        down_in.ready()

    def block(i):
        at = block_at(i, own)
        rows = rows_in.ref[at, :]
        mean, spread = layer_stats(rows.astype(F32))
        unit = (rows.astype(F32) - mean) * spread
        normed = (unit * gain.ref[...] + bias.ref[...]).astype(BF16)
        gate = jax.nn.sigmoid(nt(normed, router.ref[...])) * hits.ref[at, :]
        pre = nt(rows, up_in.ref[...].reshape(count * hidden, width))
        if n_blocks == 1:
            grad_in.ready()
            down_in.ready()
        back = nt(grad_in.ref[at, :], down_in.ref[...].reshape(count * hidden, width))
        d_gate = []
        for e in range(count):
            col = slice(e * hidden, (e + 1) * hidden)
            p, b, g = pre[:, col], back[:, col], gate[:, e : e + 1]
            bell = 0.5 * (1.0 + lax.erf(p * ROOT_HALF))
            active = p * bell
            slope = bell + p * jnp.exp(-0.5 * p * p) * INV_ROOT_2PI
            gated[at, col] = (g * active).astype(BF16)
            dpre[at, col] = (g * b * slope).astype(BF16)
            d_gate.append(jnp.sum(active * b, -1, keepdims=True))
        gated.block(i, own).start()
        dpre.block(i, own).start()
        d_logit = (jnp.concatenate(d_gate, 1) * gate * (1.0 - gate)).astype(BF16)
        d_n2 = nn(d_logit, router.ref[...])
        backs[at, :] = (
            nn(dpre[at, :], up_in.ref[...].reshape(count * hidden, width))
            + norm_back(d_n2 * gain.ref[...], unit, spread)
        ).astype(BF16)
        norm[...] += jnp.concatenate(
            [jnp.sum(d_n2 * unit, 0, keepdims=True), jnp.sum(d_n2, 0, keepdims=True)], 0
        )
        route[...] += tn(d_logit, normed)

    repeat(n_blocks, block)
    gated.blocks_sent(n_blocks, own)
    dpre.blocks_sent(n_blocks, own)
    backs.send()


def expert_out_kernel(count, hidden, gated, down, outs):
    own, width = gated.ref.shape[0] // 4, outs.ref.shape[1]
    gated.ready()
    down.ready()

    def block(i):
        at = block_at(i, own)
        rows = gated.ref[at, :]
        outs[at, :] = nn(rows, down.ref[...].reshape(count * hidden, width)).astype(BF16)

    repeat(4, block)
    outs.send()


def expert_grad_kernel(count, hidden, gated, grad, dpre, rows, *refs):
    routes, out = refs[:-1], refs[-1]
    pair = WIDE // hidden
    for value in (gated, grad):
        value.ready()

    def lower(c):
        down = tn(gated.ref[:, block_at(c, WIDE)], grad.ref[...]).astype(BF16)
        for j in range(pair):
            out[c * pair + j, hidden : 2 * hidden, :] = down[j * hidden : (j + 1) * hidden]

    repeat(count // pair, lower)
    for value in (dpre, rows, *routes):
        value.ready()
    for e in range(count):
        route = sum(r.ref[e : e + 1, :] for r in routes)
        out[e, 2 * hidden :, :] = jnp.broadcast_to(route, (PAD, route.shape[1])).astype(BF16)

    def upper(c):
        up = tn(dpre.ref[:, block_at(c, WIDE)], rows.ref[...]).astype(BF16)
        for j in range(pair):
            out[c * pair + j, :hidden, :] = up[j * hidden : (j + 1) * hidden]
        out.block(c, pair).start()

    repeat(count // pair, upper)
    out.blocks_sent(count // pair, pair)


def attend_back_rows(own, b, d_rows, kinds, size, w, q, k, v, info, code, gate, att, lse):
    at = block_at(b, own)
    lane = lax.broadcasted_iota(jnp.int32, (own, LANES), 1)
    found, opened, queries = att.ref[at, :], gate.ref[at, :], q.ref[at, :]
    scores = jnp.where(visible(info.ref[at, :], code.ref[...]), nt(queries, k.ref[...]), -jnp.inf)
    probs = jnp.exp(scores - lse.ref[at, 0:1])
    d_mixed = nn(d_rows, w.ref[...])
    d_att = jnp.zeros((own, size), F32)
    d_sel = jnp.zeros((own, LANES), F32)
    for e in range(kinds):
        part = d_mixed[:, e * size : (e + 1) * size]
        d_att = d_att + opened[:, kinds + e : kinds + e + 1] * part
        d_sel = jnp.where(lane == kinds + e, jnp.sum(part * found, -1, keepdims=True), d_sel)
    d_att = d_att.astype(BF16)
    d_probs = nt(d_att, v.ref[...])
    centered = jnp.sum(probs * d_probs, -1, keepdims=True)
    d_scores = (probs * (d_probs - centered)).astype(BF16)
    return (
        nn(d_scores, k.ref[...]).astype(BF16),
        d_sel * opened * (1.0 - opened),
        tn(d_scores, queries),
        tn(probs.astype(BF16), d_att),
    )


def attend_back_kernel(own, n, kinds, size, q, k, info, code, lse, w, d_rows, v, gate, att, dq, dsel, dk, dv):
    for value in (q, k, info, code, lse, w, d_rows, v, gate, att):
        value.ready()
    dk[...] = jnp.zeros(dk.ref.shape, F32)
    dv[...] = jnp.zeros(dv.ref.shape, F32)

    def block(b):
        at = block_at(b, own)
        query, selector, key, value = attend_back_rows(
            own, b, d_rows.ref[at, :], kinds, size, w, q, k, v, info, code, gate, att, lse
        )
        dq[at, :] = query
        dsel[at, :] = selector
        dk[...] += key
        dv[...] += value

    repeat(n, block)


def attend_last_kernel(own, kinds, size, q, k, info, code, lse, w, d_rows, v, gate, att, dq, dsel, dk, dv, ev, din, dexp):
    last = 3 * own
    for value in (q, k, info, code, lse, w, d_rows, v, gate, att):
        value.ready()
    query, selector, more_k, more_v = attend_back_rows(
        own, 3, d_rows.ref[...], kinds, size, w, q, k, v, info, code, gate, att, lse
    )
    for value in (dq, dsel, dk, dv, ev):
        value.ready()
    din[last:, :size] = query
    din[:last, :size] = dq.ref[...]
    dk.ref[...] += more_k
    dv.ref[...] += more_v
    dsel.ref[last:, :] = selector
    lane = lax.broadcasted_iota(jnp.int32, (own, LANES), 1)

    def block(b):
        at = block_at(b, own)
        opened, value = gate.ref[at, :], dv.ref[at, :]
        factor = opened * (1.0 - opened)
        din[at, size : 2 * size] = dk.ref[at, :].astype(BF16)
        d_sel = dsel.ref[at, :]
        for e in range(kinds):
            col = slice(e * size, (e + 1) * size)
            moved = jnp.sum(ev.ref[at, col].astype(F32) * value, -1, keepdims=True)
            d_sel = jnp.where(lane == e, moved * factor, d_sel)
            dexp[at, col] = (opened[:, e : e + 1] * value).astype(BF16)
        din[at, 2 * size :] = d_sel.astype(BF16)

    repeat(4, block)


def weight_kernel(d_rows, mixed, x, gate, gain, bias, din, dexp, out):
    width = x.ref.shape[1]
    first_end = din.ref.shape[1]
    second_end = first_end + dexp.ref.shape[1]
    cuts = [slice(first, first + WIDE) for first in range(0, width, WIDE)]
    for at in cuts:
        out[at, second_end:] = tn(d_rows[:, at], mixed[...]).astype(BF16)
    mean, spread = gate[:, MEAN : MEAN + 1], gate[:, SPREAD : SPREAD + 1]
    for at in cuts:
        rows = x[:, at]
        normed = (rows.astype(F32) - mean) * spread * gain[:, at] + bias[:, at]
        out[at, :first_end] = tn(normed.astype(BF16), din[...]).astype(BF16)
        out[at, first_end:second_end] = tn(rows, dexp[...]).astype(BF16)
        out.send(at.start, WIDE)


def input_grad_kernel(own, scale, size, x, din, gate, gain, w, dexp, outs, norm):
    for value in (x, din, gate, gain, w, dexp):
        value.ready()
    norm[...] = jnp.zeros(norm.ref.shape, F32)

    def block(b):
        at = block_at(b, own)
        spread = gate.ref[at, SPREAD : SPREAD + 1]
        unit = (x.ref[at, :].astype(F32) - gate.ref[at, MEAN : MEAN + 1]) * spread
        d_normed = nt(din.ref[at, :size], w.ref[:, :size]) * scale + nt(
            din.ref[at, size:], w.ref[:, size : 3 * LANES]
        )
        outs[at, :] = (
            norm_back(d_normed * gain.ref[...], unit, spread)
            + nt(dexp.ref[at, :], w.ref[:, 3 * LANES :])
        ).astype(BF16)
        norm[...] += jnp.concatenate(
            [jnp.sum(d_normed * unit, 0, keepdims=True), jnp.sum(d_normed, 0, keepdims=True)], 0
        )

    repeat(4, block)
    outs.send()


def to_head(value, flip):
    n = lax.axis_size("head")
    return lax.ppermute(value, "head", [(i, i ^ flip) for i in range(n)])


def spread_rows(top, bottom):
    y_top, x_bottom = to_head(top, 2), to_head(bottom, 1)
    y_bottom, x_top = to_head(bottom, 2), to_head(top, 1)
    far_top, far_bottom = to_head(y_top, 1), to_head(x_bottom, 2)
    return [[top, bottom], [x_top, x_bottom], [y_top, y_bottom], [far_top, far_bottom]]


def flat(blocks):
    return [piece for block in blocks for piece in block]


def expert_blocks(name, rows, grads, hits, weights, router, gain, bias, after=()):
    count, hidden = weights.shape[0], (weights.shape[1] - PAD) // 2
    n, own, width = len(hits), hits[0].shape[0], weights.shape[2]
    wide = shape((n * own, count * hidden), BF16)
    got = call(
        name,
        3 * n + 2,
        functools.partial(expert_kernel, n, count, hidden),
        [
            Split(n, (own, width), BF16),
            wide,
            wide,
            shape((2, width), F32),
            shape((count, width), F32),
        ],
        [
            Rows(flat(rows)),
            gain,
            bias,
            router,
            Rows(hits),
            Part(weights, 0, hidden),
            Rows(flat(grads), most=[own // min(2, len(g)) for g in grads for _ in g]),
            Part(weights, hidden, hidden),
        ],
        after,
    )
    return [list(got[:n]), [got[n]], [got[n + 1]], got[-2], got[-1]]


def expert_chunk(rows, grads, hits, weights, router, gain, bias, moves=()):
    count, hidden = weights.shape[0], (weights.shape[1] - PAD) // 2
    width, own = weights.shape[2], hits[0].shape[0]
    shared = (weights, router, gain, bias)
    first = expert_blocks("experts_own", rows[:1], grads[:1], hits[:1], *shared)
    near = expert_blocks("experts_near", rows[1:3], grads[1:3], hits[1:3], *shared, first[0])
    far = expert_blocks("experts_far", rows[3:], grads[3:], hits[3:], *shared, near[0])
    back, dpre, gated = (first[i] + near[i] + far[i] for i in range(3))
    norm = first[3] + near[3] + far[3]
    moved = [to_head(back[flip], flip) for flip in moves]
    slabs = call(
        "experts_weights",
        8,
        functools.partial(expert_grad_kernel, count, hidden),
        shape((count, 2 * hidden + PAD, width), BF16),
        [
            Rows(gated),
            Rows(flat(grads), most=[own] * 3 + [own // 2] * 2),
            Rows(dpre),
            Rows(flat(rows)),
            first[4],
            near[4],
            far[4],
        ],
    )
    return back, moved, gated, norm, slabs


def expert_out(gated, weights, after):
    count, hidden = weights.shape[0], (weights.shape[1] - PAD) // 2
    return call(
        "experts_out",
        12,
        functools.partial(expert_out_kernel, count, hidden),
        [Split(4, (sum(g.shape[0] for g in gated) // 4, weights.shape[2]), BF16)],
        [Rows(gated), Part(weights, hidden, hidden)],
        after,
    )


def shards(
    tokens,
    cotangent,
    segments,
    value_expert_route,
    output_expert_route,
    feedforward_route,
    attention_norm_gain,
    attention_norm_bias,
    feedforward_norm_gain,
    feedforward_norm_bias,
    query_projection,
    key_projection,
    value_selector,
    output_selector,
    value_experts,
    output_experts,
    feedforward_selector,
    expert_up_weight,
    expert_down_weight,
):
    n_data = lax.axis_size("dp")
    head = lax.axis_index("head")
    own, width = tokens.shape[1:]
    half = own // 2
    length = segments.shape[1]
    size = query_projection.shape[1]
    kinds = value_selector.shape[1]
    hidden = expert_up_weight.shape[2]
    scale = size ** (-0.5)
    mixed_width = kinds * size

    def arranged(value):
        return jnp.concatenate(
            [lax.dynamic_slice_in_dim(value, (head ^ k) * own, own, 0) for k in range(4)]
        )

    x_own, grad_own = tokens[0], cotangent[0]
    last = 3 * LANES + mixed_width
    all_own = call(
        "pack_weights",
        1,
        functools.partial(pack_in_kernel, kinds),
        shape((query_projection.shape[0], last + mixed_width), BF16),
        [
            query_projection,
            key_projection,
            value_experts[0],
            value_selector.T,
            output_selector.T,
            output_experts[0],
        ],
    )
    all_in = lax.all_gather(all_own, "dp", axis=0, tiled=True)
    in_all, out_all = Part(all_in, 0, last), Part(all_in, last, mixed_width)
    experts = 4 * n_data
    hot = jnp.sum(jax.nn.one_hot(feedforward_route[0], experts, dtype=BF16), 1)
    hot_rows = own * experts // width
    hot = hot.reshape(hot_rows, width)
    hot = jnp.concatenate([hot, jnp.zeros((-hot_rows % PAD, width), BF16)])
    grad_sent = call(
        "pack_grad",
        2,
        stack_kernel,
        shape((own + hot.shape[0], width), BF16),
        [Rows([grad_own, hot])],
    )

    def spread_whole(value):
        near_x, near_y = to_head(value, 1), to_head(value, 2)
        far = [to_head(near_y[:half], 1), to_head(near_x[half:], 2)]
        return [near_x], [near_y], far

    x = [[x_own], *spread_whole(x_own)]
    grad = [[grad_own], *spread_whole(grad_sent)]
    (near_x,), (near_y,), (_, far_bottom) = grad[1:]

    def hits_of(rows):
        found = rows[:hot_rows].reshape(own, experts)
        return lax.dynamic_slice_in_dim(found, head * n_data, n_data, 1).astype(F32)

    hits = [hits_of(v) for v in (hot, near_x[own:], near_y[own:], far_bottom[half:])]
    ffn_own = call(
        "pack_experts",
        2,
        pack_experts_kernel,
        shape((2 * hidden + PAD, width), BF16),
        [expert_up_weight[0], expert_down_weight[0], feedforward_selector],
        [all_own, grad_sent],
    )
    ffn_all = lax.all_gather(ffn_own, "dp", axis=0, tiled=False)
    router = ffn_all[:, 2 * hidden]

    spots = jnp.arange(length, dtype=jnp.int32)
    first_code = segments[0] * length
    info = arranged(
        jnp.concatenate(
            [
                first_code[:, None],
                (first_code + spots)[:, None],
                value_expert_route[0, :, 0],
                output_expert_route[0, :, 0] + kinds,
                jnp.zeros((length, 2), jnp.int32),
            ],
            1,
        )
    )
    code = arranged(first_code + spots)[None]
    gain1, bias1 = attention_norm_gain[None], attention_norm_bias[None]
    gain2, bias2 = feedforward_norm_gain[None], feedforward_norm_bias[None]
    (
        part_own,
        part_x,
        part_y,
        part_far,
        query,
        key,
        value,
        experts_v,
        gate,
        att,
        lse,
        mixed,
    ) = call(
        "forward",
        14,
        functools.partial(forward_kernel, own, scale, kinds, size),
        [Split(4, (own, width), BF16)]
        + [shape((length, size), BF16)] * 3
        + [
            shape((length, mixed_width), BF16),
            shape((length, LANES), F32),
            shape((length, size), F32),
            shape((length, LANES), F32),
            shape((length, mixed_width), BF16),
        ],
        [Rows(flat(x)), gain1, bias1, info, in_all, code, out_all],
        flat(grad[1:]),
    )

    def residual(name, parts, after=()):
        return call(
            name,
            2,
            residual_kernel,
            [shape((own, width), F32)] + [shape((half, width), BF16)] * 2,
            parts,
            after,
        )

    parts = [to_head(part, flip) for part, flip in ((part_far, 3), (part_x, 1), (part_y, 2))]
    resid, top, bottom = residual("residual", [x_own, part_own, *parts])
    rows = spread_rows(top, bottom)

    if n_data <= CHUNK:
        back, moved, gated, norm2, slabs = expert_chunk(
            rows,
            grad,
            hits,
            ffn_all,
            router,
            gain2,
            bias2,
            (1, 2, 3),
        )
    else:
        cut = lambda a: a.reshape((n_data // CHUNK, CHUNK) + a.shape[1:])
        hit_cuts = [
            h.reshape(own, n_data // CHUNK, CHUNK).transpose(1, 0, 2) for h in hits
        ]

        def step(carry, item):
            hit, rt, w = item
            got_back, _, got_gated, got_norm, slab = expert_chunk(
                rows, grad, hit, w, rt, gain2, bias2
            )
            got_out = expert_out(got_gated, w, ())
            add = lambda old, new: [o + v.astype(F32) for o, v in zip(old, new)]
            new = (add(carry[0], got_out), add(carry[1], got_back), carry[2] + got_norm)
            return new, slab

        zero = [jnp.zeros((own, width), F32)] * 4
        (out, back, norm2), slabs = lax.scan(
            step,
            (zero, zero, jnp.zeros((2, width), F32)),
            (hit_cuts, cut(router), cut(ffn_all)),
        )
        out, back = [v.astype(BF16) for v in out], [v.astype(BF16) for v in back]
        moved = [to_head(back[flip], flip) for flip in (1, 2, 3)]
        slabs = slabs.reshape((n_data,) + slabs.shape[2:])

    ffn_grads = lax.psum_scatter(slabs, "dp", scatter_dimension=0, tiled=True)
    if n_data <= CHUNK:
        out = expert_out(gated, ffn_all, ())
    d_resid, top, bottom = residual("residual_back", [grad_own, back[0], *moved], [slabs, *out])
    d_pack = spread_rows(top, bottom)

    dq, dsel, dk, dv = call(
        "attend_back",
        40,
        functools.partial(attend_back_kernel, own, 3, kinds, size),
        [
            shape((3 * own, size), BF16),
            shape((length, LANES), F32),
            shape((length, size), F32),
            shape((length, size), F32),
        ],
        [query, key, info, code, lse, out_all, Rows(flat(d_pack[:3])), value, gate, att],
        out,
    )
    out_moved = [to_head(out[flip], flip) for flip in (3, 1, 2)]
    d_in, d_exp = call(
        "attend_last",
        40,
        functools.partial(attend_last_kernel, own, kinds, size),
        [shape((length, 3 * LANES), BF16), shape((length, mixed_width), BF16)],
        [
            query,
            key,
            info,
            code,
            lse,
            out_all,
            Rows(d_pack[3]),
            value,
            gate,
            att,
            dq,
            dsel,
            dk,
            dv,
            experts_v,
        ],
    )
    weight_part = call(
        "weights",
        6,
        weight_kernel,
        shape((width, 3 * LANES + 2 * mixed_width), BF16),
        [
            Rows(flat(d_pack)),
            mixed,
            Rows(flat(x)),
            gate,
            gain1,
            bias1,
            d_in,
            d_exp,
        ],
        (ffn_grads, *out_moved[1:]),
    )
    d_own, d_x, d_y, d_far, norm1 = call(
        "input_back",
        6,
        functools.partial(input_grad_kernel, own, scale, size),
        [Split(4, (own, width), BF16), shape((2, width), F32)],
        [Rows(flat(x)), d_in, gate, gain1, in_all, d_exp],
        (weight_part,),
    )
    moved = [to_head(part, flip) for part, flip in ((d_far, 3), (d_x, 1), (d_y, 2))]
    block = shape((own, width), BF16)
    up_grad, down_grad, router_grad = call(
        "finish_experts",
        2,
        finish_experts_kernel,
        [shape((width, hidden), F32), shape((hidden, width), F32), shape((1, width), F32)],
        [ffn_grads[0]],
    )
    output = call(
        "output",
        2,
        finish_kernel,
        block,
        [resid, out[0], *out_moved],
        moved[1:],
    )
    grad_tokens = call(
        "token_grads", 2, finish_kernel, block, [d_resid, d_own, *moved]
    )

    part = width // n_data
    grads = lax.psum_scatter(weight_part, "dp", scatter_dimension=0, tiled=True)
    query_grad, key_grad, value_sel, output_sel, value_grad, output_grad = call(
        "finish_weights",
        2,
        functools.partial(finish_weights_kernel, scale, kinds),
        [
            shape((part, size), F32),
            shape((part, size), F32),
            shape((kinds, part), F32),
            shape((kinds, part), F32),
            shape((part, mixed_width), F32),
            shape((mixed_width, part), F32),
        ],
        [grads],
    )
    norms = jnp.concatenate([norm1, norm2]).reshape(4, 4 * n_data, -1).transpose(1, 0, 2)
    norms = lax.all_to_all(norms, ("head", "dp"), split_axis=0, concat_axis=0, tiled=True)
    norms = jnp.sum(norms, 0)
    return (
        output[None],
        grad_tokens[None],
        norms,
        query_grad,
        key_grad,
        value_sel.T,
        output_sel.T,
        value_grad[None],
        output_grad[None],
        router_grad,
        up_grad[None],
        down_grad[None],
    )


def solution(mesh):
    placed = (
        P("dp", "head", None),
        P("dp", "head", None),
        P("dp", None),
        P("dp", None, "head", None),
        P("dp", None, "head", None),
        P("dp", "head", None),
        P(),
        P(),
        P(),
        P(),
        P("dp", "head"),
        P("dp", "head"),
        P("dp", "head"),
        P("dp", "head"),
        P("head", "dp", None),
        P("head", None, "dp"),
        P(("head", "dp"), None),
        P(("head", "dp"), None, None),
        P(("head", "dp"), None, None),
    )
    return jax.shard_map(
        shards,
        mesh=mesh,
        in_specs=placed,
        out_specs=(
            P("dp", "head", None),
            P("dp", "head", None),
            P(None, ("head", "dp")),
            P("dp", "head"),
            P("dp", "head"),
            P("dp", "head"),
            P("dp", "head"),
            P("head", "dp", None),
            P("head", None, "dp"),
            P(("head", "dp"), None),
            P(("head", "dp"), None, None),
            P(("head", "dp"), None, None),
        ),
        check_vma=False,
    )
```

```python
import functools

import jax
import jax.numpy as jnp
from jax import lax
from jax.experimental import pallas as pl
from jax.experimental.pallas import tpu as pltpu
from jax.sharding import PartitionSpec as P

EPS = 1e-05
F32 = jnp.float32
BF16 = jnp.bfloat16
CHUNK = 8
LANES = 128
WIDE = 256
PAD = 16
MEAN, SPREAD = 16, 17
VMEM_BYTES = 56 * 2**20
ROOT_HALF = 0.7071067811865476
INV_ROOT_2PI = 0.3989422804014327
ANY = pl.BlockSpec(memory_space=pl.ANY)
SMEM = pl.BlockSpec(memory_space=pltpu.SMEM)


def dot(a, b, dims):
    return lax.dot_general(a, b, (dims, ((), ())), preferred_element_type=F32)


def nn(a, b):
    return dot(a, b, ((1,), (0,)))


def nt(a, b):
    return dot(a, b, ((1,), (1,)))


def tn(a, b):
    return dot(a, b, ((0,), (0,)))


def shape(dims, kind):
    return jax.ShapeDtypeStruct(dims, kind)


def cost(micros):
    return pl.CostEstimate(flops=int(micros * 1e9), bytes_accessed=0, transcendentals=0)


class Rows:
    def __init__(self, arrays, most=1 << 20):
        self.arrays = list(arrays)
        most = most if isinstance(most, list) else [most] * len(self.arrays)
        self.counts = [min(a.shape[0], m) for a, m in zip(arrays, most)]
        self.dims = (sum(self.counts),) + tuple(arrays[0].shape[1:])


class Part:
    def __init__(self, array, first, count):
        self.arrays, self.first, self.count = [array], first, count
        self.dims = (array.shape[0], count) + tuple(array.shape[2:])


class In:
    def __init__(self, ref, copies, spans):
        self.ref, self.copies, self.spans, self.waited = ref, copies, spans, set()

    def ready(self, first=0, count=1 << 20):
        for i, (copy, (start, size)) in enumerate(zip(self.copies, self.spans)):
            if i not in self.waited and start < first + count and first < start + size:
                copy.wait()
                self.waited.add(i)
        return self.ref

    def rows(self, first, count):
        return self.ready(first, count)[pl.ds(first, count), :]

    def __getitem__(self, at):
        return self.ready()[at]


class Split:
    def __init__(self, n, dims, kind):
        self.n, self.block, self.kind = n, dims, kind
        self.shape, self.dtype = (n * dims[0], dims[1]), kind


class Out:
    def __init__(self, ref, dest, sems):
        self.ref, self.dest, self.sems, self.copies = ref, dest, sems, []

    def block(self, i, count):
        at = pl.ds(i * count if isinstance(i, int) else pl.multiple_of(i * count, count), count)
        return pltpu.make_async_copy(self.ref.at[at], self.dest.at[at], self.sems.at[i])

    def blocks_sent(self, n, count):
        self.copies += [self.block(i, count) for i in range(n)]

    def __setitem__(self, at, value):
        self.ref[at] = value

    def __getitem__(self, at):
        return self.ref[at]

    def send(self, first=None, count=None):
        if isinstance(self.dest, list):
            n = self.dest[0].shape[0]
            for i, dest in enumerate(self.dest):
                source = self.ref.at[pl.ds(i * n, n)]
                self.copies.append(pltpu.make_async_copy(source, dest, self.sems.at[i]))
                self.copies[-1].start()
            return
        source, dest = self.ref, self.dest
        if first is not None:
            source, dest = source.at[pl.ds(first, count)], dest.at[pl.ds(first, count)]
        copy = pltpu.make_async_copy(source, dest, self.sems.at[len(self.copies)])
        copy.start()
        self.copies.append(copy)


def call(name, micros, body, outs, args, after=()):
    entries = [a if isinstance(a, (Rows, Part)) else Rows([a]) for a in args]
    arrays = [a for e in entries for a in e.arrays]
    single = not isinstance(outs, (list, tuple))
    out_list = [outs] if single else list(outs)

    def kernel(*refs):
        refs = list(refs)
        sources, refs = refs[: len(arrays)], refs[len(arrays) + len(after) :]
        dests = []
        for out in out_list:
            if isinstance(out, Split):
                dests.append(refs[: out.n])
                refs = refs[out.n :]
            else:
                dests.append(refs.pop(0))
        bufs, refs = refs[: len(entries)], refs[len(entries) :]
        in_sems, refs = refs[: len(entries)], refs[len(entries) :]
        out_bufs, out_sems = refs[: len(out_list)], refs[len(out_list) :]
        ins = []
        for entry, buf, sems in zip(entries, bufs, in_sems):
            pairs, spans, at = [], [], 0
            for i, array in enumerate(entry.arrays):
                source, n = sources.pop(0), array.shape[0]
                if isinstance(entry, Rows) and entry.counts[i] < n:
                    n = entry.counts[i]
                    source = source.at[pl.ds(0, n)]
                spans.append((at, n))
                if isinstance(entry, Part):
                    pairs.append((source.at[:, pl.ds(entry.first, entry.count)], buf))
                elif len(entry.arrays) == 1:
                    pairs.append((source, buf))
                else:
                    pairs.append((source, buf.at[pl.ds(at, n)]))
                at += n
            copies = [
                pltpu.make_async_copy(source, dest, sems.at[i])
                for i, (source, dest) in enumerate(pairs)
            ]
            for copy in copies:
                copy.start()
            ins.append(In(buf, copies, spans))
        results = [Out(b, d, s) for b, d, s in zip(out_bufs, dests, out_sems)]
        body(*ins, *results)
        for entry in ins:
            entry.ready()
        for result in results:
            if not result.copies:
                result.send()
        for result in results:
            for copy in result.copies:
                copy.wait()

    shapes = []
    for out in out_list:
        shapes += [shape(out.block, out.kind)] * out.n if isinstance(out, Split) else [out]
    return pl.pallas_call(
        kernel,
        name=name,
        out_shape=shapes[0] if single else shapes,
        in_specs=[ANY] * (len(arrays) + len(after)),
        out_specs=ANY if single else [ANY] * len(shapes),
        scratch_shapes=[pltpu.VMEM(e.dims, e.arrays[0].dtype) for e in entries]
        + [pltpu.SemaphoreType.DMA((len(e.arrays),)) for e in entries]
        + [pltpu.VMEM(o.shape, o.dtype) for o in out_list]
        + [pltpu.SemaphoreType.DMA((8,)) for o in out_list],
        compiler_params=pltpu.CompilerParams(vmem_limit_bytes=VMEM_BYTES),
        cost_estimate=cost(micros),
    )(*arrays, *after)


def repeat(n, body):
    if n == 1:
        body(0)
    else:
        lax.fori_loop(0, n, lambda i, carry: (body(i), carry)[1], 0)


def block_at(i, count):
    return pl.ds(i * count if isinstance(i, int) else pl.multiple_of(i * count, count), count)


def pack_in_kernel(kinds, q, k, v, vsel, osel, o, out):
    size = q.ref.shape[1]
    out[:, 3 * LANES + kinds * size :] = o[...].T
    out[:, 2 * size : 3 * LANES] = jnp.zeros((q.ref.shape[0], LANES), BF16)
    out[:, :size] = q[...]
    out[:, size : 2 * size] = k[...]
    out[:, 2 * size : 2 * size + kinds] = vsel[...].T
    out[:, 2 * size + kinds : 2 * size + 2 * kinds] = osel[...].T
    out[:, 3 * LANES : 3 * LANES + kinds * size] = v[...]


def pack_experts_kernel(up, down, router, out):
    hidden = up.ref.shape[1]
    out[:hidden, :] = up[...].T
    out[hidden : 2 * hidden, :] = down[...]
    out[2 * hidden :, :] = jnp.broadcast_to(router[...], (PAD, router.ref.shape[1]))


def stack_kernel(pieces, out):
    out[...] = pieces[...]


def residual_kernel(*refs):
    parts, (total, top, bottom) = refs[:-3], refs[-3:]
    half = top.ref.shape[0]
    for first, low in ((0, top), (half, bottom)):
        at = pl.ds(first, half)
        found = parts[0][at, :].astype(F32)
        for part in parts[1:]:
            found = found + part[at, :].astype(F32)
        low[...] = found.astype(BF16)
        low.send()
        total[at, :] = found
        total.send(first, half)


def finish_kernel(*refs):
    parts, out = refs[:-1], refs[-1]
    found = parts[0][...].astype(F32)
    for part in parts[1:]:
        found = found + part[...].astype(F32)
    out[...] = found.astype(BF16)


def finish_experts_kernel(found, up, down, router):
    hidden = up.ref.shape[1]
    up[...] = found[:hidden, :].astype(F32).T
    down[...] = found[hidden : 2 * hidden, :].astype(F32)
    router[...] = found[2 * hidden : 2 * hidden + 1, :].astype(F32)


def finish_weights_kernel(scale, kinds, found, q, k, vsel, osel, v, o):
    size = q.ref.shape[1]
    at = 3 * LANES
    q[...] = found[:, :size].astype(F32) * scale
    k[...] = found[:, size : 2 * size].astype(F32)
    both = found[:, 2 * size : at].astype(F32).T
    vsel[...] = both[:kinds, :]
    osel[...] = both[kinds : 2 * kinds, :]
    v[...] = found[:, at : at + kinds * size].astype(F32)
    o[...] = found[:, at + kinds * size :].astype(F32).T


def layer_stats(values):
    mean = jnp.mean(values, -1, keepdims=True)
    center = values - mean
    return mean, lax.rsqrt(jnp.mean(center * center, -1, keepdims=True) + EPS)


def norm_back(scaled, unit, spread):
    return spread * (
        scaled
        - jnp.mean(scaled, -1, keepdims=True)
        - unit * jnp.mean(scaled * unit, -1, keepdims=True)
    )


def project_block(own, scale, kinds, size, x, gain, bias, info, w, q, k, v, ev, gate):

    def block(b):
        at = block_at(b, own)
        rows = x.ref[at, :]
        mean, spread = layer_stats(rows.astype(F32))
        normed = ((rows.astype(F32) - mean) * spread * gain.ref[...] + bias.ref[...]).astype(BF16)
        first = nn(normed, w.ref[:, : 3 * LANES])
        q[at, :] = (first[:, :size] * scale).astype(BF16)
        k[at, :] = first[:, size : 2 * size].astype(BF16)
        lane = lax.broadcasted_iota(jnp.int32, (own, LANES), 1)
        chosen = lane < 0
        for c in range(2, 6):
            chosen = chosen | (lane == info.ref[at, c : c + 1])
        found = jnp.where(chosen, jax.nn.sigmoid(first[:, 2 * size :]), 0.0)
        gate[at, :] = jnp.where(lane == MEAN, mean, jnp.where(lane == SPREAD, spread, found))
        experts = nn(rows, w.ref[:, 3 * LANES :])
        ev[at, :] = experts.astype(BF16)
        ev.block(b, own).start()
        value = found[:, :1] * experts[:, :size]
        for e in range(1, kinds):
            value = value + found[:, e : e + 1] * experts[:, e * size : (e + 1) * size]
        v[at, :] = value.astype(BF16)

    return block


def visible(info, code):
    return (code >= info[:, 0:1]) & (code <= info[:, 1:2])


def forward_kernel(
    own, scale, kinds, size, x, gain, bias, info, w_in, code, w, parts, q, k, v, ev, gate, att, lse, mixed
):
    for value in (x, gain, bias, info, w_in):
        value.ready()
    repeat(4, project_block(own, scale, kinds, size, x, gain, bias, info, w_in, q, k, v, ev, gate))
    ev.blocks_sent(4, own)
    for value in (code, w):
        value.ready()
    for value in (q, k, v, gate):
        value.send()

    def block(b):
        at = block_at(b, own)
        scores = jnp.where(
            visible(info.ref[at, :], code.ref[...]), nt(q.ref[at, :], k.ref[...]), -jnp.inf
        )
        top = jnp.max(scores, -1, keepdims=True)
        weights = jnp.exp(scores - top)
        total = jnp.sum(weights, -1, keepdims=True)
        probs = (weights / total).astype(BF16)
        found = nn(probs, v.ref[...])
        att[at, :] = found
        lse[at, :] = jnp.broadcast_to(top + jnp.log(total), (own, LANES))
        opened = gate.ref[at, :]
        for e in range(kinds):
            mixed[at, e * size : (e + 1) * size] = (
                opened[:, kinds + e : kinds + e + 1] * found
            ).astype(BF16)
        parts[at, :] = nt(mixed[at, :], w.ref[...]).astype(BF16)

    repeat(4, block)
    parts.send()


def expert_kernel(n_blocks, count, hidden, rows_in, gain, bias, router, hits, up_in, grad_in, down_in, backs, dpre, gated, norm, route):
    width = rows_in.ref.shape[1]
    own = rows_in.ref.shape[0] // n_blocks
    for value in (rows_in, gain, bias, router, hits, up_in):
        value.ready()
    norm[...] = jnp.zeros(norm.ref.shape, F32)
    route[...] = jnp.zeros(route.ref.shape, F32)
    if n_blocks > 1:
        grad_in.ready()
        down_in.ready()

    def block(i):
        at = block_at(i, own)
        rows = rows_in.ref[at, :]
        mean, spread = layer_stats(rows.astype(F32))
        unit = (rows.astype(F32) - mean) * spread
        normed = (unit * gain.ref[...] + bias.ref[...]).astype(BF16)
        gate = jax.nn.sigmoid(nt(normed, router.ref[...])) * hits.ref[at, :]
        pre = nt(rows, up_in.ref[...].reshape(count * hidden, width))
        if n_blocks == 1:
            grad_in.ready()
            down_in.ready()
        back = nt(grad_in.ref[at, :], down_in.ref[...].reshape(count * hidden, width))
        d_gate = []
        for e in range(count):
            col = slice(e * hidden, (e + 1) * hidden)
            p, b, g = pre[:, col], back[:, col], gate[:, e : e + 1]
            bell = 0.5 * (1.0 + lax.erf(p * ROOT_HALF))
            active = p * bell
            slope = bell + p * jnp.exp(-0.5 * p * p) * INV_ROOT_2PI
            gated[at, col] = (g * active).astype(BF16)
            dpre[at, col] = (g * b * slope).astype(BF16)
            d_gate.append(jnp.sum(active * b, -1, keepdims=True))
        gated.block(i, own).start()
        dpre.block(i, own).start()
        d_logit = (jnp.concatenate(d_gate, 1) * gate * (1.0 - gate)).astype(BF16)
        d_n2 = nn(d_logit, router.ref[...])
        backs[at, :] = (
            nn(dpre[at, :], up_in.ref[...].reshape(count * hidden, width))
            + norm_back(d_n2 * gain.ref[...], unit, spread)
        ).astype(BF16)
        norm[...] += jnp.concatenate(
            [jnp.sum(d_n2 * unit, 0, keepdims=True), jnp.sum(d_n2, 0, keepdims=True)], 0
        )
        route[...] += tn(d_logit, normed)

    repeat(n_blocks, block)
    gated.blocks_sent(n_blocks, own)
    dpre.blocks_sent(n_blocks, own)
    backs.send()


def expert_out_kernel(count, hidden, gated, down, outs):
    own, width = gated.ref.shape[0] // 4, outs.ref.shape[1]
    gated.ready()
    down.ready()

    def block(i):
        at = block_at(i, own)
        rows = gated.ref[at, :]
        outs[at, :] = nn(rows, down.ref[...].reshape(count * hidden, width)).astype(BF16)

    repeat(4, block)
    outs.send()


def expert_grad_kernel(count, hidden, gated, grad, dpre, rows, *refs):
    routes, out = refs[:-1], refs[-1]
    pair = WIDE // hidden
    for value in (gated, grad):
        value.ready()

    def lower(c):
        down = tn(gated.ref[:, block_at(c, WIDE)], grad.ref[...]).astype(BF16)
        for j in range(pair):
            out[c * pair + j, hidden : 2 * hidden, :] = down[j * hidden : (j + 1) * hidden]

    repeat(count // pair, lower)
    for value in (dpre, rows, *routes):
        value.ready()
    for e in range(count):
        route = sum(r.ref[e : e + 1, :] for r in routes)
        out[e, 2 * hidden :, :] = jnp.broadcast_to(route, (PAD, route.shape[1])).astype(BF16)

    def upper(c):
        up = tn(dpre.ref[:, block_at(c, WIDE)], rows.ref[...]).astype(BF16)
        for j in range(pair):
            out[c * pair + j, :hidden, :] = up[j * hidden : (j + 1) * hidden]
        out.block(c, pair).start()

    repeat(count // pair, upper)
    out.blocks_sent(count // pair, pair)


def attend_back_rows(own, b, d_rows, kinds, size, w, q, k, v, info, code, gate, att, lse):
    at = block_at(b, own)
    lane = lax.broadcasted_iota(jnp.int32, (own, LANES), 1)
    found, opened, queries = att.ref[at, :], gate.ref[at, :], q.ref[at, :]
    scores = jnp.where(visible(info.ref[at, :], code.ref[...]), nt(queries, k.ref[...]), -jnp.inf)
    probs = jnp.exp(scores - lse.ref[at, 0:1])
    d_mixed = nn(d_rows, w.ref[...])
    d_att = jnp.zeros((own, size), F32)
    d_sel = jnp.zeros((own, LANES), F32)
    for e in range(kinds):
        part = d_mixed[:, e * size : (e + 1) * size]
        d_att = d_att + opened[:, kinds + e : kinds + e + 1] * part
        d_sel = jnp.where(lane == kinds + e, jnp.sum(part * found, -1, keepdims=True), d_sel)
    d_att = d_att.astype(BF16)
    d_probs = nt(d_att, v.ref[...])
    centered = jnp.sum(probs * d_probs, -1, keepdims=True)
    d_scores = (probs * (d_probs - centered)).astype(BF16)
    return (
        nn(d_scores, k.ref[...]).astype(BF16),
        d_sel * opened * (1.0 - opened),
        tn(d_scores, queries),
        tn(probs.astype(BF16), d_att),
    )


def attend_back_kernel(own, n, kinds, size, q, k, info, code, lse, w, d_rows, v, gate, att, dq, dsel, dk, dv):
    for value in (q, k, info, code, lse, w, d_rows, v, gate, att):
        value.ready()
    dk[...] = jnp.zeros(dk.ref.shape, F32)
    dv[...] = jnp.zeros(dv.ref.shape, F32)

    def block(b):
        at = block_at(b, own)
        query, selector, key, value = attend_back_rows(
            own, b, d_rows.ref[at, :], kinds, size, w, q, k, v, info, code, gate, att, lse
        )
        dq[at, :] = query
        dsel[at, :] = selector
        dk[...] += key
        dv[...] += value

    repeat(n, block)


def attend_last_kernel(own, kinds, size, q, k, info, code, lse, w, d_rows, v, gate, att, dq, dsel, dk, dv, ev, din, dexp):
    last = 3 * own
    for value in (q, k, info, code, lse, w, d_rows, v, gate, att):
        value.ready()
    query, selector, more_k, more_v = attend_back_rows(
        own, 3, d_rows.ref[...], kinds, size, w, q, k, v, info, code, gate, att, lse
    )
    for value in (dq, dsel, dk, dv, ev):
        value.ready()
    din[last:, :size] = query
    din[:last, :size] = dq.ref[...]
    dk.ref[...] += more_k
    dv.ref[...] += more_v
    dsel.ref[last:, :] = selector
    lane = lax.broadcasted_iota(jnp.int32, (own, LANES), 1)

    def block(b):
        at = block_at(b, own)
        opened, value = gate.ref[at, :], dv.ref[at, :]
        factor = opened * (1.0 - opened)
        din[at, size : 2 * size] = dk.ref[at, :].astype(BF16)
        d_sel = dsel.ref[at, :]
        for e in range(kinds):
            col = slice(e * size, (e + 1) * size)
            moved = jnp.sum(ev.ref[at, col].astype(F32) * value, -1, keepdims=True)
            d_sel = jnp.where(lane == e, moved * factor, d_sel)
            dexp[at, col] = (opened[:, e : e + 1] * value).astype(BF16)
        din[at, 2 * size :] = d_sel.astype(BF16)

    repeat(4, block)


def weight_kernel(d_rows, mixed, x, gate, gain, bias, din, dexp, out):
    width = x.ref.shape[1]
    first_end = din.ref.shape[1]
    second_end = first_end + dexp.ref.shape[1]
    cuts = [slice(first, first + WIDE) for first in range(0, width, WIDE)]
    for at in cuts:
        out[at, second_end:] = tn(d_rows[:, at], mixed[...]).astype(BF16)
    mean, spread = gate[:, MEAN : MEAN + 1], gate[:, SPREAD : SPREAD + 1]
    for at in cuts:
        rows = x[:, at]
        normed = (rows.astype(F32) - mean) * spread * gain[:, at] + bias[:, at]
        out[at, :first_end] = tn(normed.astype(BF16), din[...]).astype(BF16)
        out[at, first_end:second_end] = tn(rows, dexp[...]).astype(BF16)
        out.send(at.start, WIDE)


def input_grad_kernel(own, scale, size, x, din, gate, gain, w, dexp, outs, norm):
    for value in (x, din, gate, gain, w, dexp):
        value.ready()
    norm[...] = jnp.zeros(norm.ref.shape, F32)

    def block(b):
        at = block_at(b, own)
        spread = gate.ref[at, SPREAD : SPREAD + 1]
        unit = (x.ref[at, :].astype(F32) - gate.ref[at, MEAN : MEAN + 1]) * spread
        d_normed = nt(din.ref[at, :size], w.ref[:, :size]) * scale + nt(
            din.ref[at, size:], w.ref[:, size : 3 * LANES]
        )
        outs[at, :] = (
            norm_back(d_normed * gain.ref[...], unit, spread)
            + nt(dexp.ref[at, :], w.ref[:, 3 * LANES :])
        ).astype(BF16)
        norm[...] += jnp.concatenate(
            [jnp.sum(d_normed * unit, 0, keepdims=True), jnp.sum(d_normed, 0, keepdims=True)], 0
        )

    repeat(4, block)
    outs.send()


def to_head(value, flip):
    n = lax.axis_size("head")
    return lax.ppermute(value, "head", [(i, i ^ flip) for i in range(n)])


def spread_rows(top, bottom):
    y_top, x_bottom = to_head(top, 2), to_head(bottom, 1)
    y_bottom, x_top = to_head(bottom, 2), to_head(top, 1)
    far_top, far_bottom = to_head(y_top, 1), to_head(x_bottom, 2)
    return [[top, bottom], [x_top, x_bottom], [y_top, y_bottom], [far_top, far_bottom]]


def flat(blocks):
    return [piece for block in blocks for piece in block]


def expert_blocks(name, rows, grads, hits, weights, router, gain, bias, after=()):
    count, hidden = weights.shape[0], (weights.shape[1] - PAD) // 2
    n, own, width = len(hits), hits[0].shape[0], weights.shape[2]
    wide = shape((n * own, count * hidden), BF16)
    got = call(
        name,
        3 * n + 2,
        functools.partial(expert_kernel, n, count, hidden),
        [
            Split(n, (own, width), BF16),
            wide,
            wide,
            shape((2, width), F32),
            shape((count, width), F32),
        ],
        [
            Rows(flat(rows)),
            gain,
            bias,
            router,
            Rows(hits),
            Part(weights, 0, hidden),
            Rows(flat(grads), most=[own // min(2, len(g)) for g in grads for _ in g]),
            Part(weights, hidden, hidden),
        ],
        after,
    )
    return [list(got[:n]), [got[n]], [got[n + 1]], got[-2], got[-1]]


def expert_chunk(rows, grads, hits, weights, router, gain, bias, moves=()):
    count, hidden = weights.shape[0], (weights.shape[1] - PAD) // 2
    width, own = weights.shape[2], hits[0].shape[0]
    shared = (weights, router, gain, bias)
    first = expert_blocks("experts_own", rows[:1], grads[:1], hits[:1], *shared)
    near = expert_blocks("experts_near", rows[1:3], grads[1:3], hits[1:3], *shared, first[0])
    far = expert_blocks("experts_far", rows[3:], grads[3:], hits[3:], *shared, near[0])
    back, dpre, gated = (first[i] + near[i] + far[i] for i in range(3))
    norm = first[3] + near[3] + far[3]
    moved = [to_head(back[flip], flip) for flip in moves]
    slabs = call(
        "experts_weights",
        8,
        functools.partial(expert_grad_kernel, count, hidden),
        shape((count, 2 * hidden + PAD, width), BF16),
        [
            Rows(gated),
            Rows(flat(grads), most=[own] * 3 + [own // 2] * 2),
            Rows(dpre),
            Rows(flat(rows)),
            first[4],
            near[4],
            far[4],
        ],
    )
    return back, moved, gated, norm, slabs


def expert_out(gated, weights, after):
    count, hidden = weights.shape[0], (weights.shape[1] - PAD) // 2
    return call(
        "experts_out",
        12,
        functools.partial(expert_out_kernel, count, hidden),
        [Split(4, (sum(g.shape[0] for g in gated) // 4, weights.shape[2]), BF16)],
        [Rows(gated), Part(weights, hidden, hidden)],
        after,
    )


def shards(
    tokens,
    cotangent,
    segments,
    value_expert_route,
    output_expert_route,
    feedforward_route,
    attention_norm_gain,
    attention_norm_bias,
    feedforward_norm_gain,
    feedforward_norm_bias,
    query_projection,
    key_projection,
    value_selector,
    output_selector,
    value_experts,
    output_experts,
    feedforward_selector,
    expert_up_weight,
    expert_down_weight,
):
    n_data = lax.axis_size("dp")
    head = lax.axis_index("head")
    own, width = tokens.shape[1:]
    half = own // 2
    length = segments.shape[1]
    size = query_projection.shape[1]
    kinds = value_selector.shape[1]
    hidden = expert_up_weight.shape[2]
    scale = size ** (-0.5)
    mixed_width = kinds * size

    def arranged(value):
        return jnp.concatenate(
            [lax.dynamic_slice_in_dim(value, (head ^ k) * own, own, 0) for k in range(4)]
        )

    x_own, grad_own = tokens[0], cotangent[0]
    last = 3 * LANES + mixed_width
    all_own = call(
        "pack_weights",
        1,
        functools.partial(pack_in_kernel, kinds),
        shape((query_projection.shape[0], last + mixed_width), BF16),
        [
            query_projection,
            key_projection,
            value_experts[0],
            value_selector.T,
            output_selector.T,
            output_experts[0],
        ],
    )
    all_in = lax.all_gather(all_own, "dp", axis=0, tiled=True)
    in_all, out_all = Part(all_in, 0, last), Part(all_in, last, mixed_width)
    experts = 4 * n_data
    hot = jnp.sum(jax.nn.one_hot(feedforward_route[0], experts, dtype=BF16), 1)
    hot_rows = own * experts // width
    hot = hot.reshape(hot_rows, width)
    hot = jnp.concatenate([hot, jnp.zeros((-hot_rows % PAD, width), BF16)])
    grad_sent = call(
        "pack_grad",
        2,
        stack_kernel,
        shape((own + hot.shape[0], width), BF16),
        [Rows([grad_own, hot])],
    )

    def spread_whole(value):
        near_x, near_y = to_head(value, 1), to_head(value, 2)
        far = [to_head(near_y[:half], 1), to_head(near_x[half:], 2)]
        return [near_x], [near_y], far

    x = [[x_own], *spread_whole(x_own)]
    grad = [[grad_own], *spread_whole(grad_sent)]
    (near_x,), (near_y,), (_, far_bottom) = grad[1:]

    def hits_of(rows):
        found = rows[:hot_rows].reshape(own, experts)
        return lax.dynamic_slice_in_dim(found, head * n_data, n_data, 1).astype(F32)

    hits = [hits_of(v) for v in (hot, near_x[own:], near_y[own:], far_bottom[half:])]
    ffn_own = call(
        "pack_experts",
        2,
        pack_experts_kernel,
        shape((2 * hidden + PAD, width), BF16),
        [expert_up_weight[0], expert_down_weight[0], feedforward_selector],
        [all_own, grad_sent],
    )
    ffn_all = lax.all_gather(ffn_own, "dp", axis=0, tiled=False)
    router = ffn_all[:, 2 * hidden]

    spots = jnp.arange(length, dtype=jnp.int32)
    first_code = segments[0] * length
    info = arranged(
        jnp.concatenate(
            [
                first_code[:, None],
                (first_code + spots)[:, None],
                value_expert_route[0, :, 0],
                output_expert_route[0, :, 0] + kinds,
                jnp.zeros((length, 2), jnp.int32),
            ],
            1,
        )
    )
    code = arranged(first_code + spots)[None]
    gain1, bias1 = attention_norm_gain[None], attention_norm_bias[None]
    gain2, bias2 = feedforward_norm_gain[None], feedforward_norm_bias[None]
    (
        part_own,
        part_x,
        part_y,
        part_far,
        query,
        key,
        value,
        experts_v,
        gate,
        att,
        lse,
        mixed,
    ) = call(
        "forward",
        14,
        functools.partial(forward_kernel, own, scale, kinds, size),
        [Split(4, (own, width), BF16)]
        + [shape((length, size), BF16)] * 3
        + [
            shape((length, mixed_width), BF16),
            shape((length, LANES), F32),
            shape((length, size), F32),
            shape((length, LANES), F32),
            shape((length, mixed_width), BF16),
        ],
        [Rows(flat(x)), gain1, bias1, info, in_all, code, out_all],
        flat(grad[1:]),
    )

    def residual(name, parts, after=()):
        return call(
            name,
            2,
            residual_kernel,
            [shape((own, width), F32)] + [shape((half, width), BF16)] * 2,
            parts,
            after,
        )

    parts = [to_head(part, flip) for part, flip in ((part_far, 3), (part_x, 1), (part_y, 2))]
    resid, top, bottom = residual("residual", [x_own, part_own, *parts])
    rows = spread_rows(top, bottom)

    if n_data <= CHUNK:
        back, moved, gated, norm2, slabs = expert_chunk(
            rows,
            grad,
            hits,
            ffn_all,
            router,
            gain2,
            bias2,
            (1, 2, 3),
        )
    else:
        cut = lambda a: a.reshape((n_data // CHUNK, CHUNK) + a.shape[1:])
        hit_cuts = [
            h.reshape(own, n_data // CHUNK, CHUNK).transpose(1, 0, 2) for h in hits
        ]

        def step(carry, item):
            hit, rt, w = item
            got_back, _, got_gated, got_norm, slab = expert_chunk(
                rows, grad, hit, w, rt, gain2, bias2
            )
            got_out = expert_out(got_gated, w, ())
            add = lambda old, new: [o + v.astype(F32) for o, v in zip(old, new)]
            new = (add(carry[0], got_out), add(carry[1], got_back), carry[2] + got_norm)
            return new, slab

        zero = [jnp.zeros((own, width), F32)] * 4
        (out, back, norm2), slabs = lax.scan(
            step,
            (zero, zero, jnp.zeros((2, width), F32)),
            (hit_cuts, cut(router), cut(ffn_all)),
        )
        out, back = [v.astype(BF16) for v in out], [v.astype(BF16) for v in back]
        moved = [to_head(back[flip], flip) for flip in (1, 2, 3)]
        slabs = slabs.reshape((n_data,) + slabs.shape[2:])

    ffn_grads = lax.psum_scatter(slabs, "dp", scatter_dimension=0, tiled=True)
    if n_data <= CHUNK:
        out = expert_out(gated, ffn_all, ())
    d_resid, top, bottom = residual("residual_back", [grad_own, back[0], *moved], [slabs, *out])
    d_pack = spread_rows(top, bottom)

    dq, dsel, dk, dv = call(
        "attend_back",
        46,
        functools.partial(attend_back_kernel, own, 3, kinds, size),
        [
            shape((3 * own, size), BF16),
            shape((length, LANES), F32),
            shape((length, size), F32),
            shape((length, size), F32),
        ],
        [query, key, info, code, lse, out_all, Rows(flat(d_pack[:3])), value, gate, att],
        out,
    )
    out_moved = [to_head(out[flip], flip) for flip in (3, 1, 2)]
    d_in, d_exp = call(
        "attend_last",
        46,
        functools.partial(attend_last_kernel, own, kinds, size),
        [shape((length, 3 * LANES), BF16), shape((length, mixed_width), BF16)],
        [
            query,
            key,
            info,
            code,
            lse,
            out_all,
            Rows(d_pack[3]),
            value,
            gate,
            att,
            dq,
            dsel,
            dk,
            dv,
            experts_v,
        ],
    )
    weight_part = call(
        "weights",
        6,
        weight_kernel,
        shape((width, 3 * LANES + 2 * mixed_width), BF16),
        [
            Rows(flat(d_pack)),
            mixed,
            Rows(flat(x)),
            gate,
            gain1,
            bias1,
            d_in,
            d_exp,
        ],
        (ffn_grads, *out_moved[1:]),
    )
    d_own, d_x, d_y, d_far, norm1 = call(
        "input_back",
        6,
        functools.partial(input_grad_kernel, own, scale, size),
        [Split(4, (own, width), BF16), shape((2, width), F32)],
        [Rows(flat(x)), d_in, gate, gain1, in_all, d_exp],
        (weight_part,),
    )
    moved = [to_head(part, flip) for part, flip in ((d_far, 3), (d_x, 1), (d_y, 2))]
    block = shape((own, width), BF16)
    up_grad, down_grad, router_grad = call(
        "finish_experts",
        2,
        finish_experts_kernel,
        [shape((width, hidden), F32), shape((hidden, width), F32), shape((1, width), F32)],
        [ffn_grads[0]],
    )
    output = call(
        "output",
        2,
        finish_kernel,
        block,
        [resid, out[0], *out_moved],
        moved[1:],
    )
    grad_tokens = call(
        "token_grads", 2, finish_kernel, block, [d_resid, d_own, *moved]
    )

    part = width // n_data
    grads = lax.psum_scatter(weight_part, "dp", scatter_dimension=0, tiled=True)
    query_grad, key_grad, value_sel, output_sel, value_grad, output_grad = call(
        "finish_weights",
        2,
        functools.partial(finish_weights_kernel, scale, kinds),
        [
            shape((part, size), F32),
            shape((part, size), F32),
            shape((kinds, part), F32),
            shape((kinds, part), F32),
            shape((part, mixed_width), F32),
            shape((mixed_width, part), F32),
        ],
        [grads],
    )
    norms = jnp.concatenate([norm1, norm2]).reshape(4, 4 * n_data, -1).transpose(1, 0, 2)
    norms = lax.all_to_all(norms, ("head", "dp"), split_axis=0, concat_axis=0, tiled=True)
    norms = jnp.sum(norms, 0)
    return (
        output[None],
        grad_tokens[None],
        norms,
        query_grad,
        key_grad,
        value_sel.T,
        output_sel.T,
        value_grad[None],
        output_grad[None],
        router_grad,
        up_grad[None],
        down_grad[None],
    )


def solution(mesh):
    placed = (
        P("dp", "head", None),
        P("dp", "head", None),
        P("dp", None),
        P("dp", None, "head", None),
        P("dp", None, "head", None),
        P("dp", "head", None),
        P(),
        P(),
        P(),
        P(),
        P("dp", "head"),
        P("dp", "head"),
        P("dp", "head"),
        P("dp", "head"),
        P("head", "dp", None),
        P("head", None, "dp"),
        P(("head", "dp"), None),
        P(("head", "dp"), None, None),
        P(("head", "dp"), None, None),
    )
    return jax.shard_map(
        shards,
        mesh=mesh,
        in_specs=placed,
        out_specs=(
            P("dp", "head", None),
            P("dp", "head", None),
            P(None, ("head", "dp")),
            P("dp", "head"),
            P("dp", "head"),
            P("dp", "head"),
            P("dp", "head"),
            P("head", "dp", None),
            P("head", None, "dp"),
            P(("head", "dp"), None),
            P(("head", "dp"), None, None),
            P(("head", "dp"), None, None),
        ),
        check_vma=False,
    )
```
